32 devices in a mesh: seq: 8 (over z, y), ch: 4 (over x, core).
Axes of the slice: x: 2, y: 2, z: 4, core: 2. Of those that a mesh axis runs over, the one named last changes fastest.
Arguments:
- signal_x: bfloat16 [64, 4096], P('ch', 'seq'), may hold values from -6 to 6
- gate_q: bfloat16 [64, 4096], P('ch', 'seq'), may hold values from -6 to 6
- gate_k: bfloat16 [64, 4096], P('ch', 'seq'), may hold values from -6 to 6
- skip_gain: float32 [64], P('ch'), may hold values from 0.5 to 1.5
- residue: float32 [16], replicated, may hold values from -1.5 to 1.5
- memory: float32 [16], replicated, may hold values from 30 to 16384
- cotangent: bfloat16 [64, 4096], P('ch', 'seq'), may hold values from -6 to 6
Outputs:
- output: bfloat16 [64, 4096], P('ch', 'seq')
- grad_x: bfloat16 [64, 4096], P('ch', 'seq')
- grad_q: bfloat16 [64, 4096], P('ch', 'seq')
- grad_k: bfloat16 [64, 4096], P('ch', 'seq')
- grad_skip: float32 [64], P('ch')
- grad_residue: float32 [16], replicated
- grad_memory: float32 [16], replicated
The draws below stay inside these ranges and needn't reach their ends.
All inputs are finite; a program needn't handle non-finite values.
Results may differ from the reference program's by a relative error of at most 0.002.
Values sent between devices are 32-bit elements; how exact they have to be, the bound alone decides.
No kernel may reach another device: no remote copies, remote signals or barrier semaphores. Data moves between devices by JAX's collectives and lax.ppermute only.
A program may use at most 64 MiB of HBM per device.

```python
import math
import jax
import jax.numpy as jnp
from jax import lax

ORDER = 16
SEQLEN = 4096
CHANNELS = 64


def steps_of(own_key, dims, split, smallest, largest):
    loudness, own = 1.0, jax.random.fold_in(own_key, 6)
    for dim, parts in split:
        steps = jnp.exp(jax.random.uniform(jax.random.fold_in(own, dim), (parts,), jnp.float32, smallest / len(split), largest / len(split)))
        loudness = loudness * jnp.repeat(steps, dims[dim] // parts).reshape([-1 if axis == dim else 1 for axis in range(len(dims))])
    return loudness


def centred(key, shape, spread, most, shards=(), kind=jnp.bfloat16):
    values = jax.random.normal(key, shape, jnp.float32) * spread
    if len(shards) > 0:
        values = steps_of(key, shape, shards, -0.22, 0.18) * values
    return jnp.clip(values, min=-most, max=most).astype(kind)


def setup_inputs(seed: int = 0) -> dict:
    arg_keys = jax.random.split(jax.random.key(seed), 8)
    return {
        "signal_x": centred(arg_keys[0], (CHANNELS, SEQLEN), 1.0, 6.0, ((0, 4), (1, 8))),
        "gate_q": centred(arg_keys[1], (CHANNELS, SEQLEN), 1.0, 6.0, ((0, 4), (1, 8))),
        "gate_k": centred(arg_keys[2], (CHANNELS, SEQLEN), 1.0, 6.0, ((0, 4), (1, 8))),
        "skip_gain": jnp.clip(0.5 + 1.0 * jax.random.uniform(arg_keys[3], (CHANNELS,), jnp.float32) ** steps_of(arg_keys[3], (CHANNELS,), ((0, 4),), -0.2, 0.2), 0.5, 1.5),
        "residue": centred(arg_keys[4], (ORDER,), 0.25, 1.5, (), jnp.float32),
        "memory": jnp.clip(jnp.exp(jax.random.uniform(arg_keys[5], (ORDER,), jnp.float32, math.log(30.0), math.log(16384.0))), 30.0, 16384.0),
        "cotangent": centred(arg_keys[6], (CHANNELS, SEQLEN), 1.0, 6.0, ((0, 4), (1, 8))),
    }


def reference(signal_x, gate_q, gate_k, skip_gain, residue, memory, cotangent):
    seq_len = signal_x.shape[1]
    positions = jnp.arange(seq_len).astype(jnp.float32)
    weights = jnp.sqrt(2.0 / memory)[:, None] * jnp.exp(-positions[None, :] / memory[:, None])
    filter_taps = lax.optimization_barrier(jnp.sum(residue[:, None] * weights, axis=0))
    spec_taps = jnp.fft.fft(filter_taps, n=2 * seq_len)
    x_float = signal_x.astype(jnp.float32)
    q_float = gate_q.astype(jnp.float32)
    k_float = gate_k.astype(jnp.float32)
    d_float = cotangent.astype(jnp.float32)
    values = x_float * k_float
    grad_mixed = d_float * q_float

    def per_channel(carried, inputs):
        channel_val, channel_grad = inputs
        spec_val = jnp.fft.fft(channel_val, n=2 * seq_len)
        spec_grad = jnp.fft.fft(channel_grad, n=2 * seq_len)
        conv_out = jnp.fft.ifft(spec_val * spec_taps)[:seq_len].real
        corr_out = jnp.fft.ifft(jnp.conj(spec_taps) * spec_grad)[:seq_len].real
        taps_term = jnp.fft.ifft(jnp.conj(spec_val) * spec_grad)[:seq_len].real
        return (carried + taps_term, (conv_out, corr_out))
    grad_taps, (conv_out, corr_out) = lax.scan(per_channel, jnp.zeros((seq_len,), jnp.float32), (values, grad_mixed))
    mixed_out = conv_out + skip_gain[:, None] * values
    output = (q_float * mixed_out).astype(jnp.bfloat16)
    grad_values = skip_gain[:, None] * grad_mixed + corr_out
    grad_x = (grad_values * k_float).astype(jnp.bfloat16)
    grad_q = (d_float * mixed_out).astype(jnp.bfloat16)
    grad_k = (grad_values * x_float).astype(jnp.bfloat16)
    norm_scale = 1.0 / math.sqrt(CHANNELS * SEQLEN)
    grad_skip = lax.optimization_barrier(jnp.sum(grad_mixed * values, axis=1)) / math.sqrt(SEQLEN)
    weighted = weights * grad_taps[None, :]
    grad_residue = lax.optimization_barrier(jnp.sum(weighted, axis=1)) * norm_scale
    grad_memory = residue * lax.optimization_barrier(jnp.sum(weighted * (positions[None, :] / memory[:, None] - 0.5), axis=1)) * norm_scale
    return (output, grad_x, grad_q, grad_k, grad_skip, grad_residue, grad_memory)
```

```python
import functools
import math

import jax
import jax.numpy as jnp
from jax import lax
from jax.experimental import pallas as pl
from jax.experimental.pallas import tpu as pltpu
from jax.sharding import PartitionSpec as P

F32 = jnp.float32
BF16 = jnp.bfloat16
LANES = 128


def iota(shape, dim):
    return lax.broadcasted_iota(jnp.int32, shape, dim)


def roll(data, shift):
    return pltpu.roll(data, shift % LANES, 1)


def nt_dot(left, right):
    return lax.dot_general(left, right, (((1,), (1,)), ((), ())), preferred_element_type=F32)


def nn_dot(left, right):
    return lax.dot_general(left, right, (((1,), (0,)), ((), ())), preferred_element_type=F32)


def tn_dot(left, right):
    return lax.dot_general(left, right, (((0,), (0,)), ((), ())), preferred_element_type=F32)


def halves(data):
    high = data.astype(BF16)
    return high, (data - high.astype(F32)).astype(BF16)


def left_split(data):
    high, low = halves(data)
    return jnp.concatenate([high, low, high], axis=1)


def right_split(data, axis=1):
    high, low = halves(data)
    return jnp.concatenate([high, high, low], axis=axis)


def by_chunk(ref):
    chunks = ref.shape[1] // LANES
    return jnp.concatenate([ref[:, j * LANES : (j + 1) * LANES].astype(F32) for j in range(chunks)], axis=0)


def column(row):
    size = row.shape[1]
    square = jnp.broadcast_to(row, (size, size))
    return jnp.sum(jnp.where(iota((size, size), 0) == iota((size, size), 1), square, 0.0), axis=1, keepdims=True)


def tiled_row(col):
    size = col.shape[0]
    spread = jnp.where(iota((size, LANES), 1) % size == iota((size, LANES), 0), col, 0.0)
    return jnp.sum(spread, axis=0, keepdims=True)


def decays(inv_col):
    modes = inv_col.shape[0]
    offset = iota((modes, LANES), 1).astype(F32)
    age_in = (LANES - offset) * inv_col
    age_out = offset * inv_col
    return jnp.exp(-age_in), age_in, jnp.exp(-age_out), age_out


def pad_rows(data):
    return jnp.concatenate([data, jnp.zeros((LANES - data.shape[0], data.shape[1]), data.dtype)], axis=0)


def make_states(memory_ref, x_ref, q_ref, k_ref, d_ref, out_ref):
    modes = memory_ref.shape[1]
    channels, local_len = x_ref.shape
    chunks = local_len // LANES
    inv_col = column(1.0 / memory_ref[...])
    inv_row = tiled_row(inv_col)
    decay_in, age_in, decay_out, age_out = decays(inv_col)
    values = by_chunk(x_ref) * by_chunk(k_ref)
    grads = by_chunk(d_ref) * by_chunk(q_ref)
    value_split = left_split(values)
    grad_split = left_split(grads)
    first_in, first_out = decay_in * age_in, decay_out * age_out
    pair = jnp.concatenate(
        [
            pad_rows(jnp.concatenate([decay_in, first_in], axis=0)),
            pad_rows(jnp.concatenate([first_in, decay_in], axis=0)),
        ],
        axis=0,
    )
    value_states = nt_dot(value_split, right_split(pair))
    grad_states = nt_dot(grad_split, right_split(pad_rows(jnp.concatenate([decay_out, first_out], axis=0))))
    lane = iota((channels, LANES), 1)
    step = jnp.exp(-LANES * inv_row)
    growth = LANES * inv_row
    growth_low = jnp.where(lane < modes, growth, 0.0)
    growth_high = jnp.where((lane >= modes) & (lane < 2 * modes), growth, 0.0)
    prefix = jnp.zeros((channels, LANES), F32)
    swapped = prefix
    cross_zero = prefix
    cross_one = prefix
    suffix = prefix
    weighted = prefix
    power = jnp.ones_like(step)
    for j in range(chunks):
        rows = slice(j * channels, (j + 1) * channels)
        grad_part = grad_states[rows]
        if j > 0:
            cross_zero = cross_zero + prefix * grad_part
            cross_one = cross_one + swapped * grad_part
        prefix, swapped = (
            step * (prefix + growth_high * swapped) + value_states[rows, :LANES],
            step * (swapped + growth_low * prefix) + value_states[rows, LANES:],
        )
        suffix = suffix + power * grad_part
        weighted = weighted + (j * power) * grad_part
        power = power * step
    suffix = suffix + growth_high * roll(weighted, modes)
    pack = jnp.where(lane < 2 * modes, prefix, 0.0) + roll(jnp.where(lane < 2 * modes, suffix, 0.0), 2 * modes)
    half = channels // 2
    payload = pack[:half] + roll(pack[half:], 4 * modes)
    high_v, low_v = halves(values)
    high_g, low_g = halves(grads)
    outer = tn_dot(
        jnp.concatenate([high_v, low_v, high_v], axis=0), jnp.concatenate([high_g, high_g, low_g], axis=0)
    )
    outer = jnp.where(iota(outer.shape, 1) >= iota(outer.shape, 0), outer, 0.0)
    turn = (iota(outer.shape, 1) + iota(outer.shape, 0)) % LANES
    skewed = jnp.take_along_axis(outer, turn, axis=1, mode="promise_in_bounds")
    by_distance = jnp.sum(skewed, axis=0, keepdims=True)
    near = decay_out * by_distance
    near_zero = jnp.sum(near, axis=1, keepdims=True)
    near_one = jnp.sum(near * age_out, axis=1, keepdims=True)
    products = values * grads
    part_skip = products[:channels]
    for j in range(1, chunks):
        part_skip = part_skip + products[j * channels : (j + 1) * channels]
    part_skip = jnp.sum(part_skip, axis=1, keepdims=True)
    row_id = iota((channels, LANES), 0)
    extras = (
        jnp.where(lane < modes, cross_zero, 0.0)
        + roll(jnp.where(lane < 2 * modes, cross_one, 0.0), modes)
        + jnp.where(lane == row_id, near_zero, 0.0)
        + jnp.where(lane == row_id + modes, near_one, 0.0)
        + jnp.where(lane == row_id + 3 * modes, part_skip, 0.0)
    )
    for i in range(half):
        out_ref[i] = payload[i : i + 1]
    out_ref[half] = jnp.sum(extras, axis=0, keepdims=True)


def finish(seq_size, ch_size, memory_ref, residue_ref, skip_ref, x_ref, q_ref, k_ref, d_ref, all_ref,
           output_ref, grad_x_ref, grad_q_ref, grad_k_ref, grad_skip_ref, grad_residue_ref, grad_memory_ref):
    modes = memory_ref.shape[1]
    channels, local_len = x_ref.shape
    chunks = local_len // LANES
    half = channels // 2
    me_seq, me_ch = lax.axis_index("seq"), lax.axis_index("ch")
    inv = 1.0 / memory_ref[...]
    inv_col = column(inv)
    inv_row = tiled_row(inv_col)
    decay_in, _, decay_out, _ = decays(inv_col)
    amplitude = column(residue_ref[...] * jnp.sqrt(2.0 * inv))
    signal, gate_out = by_chunk(x_ref), by_chunk(q_ref)
    gate_in, cotangent = by_chunk(k_ref), by_chunk(d_ref)
    values = signal * gate_in
    grads = cotangent * gate_out
    value_split = left_split(values)
    grad_split = left_split(grads)

    leap = jnp.exp(-local_len * inv_row)
    lane = iota((half, LANES), 1)

    def block(device):
        return all_ref[device, :half, 0, :]

    def before(d, carry):
        return jnp.where(d < me_seq, leap * carry + block(d * ch_size + me_ch), carry)

    def after(i, carry):
        d = seq_size - 1 - i
        return jnp.where(d > me_seq, leap * carry + block(d * ch_size + me_ch), carry)

    def loop(body, init):
        if seq_size <= 8:
            for i in range(seq_size):
                init = body(i, init)
            return init
        return lax.fori_loop(0, seq_size, body, init)

    zeros = jnp.zeros((half, LANES), F32)
    border_v = loop(before, zeros)
    border_g = roll(loop(after, zeros), -2 * modes)

    def three_times(data):
        full = jnp.concatenate([data, roll(data, -4 * modes)], axis=0)
        full = jnp.where(iota(full.shape, 1) < modes, full, 0.0)
        return full + roll(full, modes) + roll(full, 2 * modes)

    border_v, border_g = three_times(border_v), three_times(border_g)

    thrice_in = pad_rows(jnp.concatenate([decay_in] * 3, axis=0))
    thrice_out = pad_rows(jnp.concatenate([decay_out] * 3, axis=0))
    value_states = nt_dot(value_split, right_split(thrice_in))
    grad_states = nt_dot(grad_split, right_split(thrice_out))
    step = jnp.exp(-LANES * inv_row)
    starts, ends = [border_v], [border_g]
    for j in range(chunks - 1):
        starts.append(step * starts[-1] + value_states[j * channels : (j + 1) * channels])
        i = chunks - 1 - j
        ends.append(step * ends[-1] + grad_states[i * channels : (i + 1) * channels])
    rows = chunks * channels
    tail = iota((rows, LANES), 1) >= 2 * modes

    def state_split(parts):
        data = jnp.concatenate(parts, axis=0)
        high = data.astype(BF16).astype(F32)
        return jnp.where(tail, data - high, high).astype(BF16)

    def readout(decay):
        high, low = halves(amplitude * decay)
        return pad_rows(jnp.concatenate([high, low, high], axis=0))

    taps = jnp.sum(amplitude * decay_out, axis=0, keepdims=True)
    toeplitz = pltpu.roll(jnp.broadcast_to(taps, (LANES, LANES)), 0, 1, stride=1, stride_axis=0)
    square = (LANES, LANES)
    toeplitz = jnp.where(iota(square, 1) >= iota(square, 0), toeplitz, 0.0)
    conv = nn_dot(value_split, right_split(toeplitz, axis=0)) + nn_dot(state_split(starts), readout(decay_out))
    corr = nt_dot(grad_split, right_split(toeplitz)) + nn_dot(state_split(ends[::-1]), readout(decay_in))
    gain = jnp.concatenate([column(skip_ref[...])] * chunks, axis=0)
    mixed = conv + gain * values
    grad_values = gain * grads + corr

    def put(ref, data):
        for j in range(chunks):
            ref[:, j * LANES : (j + 1) * LANES] = data[j * channels : (j + 1) * channels].astype(ref.dtype)

    put(output_ref, gate_out * mixed)
    put(grad_x_ref, grad_values * gate_in)
    put(grad_q_ref, cotangent * mixed)
    put(grad_k_ref, grad_values * signal)

    kind = iota((ch_size * half, LANES), 1) // modes % 4
    growth = local_len * inv_row
    growth_low = jnp.where(kind == 0, growth, 0.0)
    growth_high = jnp.where(kind == 1, growth, 0.0)

    def pairs(e, carry):
        prefix, swapped, cross_zero, cross_one, extras = carry
        state = jnp.concatenate([block(e * ch_size + c) for c in range(ch_size)], axis=0)
        turned = jnp.where(kind == 0, roll(state, -modes), roll(state, modes))
        grad_part = roll(state, -2 * modes)
        for c in range(ch_size):
            extras = extras + all_ref[e * ch_size + c, half]
        return (
            leap * (prefix + growth_high * swapped) + state,
            leap * (swapped + growth_low * prefix) + turned,
            cross_zero + prefix * grad_part,
            cross_one + swapped * grad_part,
            extras,
        )

    wide = jnp.zeros((ch_size * half, LANES), F32)
    _, _, cross_zero, cross_one, extras = loop(pairs, (wide, wide, wide, wide, jnp.zeros((1, LANES), F32)))
    cross_zero = jnp.sum(jnp.where(kind == 0, cross_zero, 0.0), axis=0, keepdims=True)
    cross_one = jnp.sum(jnp.where(kind <= 1, cross_one, 0.0), axis=0, keepdims=True)
    cross_one = cross_one + roll(cross_one, -modes)
    sum_zero = extras + cross_zero + roll(cross_zero, -4 * modes)
    sum_one = roll(extras, -modes) + roll(extras, -2 * modes) + cross_one + roll(cross_one, -4 * modes)
    sum_zero, sum_one = sum_zero[:, :modes], sum_one[:, :modes]
    scale = jnp.sqrt(2.0 * inv) / math.sqrt(ch_size * channels * seq_size * local_len)
    grad_residue_ref[...] = scale * sum_zero
    grad_memory_ref[...] = residue_ref[...] * scale * (sum_one - 0.5 * sum_zero)

    def skips(d, carry):
        return carry + all_ref[d * ch_size + me_ch, half]

    skip_sum = roll(loop(skips, jnp.zeros((1, LANES), F32)), -3 * modes)
    grad_skip_ref[...] = skip_sum[:, :channels] / math.sqrt(seq_size * local_len)


def per_device(signal_x, gate_q, gate_k, skip_gain, residue, memory, cotangent):
    channels, local_len = signal_x.shape
    modes = memory.shape[0]
    seq_size, ch_size = lax.axis_size("seq"), lax.axis_size("ch")
    devices = seq_size * ch_size
    params = pltpu.CompilerParams(vmem_limit_bytes=32 * 1024 * 1024)
    memory_row, residue_row, skip_row = memory[None], residue[None], skip_gain[None]
    rows = channels // 2 + 1
    mine = pl.pallas_call(
        make_states,
        out_shape=jax.ShapeDtypeStruct((rows, 1, LANES), F32),
        compiler_params=params,
    )(memory_row, signal_x, gate_q, gate_k, cotangent)
    everyone = lax.all_to_all(jnp.broadcast_to(mine[None], (devices, rows, 1, LANES)), ("seq", "ch"), 0, 0)
    big = jax.ShapeDtypeStruct((channels, local_len), BF16)
    results = pl.pallas_call(
        functools.partial(finish, seq_size, ch_size),
        out_shape=(
            big,
            big,
            big,
            big,
            jax.ShapeDtypeStruct((1, channels), F32),
            jax.ShapeDtypeStruct((1, modes), F32),
            jax.ShapeDtypeStruct((1, modes), F32),
        ),
        compiler_params=params,
    )(memory_row, residue_row, skip_row, signal_x, gate_q, gate_k, cotangent, everyone)
    return results[:4] + tuple(result[0] for result in results[4:])


def solution(mesh):
    grid = P("ch", "seq")
    return jax.shard_map(
        per_device,
        mesh=mesh,
        in_specs=(grid, grid, grid, P("ch"), P(), P(), grid),
        out_specs=(grid, grid, grid, grid, P("ch"), P(), P()),
        check_vma=False,
    )
```

```python
import functools
import math

import jax
import jax.numpy as jnp
from jax import lax
from jax.experimental import pallas as pl
from jax.experimental.pallas import tpu as pltpu
from jax.sharding import PartitionSpec as P

F32 = jnp.float32
BF16 = jnp.bfloat16
LANES = 128


def iota(shape, dim):
    return lax.broadcasted_iota(jnp.int32, shape, dim)


def roll(data, shift):
    return pltpu.roll(data, shift % LANES, 1)


def nt_dot(left, right):
    return lax.dot_general(left, right, (((1,), (1,)), ((), ())), preferred_element_type=F32)


def nn_dot(left, right):
    return lax.dot_general(left, right, (((1,), (0,)), ((), ())), preferred_element_type=F32)


def tn_dot(left, right):
    return lax.dot_general(left, right, (((0,), (0,)), ((), ())), preferred_element_type=F32)


def halves(data):
    high = data.astype(BF16)
    return high, (data - high.astype(F32)).astype(BF16)


def left_split(data):
    high, low = halves(data)
    return jnp.concatenate([high, low, high], axis=1)


def right_split(data, axis=1):
    high, low = halves(data)
    return jnp.concatenate([high, high, low], axis=axis)


def by_chunk(ref):
    chunks = ref.shape[1] // LANES
    return jnp.concatenate([ref[:, j * LANES : (j + 1) * LANES].astype(F32) for j in range(chunks)], axis=0)


def column(row):
    size = row.shape[1]
    square = jnp.broadcast_to(row, (size, size))
    return jnp.sum(jnp.where(iota((size, size), 0) == iota((size, size), 1), square, 0.0), axis=1, keepdims=True)


def tiled_row(col):
    size = col.shape[0]
    spread = jnp.where(iota((size, LANES), 1) % size == iota((size, LANES), 0), col, 0.0)
    return jnp.sum(spread, axis=0, keepdims=True)


def decays(inv_col):
    modes = inv_col.shape[0]
    offset = iota((modes, LANES), 1).astype(F32)
    age_in = (LANES - offset) * inv_col
    age_out = offset * inv_col
    return jnp.exp(-age_in), age_in, jnp.exp(-age_out), age_out


def pad_rows(data):
    return jnp.concatenate([data, jnp.zeros((LANES - data.shape[0], data.shape[1]), data.dtype)], axis=0)


def make_states(*refs):
    sources, (out_ref, *copies), arrived = refs[:7], refs[7:15], refs[15]
    moves = [pltpu.make_async_copy(*ends, arrived.at[i]) for i, ends in enumerate(zip(sources, copies))]
    for move in moves:
        move.start()
    for move in moves:
        move.wait()
    memory_ref, _, _, x_ref, q_ref, k_ref, d_ref = copies
    modes = memory_ref.shape[1]
    channels, local_len = x_ref.shape
    chunks = local_len // LANES
    inv_col = column(1.0 / memory_ref[...])
    inv_row = tiled_row(inv_col)
    decay_in, age_in, decay_out, age_out = decays(inv_col)
    values = by_chunk(x_ref) * by_chunk(k_ref)
    grads = by_chunk(d_ref) * by_chunk(q_ref)
    value_split = left_split(values)
    grad_split = left_split(grads)
    first_in, first_out = decay_in * age_in, decay_out * age_out
    pair = jnp.concatenate(
        [
            pad_rows(jnp.concatenate([decay_in, first_in], axis=0)),
            pad_rows(jnp.concatenate([first_in, decay_in], axis=0)),
        ],
        axis=0,
    )
    value_states = nt_dot(value_split, right_split(pair))
    grad_states = nt_dot(grad_split, right_split(pad_rows(jnp.concatenate([decay_out, first_out], axis=0))))
    lane = iota((channels, LANES), 1)
    step = jnp.exp(-LANES * inv_row)
    growth = LANES * inv_row
    growth_low = jnp.where(lane < modes, growth, 0.0)
    growth_high = jnp.where((lane >= modes) & (lane < 2 * modes), growth, 0.0)
    prefix = jnp.zeros((channels, LANES), F32)
    swapped = prefix
    cross_zero = prefix
    cross_one = prefix
    suffix = prefix
    weighted = prefix
    power = jnp.ones_like(step)
    for j in range(chunks):
        rows = slice(j * channels, (j + 1) * channels)
        grad_part = grad_states[rows]
        if j > 0:
            cross_zero = cross_zero + prefix * grad_part
            cross_one = cross_one + swapped * grad_part
        prefix, swapped = (
            step * (prefix + growth_high * swapped) + value_states[rows, :LANES],
            step * (swapped + growth_low * prefix) + value_states[rows, LANES:],
        )
        suffix = suffix + power * grad_part
        weighted = weighted + (j * power) * grad_part
        power = power * step
    suffix = suffix + growth_high * roll(weighted, modes)
    pack = jnp.where(lane < 2 * modes, prefix, 0.0) + roll(jnp.where(lane < 2 * modes, suffix, 0.0), 2 * modes)
    half = channels // 2
    payload = pack[:half] + roll(pack[half:], 4 * modes)
    high_v, low_v = halves(values)
    high_g, low_g = halves(grads)
    outer = tn_dot(
        jnp.concatenate([high_v, low_v, high_v], axis=0), jnp.concatenate([high_g, high_g, low_g], axis=0)
    )
    outer = jnp.where(iota(outer.shape, 1) >= iota(outer.shape, 0), outer, 0.0)
    turn = (iota(outer.shape, 1) + iota(outer.shape, 0)) % LANES
    skewed = jnp.take_along_axis(outer, turn, axis=1, mode="promise_in_bounds")
    by_distance = jnp.sum(skewed, axis=0, keepdims=True)
    near = decay_out * by_distance
    near_zero = jnp.sum(near, axis=1, keepdims=True)
    near_one = jnp.sum(near * age_out, axis=1, keepdims=True)
    products = values * grads
    part_skip = products[:channels]
    for j in range(1, chunks):
        part_skip = part_skip + products[j * channels : (j + 1) * channels]
    part_skip = jnp.sum(part_skip, axis=1, keepdims=True)
    row_id = iota((channels, LANES), 0)
    extras = (
        jnp.where(lane < modes, cross_zero, 0.0)
        + roll(jnp.where(lane < 2 * modes, cross_one, 0.0), modes)
        + jnp.where(lane == row_id, near_zero, 0.0)
        + jnp.where(lane == row_id + modes, near_one, 0.0)
        + jnp.where(lane == row_id + 3 * modes, part_skip, 0.0)
    )
    for i in range(half):
        out_ref[i] = payload[i : i + 1]
    out_ref[half] = jnp.sum(extras, axis=0, keepdims=True)


def finish(seq_size, ch_size, memory_ref, residue_ref, skip_ref, x_ref, q_ref, k_ref, d_ref, all_ref,
           *refs):
    results, scratch, sent = refs[:7], refs[7:14], refs[14]
    output_ref, grad_x_ref, grad_q_ref, grad_k_ref, grad_skip_ref, grad_residue_ref, grad_memory_ref = scratch
    moves = [pltpu.make_async_copy(*ends, sent.at[i]) for i, ends in enumerate(zip(scratch, results))]
    modes = memory_ref.shape[1]
    channels, local_len = x_ref.shape
    chunks = local_len // LANES
    half = channels // 2
    me_seq, me_ch = lax.axis_index("seq"), lax.axis_index("ch")
    inv = 1.0 / memory_ref[...]
    inv_col = column(inv)
    inv_row = tiled_row(inv_col)
    decay_in, _, decay_out, _ = decays(inv_col)
    amplitude = column(residue_ref[...] * jnp.sqrt(2.0 * inv))
    signal, gate_out = by_chunk(x_ref), by_chunk(q_ref)
    gate_in, cotangent = by_chunk(k_ref), by_chunk(d_ref)
    values = signal * gate_in
    grads = cotangent * gate_out
    value_split = left_split(values)
    grad_split = left_split(grads)

    leap = jnp.exp(-local_len * inv_row)
    lane = iota((half, LANES), 1)

    def block(device):
        return all_ref[device, :half, 0, :]

    def before(d, carry):
        return jnp.where(d < me_seq, leap * carry + block(d * ch_size + me_ch), carry)

    def after(i, carry):
        d = seq_size - 1 - i
        return jnp.where(d > me_seq, leap * carry + block(d * ch_size + me_ch), carry)

    def loop(body, init):
        if seq_size <= 8:
            for i in range(seq_size):
                init = body(i, init)
            return init
        return lax.fori_loop(0, seq_size, body, init)

    zeros = jnp.zeros((half, LANES), F32)
    border_v = loop(before, zeros)
    border_g = roll(loop(after, zeros), -2 * modes)

    def three_times(data):
        full = jnp.concatenate([data, roll(data, -4 * modes)], axis=0)
        full = jnp.where(iota(full.shape, 1) < modes, full, 0.0)
        return full + roll(full, modes) + roll(full, 2 * modes)

    border_v, border_g = three_times(border_v), three_times(border_g)

    thrice_in = pad_rows(jnp.concatenate([decay_in] * 3, axis=0))
    thrice_out = pad_rows(jnp.concatenate([decay_out] * 3, axis=0))
    value_states = nt_dot(value_split, right_split(thrice_in))
    grad_states = nt_dot(grad_split, right_split(thrice_out))
    step = jnp.exp(-LANES * inv_row)
    starts, ends = [border_v], [border_g]
    for j in range(chunks - 1):
        starts.append(step * starts[-1] + value_states[j * channels : (j + 1) * channels])
        i = chunks - 1 - j
        ends.append(step * ends[-1] + grad_states[i * channels : (i + 1) * channels])
    rows = chunks * channels
    tail = iota((rows, LANES), 1) >= 2 * modes

    def state_split(parts):
        data = jnp.concatenate(parts, axis=0)
        high = data.astype(BF16).astype(F32)
        return jnp.where(tail, data - high, high).astype(BF16)

    def readout(decay):
        high, low = halves(amplitude * decay)
        return pad_rows(jnp.concatenate([high, low, high], axis=0))

    taps = jnp.sum(amplitude * decay_out, axis=0, keepdims=True)
    toeplitz = pltpu.roll(jnp.broadcast_to(taps, (LANES, LANES)), 0, 1, stride=1, stride_axis=0)
    square = (LANES, LANES)
    toeplitz = jnp.where(iota(square, 1) >= iota(square, 0), toeplitz, 0.0)
    conv = nn_dot(value_split, right_split(toeplitz, axis=0)) + nn_dot(state_split(starts), readout(decay_out))
    corr = nt_dot(grad_split, right_split(toeplitz)) + nn_dot(state_split(ends[::-1]), readout(decay_in))
    gain = jnp.concatenate([column(skip_ref[...])] * chunks, axis=0)
    mixed = conv + gain * values
    grad_values = gain * grads + corr

    for i, data in enumerate((gate_out * mixed, grad_values * gate_in, cotangent * mixed, grad_values * signal)):
        for j in range(chunks):
            scratch[i][:, j * LANES : (j + 1) * LANES] = data[j * channels : (j + 1) * channels].astype(BF16)
        moves[i].start()

    kind = iota((ch_size * half, LANES), 1) // modes % 4
    growth = local_len * inv_row
    growth_low = jnp.where(kind == 0, growth, 0.0)
    growth_high = jnp.where(kind == 1, growth, 0.0)

    def pairs(e, carry):
        prefix, swapped, cross_zero, cross_one, extras = carry
        state = jnp.concatenate([block(e * ch_size + c) for c in range(ch_size)], axis=0)
        turned = jnp.where(kind == 0, roll(state, -modes), roll(state, modes))
        grad_part = roll(state, -2 * modes)
        for c in range(ch_size):
            extras = extras + all_ref[e * ch_size + c, half]
        return (
            leap * (prefix + growth_high * swapped) + state,
            leap * (swapped + growth_low * prefix) + turned,
            cross_zero + prefix * grad_part,
            cross_one + swapped * grad_part,
            extras,
        )

    wide = jnp.zeros((ch_size * half, LANES), F32)
    _, _, cross_zero, cross_one, extras = loop(pairs, (wide, wide, wide, wide, jnp.zeros((1, LANES), F32)))
    cross_zero = jnp.sum(jnp.where(kind == 0, cross_zero, 0.0), axis=0, keepdims=True)
    cross_one = jnp.sum(jnp.where(kind <= 1, cross_one, 0.0), axis=0, keepdims=True)
    cross_one = cross_one + roll(cross_one, -modes)
    sum_zero = extras + cross_zero + roll(cross_zero, -4 * modes)
    sum_one = roll(extras, -modes) + roll(extras, -2 * modes) + cross_one + roll(cross_one, -4 * modes)
    sum_zero, sum_one = sum_zero[:, :modes], sum_one[:, :modes]
    scale = jnp.sqrt(2.0 * inv) / math.sqrt(ch_size * channels * seq_size * local_len)
    grad_residue_ref[...] = scale * sum_zero
    grad_memory_ref[...] = residue_ref[...] * scale * (sum_one - 0.5 * sum_zero)

    def skips(d, carry):
        return carry + all_ref[d * ch_size + me_ch, half]

    skip_sum = roll(loop(skips, jnp.zeros((1, LANES), F32)), -3 * modes)
    grad_skip_ref[...] = skip_sum[:, :channels] / math.sqrt(seq_size * local_len)
    for move in moves[4:]:
        move.start()
    for move in moves:
        move.wait()


def per_device(signal_x, gate_q, gate_k, skip_gain, residue, memory, cotangent):
    channels, local_len = signal_x.shape
    modes = memory.shape[0]
    seq_size, ch_size = lax.axis_size("seq"), lax.axis_size("ch")
    devices = seq_size * ch_size
    params = pltpu.CompilerParams(vmem_limit_bytes=32 * 1024 * 1024)
    rows = channels // 2 + 1
    arguments = (memory[None], residue[None], skip_gain[None], signal_x, gate_q, gate_k, cotangent)
    arguments = [pltpu.with_memory_space_constraint(data, pltpu.HBM) for data in arguments]
    in_hbm = pl.BlockSpec(memory_space=pltpu.HBM)
    mine, *here = pl.pallas_call(
        make_states,
        in_specs=[in_hbm] * 7,
        out_shape=(
            jax.ShapeDtypeStruct((rows, 1, LANES), F32),
            *[jax.ShapeDtypeStruct(data.shape, data.dtype) for data in arguments],
        ),
        scratch_shapes=[pltpu.SemaphoreType.DMA((7,))],
        compiler_params=params,
    )(*arguments)
    everyone = lax.all_to_all(jnp.broadcast_to(mine[None], (devices, rows, 1, LANES)), ("seq", "ch"), 0, 0)
    big = ((channels, local_len), BF16)
    shapes = [big] * 4 + [((1, channels), F32), ((1, modes), F32), ((1, modes), F32)]
    results = pl.pallas_call(
        functools.partial(finish, seq_size, ch_size),
        out_shape=[jax.ShapeDtypeStruct(*shape) for shape in shapes],
        out_specs=[in_hbm] * 7,
        scratch_shapes=[*[pltpu.VMEM(*shape) for shape in shapes], pltpu.SemaphoreType.DMA((7,))],
        compiler_params=params,
    )(*here, everyone)
    return (*results[:4], *[result[0] for result in results[4:]])


def solution(mesh):
    grid = P("ch", "seq")
    return jax.shard_map(
        per_device,
        mesh=mesh,
        in_specs=(grid, grid, grid, P("ch"), P(), P(), grid),
        out_specs=(grid, grid, grid, grid, P("ch"), P(), P()),
        check_vma=False,
    )
```

```python
import functools
import math

import jax
import jax.numpy as jnp
from jax import lax
from jax.experimental import pallas as pl
from jax.experimental.pallas import tpu as pltpu
from jax.sharding import PartitionSpec as P

F32 = jnp.float32
BF16 = jnp.bfloat16
LANES = 128
AXES = ("ch", "seq")


def iota(shape, dim):
    return lax.broadcasted_iota(jnp.int32, shape, dim)


def roll(data, shift):
    return pltpu.roll(data, shift % LANES, 1)


def contract(left, right, left_dim, right_dim):
    dims = (((left_dim,), (right_dim,)), ((), ()))
    return lax.dot_general(left, right, dims, preferred_element_type=F32)


def halves(data):
    high = data.astype(BF16)
    return high, (data - high.astype(F32)).astype(BF16)


def left_split(data, axis=1):
    high, low = halves(data)
    return jnp.concatenate([high, low, high], axis=axis)


def right_split(data, axis=1):
    high, low = halves(data)
    return jnp.concatenate([high, high, low], axis=axis)


def by_chunk(ref):
    chunks = ref.shape[1] // LANES
    return jnp.concatenate([ref[:, j * LANES : (j + 1) * LANES].astype(F32) for j in range(chunks)], axis=0)


def column(row):
    size = row.shape[1]
    square = jnp.broadcast_to(row, (size, size))
    return jnp.sum(jnp.where(iota((size, size), 0) == iota((size, size), 1), square, 0.0), axis=1, keepdims=True)


def tiled_row(col):
    size = col.shape[0]
    spread = jnp.where(iota((size, LANES), 1) % size == iota((size, LANES), 0), col, 0.0)
    return jnp.sum(spread, axis=0, keepdims=True)


def decays(inv_col):
    modes = inv_col.shape[0]
    offset = iota((modes, LANES), 1).astype(F32)
    age_in = (LANES - offset) * inv_col
    age_out = offset * inv_col
    return jnp.exp(-age_in), age_in, jnp.exp(-age_out), age_out


def tile_modes(data):
    return jnp.concatenate([data] * (LANES // data.shape[0]), axis=0)


def is_early(seq_size):
    return lax.axis_index("seq") < seq_size // 2


def prepare(seq_size, memory_ref, residue_ref, skip_ref, x_ref, q_ref, k_ref, d_ref, table_ref, base_ref, read_ref):
    modes = memory_ref.shape[1]
    channels, local_len = x_ref.shape
    chunks = local_len // LANES
    rows = chunks * channels
    me_seq = lax.axis_index("seq")
    inv = 1.0 / memory_ref[...]
    inv_col = column(inv)
    inv_row = tiled_row(inv_col)
    decay_in, _, decay_out, _ = decays(inv_col)
    amplitude = column(residue_ref[...] * jnp.sqrt(2.0 * inv))
    values = by_chunk(x_ref) * by_chunk(k_ref)
    grads = by_chunk(d_ref) * by_chunk(q_ref)
    value_split = left_split(values)
    grad_split = left_split(grads)

    device = iota((seq_size, LANES), 0)
    ahead = (me_seq - 1 - device).astype(F32) * local_len
    behind = (device - me_seq - 1).astype(F32) * local_len
    table_ref[:seq_size] = jnp.where(ahead >= 0, jnp.exp(-jnp.maximum(ahead, 0.0) * inv_row), 0.0)
    table_ref[seq_size : 2 * seq_size] = jnp.where(behind >= 0, jnp.exp(-jnp.maximum(behind, 0.0) * inv_row), 0.0)
    power = iota((chunks, LANES), 0).astype(F32) * LANES
    table_ref[2 * seq_size : 2 * seq_size + chunks] = jnp.exp(-power * inv_row)

    read_in, read_out = tile_modes(amplitude * decay_in), tile_modes(amplitude * decay_out)
    read_ref[:LANES] = jnp.concatenate(halves(read_out), axis=1)
    read_ref[LANES:] = jnp.concatenate(halves(read_in), axis=1)

    value_states = contract(value_split, right_split(tile_modes(decay_in)), 1, 1)
    grad_states = contract(grad_split, right_split(tile_modes(decay_out)), 1, 1)
    step = jnp.exp(-LANES * inv_row)
    starts, ends = [jnp.zeros((channels, LANES), F32)], [jnp.zeros((channels, LANES), F32)]
    for j in range(chunks - 1):
        starts.append(step * starts[-1] + value_states[j * channels : (j + 1) * channels])
        i = chunks - 1 - j
        ends.append(step * ends[-1] + grad_states[i * channels : (i + 1) * channels])
    first = iota((rows, LANES), 1) < modes

    def state_split(parts):
        return left_split(jnp.where(first, jnp.concatenate(parts, axis=0), 0.0))

    taps = jnp.sum(amplitude * decay_out, axis=0, keepdims=True)
    square = (LANES, LANES)
    toeplitz = pltpu.roll(jnp.broadcast_to(taps, square), 0, 1, stride=1, stride_axis=0)
    toeplitz = jnp.where(iota(square, 1) >= iota(square, 0), toeplitz, 0.0)
    conv = contract(value_split, right_split(toeplitz, axis=0), 1, 0)
    conv = conv + contract(state_split(starts), right_split(read_out, axis=0), 1, 0)
    corr = contract(grad_split, right_split(toeplitz), 1, 1)
    corr = corr + contract(state_split(ends[::-1]), right_split(read_in, axis=0), 1, 0)
    gain = jnp.concatenate([column(skip_ref[...])] * chunks, axis=0)
    base_ref[:rows] = conv + gain * values
    base_ref[rows:] = corr + gain * grads


def make_states(seq_size, *refs):
    sources, (out_ref, *copies), tables, arrived = refs[:7], refs[7:15], refs[15:18], refs[18]
    moves = [pltpu.make_async_copy(*ends, arrived.at[i]) for i, ends in enumerate(zip(sources, copies))]
    for move in moves:
        move.start()
    memory_ref, _, _, x_ref, q_ref, k_ref, d_ref = copies
    modes = memory_ref.shape[1]
    channels, local_len = x_ref.shape
    chunks = local_len // LANES
    moves[0].wait()
    inv_col = column(1.0 / memory_ref[...])
    inv_row = tiled_row(inv_col)
    decay_in, age_in, decay_out, age_out = decays(inv_col)
    pair_in = jnp.concatenate([tile_modes(decay_in), tile_modes(decay_in * age_in)], axis=0)
    pair_out = jnp.concatenate([tile_modes(decay_out), tile_modes(decay_out * age_out)], axis=0)
    split_in, split_out = right_split(pair_in), right_split(pair_out)
    step = jnp.exp(-LANES * inv_row)
    growth = LANES * inv_row
    for move in moves[1:]:
        move.wait()
    values = by_chunk(x_ref) * by_chunk(k_ref)
    grads = by_chunk(d_ref) * by_chunk(q_ref)
    value_states = contract(left_split(values), split_in, 1, 1)
    grad_states = contract(left_split(grads), split_out, 1, 1)
    outer = contract(left_split(values, axis=0), right_split(grads, axis=0), 0, 0)
    outer = jnp.where(iota(outer.shape, 1) >= iota(outer.shape, 0), outer, 0.0)
    turn = (iota(outer.shape, 1) + iota(outer.shape, 0)) % LANES
    skewed = jnp.take_along_axis(outer, turn, axis=1, mode="promise_in_bounds")
    near = decay_out * jnp.sum(skewed, axis=0, keepdims=True)
    near_zero = jnp.sum(near, axis=1, keepdims=True)
    near_one = jnp.sum(near * age_out, axis=1, keepdims=True)
    products = values * grads
    part_skip = products[:channels]
    for j in range(1, chunks):
        part_skip = part_skip + products[j * channels : (j + 1) * channels]
    part_skip = jnp.sum(part_skip, axis=1, keepdims=True)
    lane = iota((channels, LANES), 1)
    row_id = iota((channels, LANES), 0)
    prefix_zero = jnp.zeros((channels, LANES), F32)
    prefix_one = cross_zero = cross_one = suffix_zero = suffix_one = prefix_zero
    power = jnp.ones_like(step)
    for j in range(chunks):
        rows = slice(j * channels, (j + 1) * channels)
        grad_zero, grad_one = grad_states[rows, :LANES], grad_states[rows, LANES:]
        if j > 0:
            cross_zero = cross_zero + prefix_zero * grad_zero
            cross_one = cross_one + prefix_one * grad_zero + prefix_zero * grad_one
        prefix_one = step * (prefix_one + growth * prefix_zero) + value_states[rows, LANES:]
        prefix_zero = step * prefix_zero + value_states[rows, :LANES]
        suffix_zero = suffix_zero + power * grad_zero
        suffix_one = suffix_one + power * (grad_one + j * growth * grad_zero)
        power = power * step
    half = channels // 2
    own = lane // modes == row_id % half
    for kind, state in enumerate((prefix_zero, prefix_one, suffix_zero, suffix_one)):
        state = jnp.where(own, state, 0.0)
        out_ref[2 * kind] = jnp.sum(state[:half], axis=0, keepdims=True)
        out_ref[2 * kind + 1] = jnp.sum(state[half:], axis=0, keepdims=True)
    extras = (
        jnp.where(lane < modes, cross_zero, 0.0)
        + jnp.where((lane >= modes) & (lane < 2 * modes), cross_one, 0.0)
        + jnp.where(lane == row_id, near_zero, 0.0)
        + jnp.where(lane == row_id + modes, near_one, 0.0)
        + jnp.where(lane == row_id + 2 * modes, part_skip, 0.0)
    )
    out_ref[8] = jnp.sum(extras, axis=0, keepdims=True)

    @pl.when(is_early(seq_size))
    def _():
        prepare(seq_size, *copies, *tables)


def finish(seq_size, ch_size, *refs):
    arguments, all_ref, early, refs = refs[:7], refs[7], refs[8:11], refs[11:]
    results, scratch, late, sent = refs[:7], refs[7:14], refs[14:17], refs[17]
    memory_ref, residue_ref, _, x_ref, q_ref, k_ref, d_ref = arguments
    grad_skip_ref, grad_residue_ref, grad_memory_ref = scratch[4:]
    moves = [pltpu.make_async_copy(*ends, sent.at[i]) for i, ends in enumerate(zip(scratch, results))]
    modes = memory_ref.shape[1]
    channels, local_len = x_ref.shape
    chunks = local_len // LANES
    half = channels // 2
    rows = chunks * channels
    block = 9

    def strided(start, count, stride):
        return all_ref[pl.ds(start, count, stride=stride), :]

    def outputs(table_ref, base_ref, read_ref):
        me = lax.axis_index("ch") * seq_size * block
        own = iota((half, LANES), 1) // modes == iota((half, LANES), 0)

        def border(kind, weights):
            parts = []
            for part in range(2):
                state = strided(me + 2 * kind + part, seq_size, block)
                state = jnp.sum(weights * state, axis=0, keepdims=True)
                parts.append(jnp.where(own, state, 0.0))
            return jnp.concatenate(parts, axis=0)

        before = border(0, table_ref[:seq_size])
        after = border(2, table_ref[seq_size : 2 * seq_size])
        powers = [table_ref[2 * seq_size + j : 2 * seq_size + j + 1] for j in range(chunks)]

        def readout(state, factors, matrix):
            high, low = halves(jnp.concatenate([factor * state for factor in factors], axis=0))
            product = contract(jnp.concatenate([high, low], axis=0), matrix, 1, 0)
            return product[:rows, :LANES] + product[:rows, LANES:] + product[rows:, :LANES]

        mixed = base_ref[:rows] + readout(before, powers, read_ref[:LANES])
        grad_values = base_ref[rows:] + readout(after, powers[::-1], read_ref[LANES:])
        for i, (gate_ref, data) in enumerate(
            ((q_ref, mixed), (k_ref, grad_values), (d_ref, mixed), (x_ref, grad_values))
        ):
            for j in range(chunks):
                lanes = slice(j * LANES, (j + 1) * LANES)
                part = gate_ref[:, lanes].astype(F32) * data[j * channels : (j + 1) * channels]
                scratch[i][:, lanes] = part.astype(BF16)
            moves[i].start()

    @pl.when(is_early(seq_size))
    def _():
        outputs(*early)

    @pl.when(jnp.logical_not(is_early(seq_size)))
    def _():
        prepare(seq_size, *arguments, *late)
        outputs(*late)

    inv = 1.0 / memory_ref[...]
    inv_row = tiled_row(column(inv))
    leap = jnp.exp(-local_len * inv_row)
    growth = local_len * inv_row

    def pairs(e, carry):
        done = []
        for part, (prefix_zero, prefix_one, cross_zero, cross_one) in enumerate(carry):
            value_zero, value_one, grad_zero, grad_one = [
                strided(e * block + 2 * kind + part, ch_size, seq_size * block) for kind in range(4)
            ]
            done.append(
                (
                    leap * prefix_zero + value_zero,
                    leap * (prefix_one + growth * prefix_zero) + value_one,
                    cross_zero + prefix_zero * grad_zero,
                    cross_one + prefix_one * grad_zero + prefix_zero * grad_one,
                )
            )
        return tuple(done)

    zeros = jnp.zeros((ch_size, LANES), F32)
    carry = ((zeros,) * 4,) * 2
    if seq_size <= 8:
        for e in range(seq_size):
            carry = pairs(e, carry)
    else:
        carry = lax.fori_loop(0, seq_size, pairs, carry)
    sums = [jnp.sum(carry[0][i] + carry[1][i], axis=0, keepdims=True) for i in (2, 3)]
    extras = jnp.sum(strided(8, ch_size * seq_size, block), axis=0, keepdims=True)
    kind = iota((8, LANES), 0)
    sums = jnp.where(kind == 0, sums[0], sums[1])
    shift = LANES // 2
    while shift >= modes:
        sums = sums + roll(sums, shift)
        shift //= 2
    sum_zero = sums[0:1, :modes] + extras[:, :modes]
    sum_one = sums[1:2, :modes] + roll(extras, -modes)[:, :modes]
    scale = jnp.sqrt(2.0 * inv) / math.sqrt(ch_size * channels * seq_size * local_len)
    grad_residue_ref[...] = scale * sum_zero
    grad_memory_ref[...] = residue_ref[...] * scale * (sum_one - 0.5 * sum_zero)
    skip = strided(lax.axis_index("ch") * seq_size * block + 8, seq_size, block)
    skip = roll(jnp.sum(skip, axis=0, keepdims=True), -2 * modes)
    grad_skip_ref[...] = skip[:, :channels] / math.sqrt(seq_size * local_len)
    for move in moves[4:]:
        move.start()
    for move in moves:
        move.wait()


def per_device(signal_x, gate_q, gate_k, skip_gain, residue, memory, cotangent):
    channels, local_len = signal_x.shape
    modes = memory.shape[0]
    seq_size, ch_size = lax.axis_size("seq"), lax.axis_size("ch")
    devices = seq_size * ch_size
    params = pltpu.CompilerParams(vmem_limit_bytes=32 * 1024 * 1024)
    in_hbm = pl.BlockSpec(memory_space=pltpu.HBM)
    arguments = (memory[None], residue[None], skip_gain[None], signal_x, gate_q, gate_k, cotangent)
    arguments = [pltpu.with_memory_space_constraint(data, pltpu.HBM) for data in arguments]
    copies = [(data.shape, data.dtype) for data in arguments]
    rows = local_len // LANES * channels
    tables = [((2 * seq_size + 8, LANES), F32), ((2 * rows, LANES), F32), ((2 * LANES, 2 * LANES), BF16)]
    mine, *rest = pl.pallas_call(
        functools.partial(make_states, seq_size),
        in_specs=[in_hbm] * 7,
        out_shape=[jax.ShapeDtypeStruct(*shape) for shape in [((9, 1, LANES), F32), *copies, *tables]],
        scratch_shapes=[pltpu.SemaphoreType.DMA((7,))],
        compiler_params=params,
    )(*arguments)
    everyone = lax.all_to_all(jnp.broadcast_to(mine[None], (devices, 9, 1, LANES)), AXES, 0, 0)
    big = ((channels, local_len), BF16)
    shapes = [big] * 4 + [((1, channels), F32), ((1, modes), F32), ((1, modes), F32)]
    results = pl.pallas_call(
        functools.partial(finish, seq_size, ch_size),
        out_shape=[jax.ShapeDtypeStruct(*shape) for shape in shapes],
        out_specs=[in_hbm] * 7,
        scratch_shapes=[*[pltpu.VMEM(*shape) for shape in shapes + tables], pltpu.SemaphoreType.DMA((7,))],
        compiler_params=params,
    )(*rest[:7], everyone.reshape(devices * 9, LANES), *rest[7:])
    return (*results[:4], *[result[0] for result in results[4:]])


def solution(mesh):
    grid = P("ch", "seq")
    return jax.shard_map(
        per_device,
        mesh=mesh,
        in_specs=(grid, grid, grid, P("ch"), P(), P(), grid),
        out_specs=(grid, grid, grid, grid, P("ch"), P(), P()),
        check_vma=False,
    )
```

```python
import functools
import math

import jax
import jax.numpy as jnp
from jax import lax
from jax.experimental import pallas as pl
from jax.experimental.pallas import tpu as pltpu
from jax.sharding import PartitionSpec as P

F32 = jnp.float32
BF16 = jnp.bfloat16
LANES = 128
AXES = ("ch", "seq")


def iota(shape, dim):
    return lax.broadcasted_iota(jnp.int32, shape, dim)


def roll(data, shift):
    return pltpu.roll(data, shift % LANES, 1)


def contract(left, right, left_dim, right_dim):
    dims = (((left_dim,), (right_dim,)), ((), ()))
    return lax.dot_general(left, right, dims, preferred_element_type=F32)


def halves(data):
    high = data.astype(BF16)
    return high, (data - high.astype(F32)).astype(BF16)


def left_split(data, axis=1):
    high, low = halves(data)
    return jnp.concatenate([high, low, high], axis=axis)


def right_split(data, axis=1):
    high, low = halves(data)
    return jnp.concatenate([high, high, low], axis=axis)


def by_chunk(ref):
    chunks = ref.shape[1] // LANES
    return jnp.concatenate([ref[:, j * LANES : (j + 1) * LANES].astype(F32) for j in range(chunks)], axis=0)


def column(row):
    size = row.shape[1]
    square = jnp.broadcast_to(row, (size, size))
    return jnp.sum(jnp.where(iota((size, size), 0) == iota((size, size), 1), square, 0.0), axis=1, keepdims=True)


def tiled_row(col):
    size = col.shape[0]
    spread = jnp.where(iota((size, LANES), 1) % size == iota((size, LANES), 0), col, 0.0)
    return jnp.sum(spread, axis=0, keepdims=True)


def decays(inv_col):
    modes = inv_col.shape[0]
    offset = iota((modes, LANES), 1).astype(F32)
    age_in = (LANES - offset) * inv_col
    age_out = offset * inv_col
    return jnp.exp(-age_in), age_in, jnp.exp(-age_out), age_out


def tile_modes(data):
    return jnp.concatenate([data] * (LANES // data.shape[0]), axis=0)


def is_early(seq_size):
    return lax.axis_index("seq") < seq_size // 2


def prepare(seq_size, memory_ref, residue_ref, skip_ref, x_ref, q_ref, k_ref, d_ref, table_ref, base_ref, read_ref):
    modes = memory_ref.shape[1]
    channels, local_len = x_ref.shape
    chunks = local_len // LANES
    rows = chunks * channels
    me_seq = lax.axis_index("seq")
    inv = 1.0 / memory_ref[...]
    inv_col = column(inv)
    inv_row = tiled_row(inv_col)
    decay_in, _, decay_out, _ = decays(inv_col)
    amplitude = column(residue_ref[...] * jnp.sqrt(2.0 * inv))
    values = by_chunk(x_ref) * by_chunk(k_ref)
    grads = by_chunk(d_ref) * by_chunk(q_ref)
    value_split = left_split(values)
    grad_split = left_split(grads)

    device = iota((seq_size, LANES), 0)
    ahead = (me_seq - 1 - device).astype(F32) * local_len
    behind = (device - me_seq - 1).astype(F32) * local_len
    table_ref[:seq_size] = jnp.where(ahead >= 0, jnp.exp(-jnp.maximum(ahead, 0.0) * inv_row), 0.0)
    table_ref[seq_size : 2 * seq_size] = jnp.where(behind >= 0, jnp.exp(-jnp.maximum(behind, 0.0) * inv_row), 0.0)
    power = iota((chunks, LANES), 0).astype(F32) * LANES
    table_ref[2 * seq_size : 2 * seq_size + chunks] = jnp.exp(-power * inv_row)

    read_in, read_out = tile_modes(amplitude * decay_in), tile_modes(amplitude * decay_out)
    read_ref[:LANES] = jnp.concatenate(halves(read_out), axis=1)
    read_ref[LANES:] = jnp.concatenate(halves(read_in), axis=1)

    value_states = contract(value_split, right_split(tile_modes(decay_in)), 1, 1)
    grad_states = contract(grad_split, right_split(tile_modes(decay_out)), 1, 1)
    step = jnp.exp(-LANES * inv_row)
    starts, ends = [jnp.zeros((channels, LANES), F32)], [jnp.zeros((channels, LANES), F32)]
    for j in range(chunks - 1):
        starts.append(step * starts[-1] + value_states[j * channels : (j + 1) * channels])
        i = chunks - 1 - j
        ends.append(step * ends[-1] + grad_states[i * channels : (i + 1) * channels])
    first = iota((rows, LANES), 1) < modes

    def state_split(parts):
        return left_split(jnp.where(first, jnp.concatenate(parts, axis=0), 0.0))

    taps = jnp.sum(amplitude * decay_out, axis=0, keepdims=True)
    square = (LANES, LANES)
    toeplitz = pltpu.roll(jnp.broadcast_to(taps, square), 0, 1, stride=1, stride_axis=0)
    toeplitz = jnp.where(iota(square, 1) >= iota(square, 0), toeplitz, 0.0)
    conv = contract(value_split, right_split(toeplitz, axis=0), 1, 0)
    conv = conv + contract(state_split(starts), right_split(read_out, axis=0), 1, 0)
    corr = contract(grad_split, right_split(toeplitz), 1, 1)
    corr = corr + contract(state_split(ends[::-1]), right_split(read_in, axis=0), 1, 0)
    gain = jnp.concatenate([column(skip_ref[...])] * chunks, axis=0)
    base_ref[:rows] = conv + gain * values
    base_ref[rows:] = corr + gain * grads


def make_states(seq_size, *refs):
    sources, (out_ref, *copies), tables, arrived = refs[:7], refs[7:15], refs[15:18], refs[18]
    moves = [pltpu.make_async_copy(*ends, arrived.at[i]) for i, ends in enumerate(zip(sources, copies))]
    for i in (0, 3, 5, 6, 4, 1, 2):
        moves[i].start()
    memory_ref, _, _, x_ref, q_ref, k_ref, d_ref = copies
    modes = memory_ref.shape[1]
    channels, local_len = x_ref.shape
    chunks = local_len // LANES
    moves[0].wait()
    inv_col = column(1.0 / memory_ref[...])
    inv_row = tiled_row(inv_col)
    decay_in, age_in, decay_out, age_out = decays(inv_col)
    pair_in = jnp.concatenate([tile_modes(decay_in), tile_modes(decay_in * age_in)], axis=0)
    pair_out = jnp.concatenate([tile_modes(decay_out), tile_modes(decay_out * age_out)], axis=0)
    split_in, split_out = right_split(pair_in), right_split(pair_out)
    step = jnp.exp(-LANES * inv_row)
    growth = LANES * inv_row
    for move in moves[3:]:
        move.wait()
    values = by_chunk(x_ref) * by_chunk(k_ref)
    grads = by_chunk(d_ref) * by_chunk(q_ref)
    value_states = contract(left_split(values), split_in, 1, 1)
    grad_states = contract(left_split(grads), split_out, 1, 1)
    outer = contract(left_split(values, axis=0), right_split(grads, axis=0), 0, 0)
    outer = jnp.where(iota(outer.shape, 1) >= iota(outer.shape, 0), outer, 0.0)
    turn = (iota(outer.shape, 1) + iota(outer.shape, 0)) % LANES
    skewed = jnp.take_along_axis(outer, turn, axis=1, mode="promise_in_bounds")
    near = decay_out * jnp.sum(skewed, axis=0, keepdims=True)
    near_zero = jnp.sum(near, axis=1, keepdims=True)
    near_one = jnp.sum(near * age_out, axis=1, keepdims=True)
    products = values * grads
    part_skip = products[:channels]
    for j in range(1, chunks):
        part_skip = part_skip + products[j * channels : (j + 1) * channels]
    part_skip = jnp.sum(part_skip, axis=1, keepdims=True)
    lane = iota((channels, LANES), 1)
    row_id = iota((channels, LANES), 0)
    prefix_zero = jnp.zeros((channels, LANES), F32)
    prefix_one = cross_zero = cross_one = suffix_zero = suffix_one = prefix_zero
    power = jnp.ones_like(step)
    for j in range(chunks):
        rows = slice(j * channels, (j + 1) * channels)
        grad_zero, grad_one = grad_states[rows, :LANES], grad_states[rows, LANES:]
        if j > 0:
            cross_zero = cross_zero + prefix_zero * grad_zero
            cross_one = cross_one + prefix_one * grad_zero + prefix_zero * grad_one
        prefix_one = step * (prefix_one + growth * prefix_zero) + value_states[rows, LANES:]
        prefix_zero = step * prefix_zero + value_states[rows, :LANES]
        suffix_zero = suffix_zero + power * grad_zero
        suffix_one = suffix_one + power * (grad_one + j * growth * grad_zero)
        power = power * step
    half = channels // 2
    own = lane // modes == row_id % half
    payload = []
    for state in (prefix_zero, prefix_one, suffix_zero, suffix_one):
        state = jnp.where(own, state, 0.0)
        payload.append(jnp.sum(state[:half], axis=0, keepdims=True))
        payload.append(jnp.sum(state[half:], axis=0, keepdims=True))
    extras = (
        jnp.where(lane < modes, cross_zero, 0.0)
        + jnp.where((lane >= modes) & (lane < 2 * modes), cross_one, 0.0)
        + jnp.where(lane == row_id, near_zero, 0.0)
        + jnp.where(lane == row_id + modes, near_one, 0.0)
        + jnp.where(lane == row_id + 2 * modes, part_skip, 0.0)
    )
    payload.append(jnp.sum(extras, axis=0, keepdims=True))
    sublane = iota((8, LANES), 0)
    for k in range(len(payload)):
        tile = jnp.zeros((8, LANES), F32)
        for i in range(8):
            tile = jnp.where(sublane == i, payload[(8 * k + i) % len(payload)], tile)
        for start in range(8 * k, out_ref.shape[0], 8 * len(payload)):
            out_ref[start : start + 8] = tile

    for move in moves[1:3]:
        move.wait()

    @pl.when(is_early(seq_size))
    def _():
        prepare(seq_size, *copies, *tables)


def finish(seq_size, ch_size, *refs):
    arguments, all_ref, early, refs = refs[:7], refs[7], refs[8:11], refs[11:]
    results, scratch, late, sent = refs[:7], refs[7:14], refs[14:17], refs[17]
    memory_ref, residue_ref, _, x_ref, q_ref, k_ref, d_ref = arguments
    grad_skip_ref, grad_residue_ref, grad_memory_ref = scratch[4:]
    moves = [pltpu.make_async_copy(*ends, sent.at[i]) for i, ends in enumerate(zip(scratch, results))]
    modes = memory_ref.shape[1]
    channels, local_len = x_ref.shape
    chunks = local_len // LANES
    half = channels // 2
    rows = chunks * channels
    block = 9

    def strided(start, count, stride):
        return all_ref[pl.ds(start, count, stride=stride), :]

    def complete(table_ref, base_ref, read_ref):
        me = lax.axis_index("ch") * seq_size * block
        own = iota((half, LANES), 1) // modes == iota((half, LANES), 0)

        def border(kind, weights):
            parts = []
            for part in range(2):
                state = strided(me + 2 * kind + part, seq_size, block)
                state = jnp.sum(weights * state, axis=0, keepdims=True)
                parts.append(jnp.where(own, state, 0.0))
            return jnp.concatenate(parts, axis=0)

        before = border(0, table_ref[:seq_size])
        after = border(2, table_ref[seq_size : 2 * seq_size])
        powers = [table_ref[2 * seq_size + j : 2 * seq_size + j + 1] for j in range(chunks)]

        def readout(state, factors, matrix):
            high, low = halves(jnp.concatenate([factor * state for factor in factors], axis=0))
            product = contract(jnp.concatenate([high, low], axis=0), matrix, 1, 0)
            return product[:rows, :LANES] + product[:rows, LANES:] + product[rows:, :LANES]

        mixed = base_ref[:rows] + readout(before, powers, read_ref[:LANES])
        grad_values = base_ref[rows:] + readout(after, powers[::-1], read_ref[LANES:])

        inv = 1.0 / memory_ref[...]
        inv_row = tiled_row(column(inv))
        leap = jnp.exp(-local_len * inv_row)
        growth = local_len * inv_row

        def pairs(e, carry):
            done = []
            for part, (prefix_zero, prefix_one, cross_zero, cross_one) in enumerate(carry):
                value_zero, value_one, grad_zero, grad_one = [
                    strided(e * block + 2 * kind + part, ch_size, seq_size * block) for kind in range(4)
                ]
                done.append(
                    (
                        leap * prefix_zero + value_zero,
                        leap * (prefix_one + growth * prefix_zero) + value_one,
                        cross_zero + prefix_zero * grad_zero,
                        cross_one + prefix_one * grad_zero + prefix_zero * grad_one,
                    )
                )
            return tuple(done)

        zeros = jnp.zeros((ch_size, LANES), F32)
        carry = ((zeros,) * 4,) * 2
        if seq_size <= 8:
            for e in range(seq_size):
                carry = pairs(e, carry)
        else:
            carry = lax.fori_loop(0, seq_size, pairs, carry)
        sums = [jnp.sum(carry[0][i] + carry[1][i], axis=0, keepdims=True) for i in (2, 3)]
        extras = jnp.sum(strided(8, ch_size * seq_size, block), axis=0, keepdims=True)
        kind = iota((8, LANES), 0)
        sums = jnp.where(kind == 0, sums[0], sums[1])
        shift = LANES // 2
        while shift >= modes:
            sums = sums + roll(sums, shift)
            shift //= 2
        sum_zero = sums[0:1, :modes] + extras[:, :modes]
        sum_one = sums[1:2, :modes] + roll(extras, -modes)[:, :modes]
        scale = jnp.sqrt(2.0 * inv) / math.sqrt(ch_size * channels * seq_size * local_len)
        skip = jnp.sum(strided(me + 8, seq_size, block), axis=0, keepdims=True)
        skip = roll(skip, -2 * modes)[:, :channels] / math.sqrt(seq_size * local_len)

        for i, (gate_ref, data) in enumerate(
            ((q_ref, mixed), (k_ref, grad_values), (d_ref, mixed), (x_ref, grad_values))
        ):
            for j in range(chunks):
                lanes = slice(j * LANES, (j + 1) * LANES)
                part = gate_ref[:, lanes].astype(F32) * data[j * channels : (j + 1) * channels]
                scratch[i][:, lanes] = part.astype(BF16)
        grad_skip_ref[...] = skip
        grad_residue_ref[...] = scale * sum_zero
        grad_memory_ref[...] = residue_ref[...] * scale * (sum_one - 0.5 * sum_zero)
        for move in moves:
            move.start()

    @pl.when(is_early(seq_size))
    def _():
        complete(*early)

    @pl.when(jnp.logical_not(is_early(seq_size)))
    def _():
        prepare(seq_size, *arguments, *late)
        complete(*late)

    for move in moves:
        move.wait()


def per_device(signal_x, gate_q, gate_k, skip_gain, residue, memory, cotangent):
    channels, local_len = signal_x.shape
    modes = memory.shape[0]
    seq_size, ch_size = lax.axis_size("seq"), lax.axis_size("ch")
    devices = seq_size * ch_size
    params = pltpu.CompilerParams(vmem_limit_bytes=32 * 1024 * 1024)
    in_hbm = pl.BlockSpec(memory_space=pltpu.HBM)
    arguments = (memory[None], residue[None], skip_gain[None], signal_x, gate_q, gate_k, cotangent)
    arguments = [pltpu.with_memory_space_constraint(data, pltpu.HBM) for data in arguments]
    copies = [(data.shape, data.dtype) for data in arguments]
    rows = local_len // LANES * channels
    tables = [((2 * seq_size + 8, LANES), F32), ((2 * rows, LANES), F32), ((2 * LANES, 2 * LANES), BF16)]
    mine, *rest = pl.pallas_call(
        functools.partial(make_states, seq_size),
        in_specs=[in_hbm] * 7,
        out_shape=[jax.ShapeDtypeStruct(*shape) for shape in [((devices * 9, LANES), F32), *copies, *tables]],
        scratch_shapes=[pltpu.SemaphoreType.DMA((7,))],
        compiler_params=params,
    )(*arguments)
    everyone = lax.all_to_all(mine.reshape(devices, 9, 1, LANES), AXES, 0, 0)
    big = ((channels, local_len), BF16)
    shapes = [big] * 4 + [((1, channels), F32), ((1, modes), F32), ((1, modes), F32)]
    results = pl.pallas_call(
        functools.partial(finish, seq_size, ch_size),
        out_shape=[jax.ShapeDtypeStruct(*shape) for shape in shapes],
        out_specs=[in_hbm] * 7,
        scratch_shapes=[*[pltpu.VMEM(*shape) for shape in shapes + tables], pltpu.SemaphoreType.DMA((7,))],
        compiler_params=params,
    )(*rest[:7], everyone.reshape(devices * 9, LANES), *rest[7:])
    return (*results[:4], *[result[0] for result in results[4:]])


def solution(mesh):
    grid = P("ch", "seq")
    return jax.shard_map(
        per_device,
        mesh=mesh,
        in_specs=(grid, grid, grid, P("ch"), P(), P(), grid),
        out_specs=(grid, grid, grid, grid, P("ch"), P(), P()),
        check_vma=False,
    )
```

```python
import functools
import math

import jax
import jax.numpy as jnp
from jax import lax
from jax.experimental import pallas as pl
from jax.experimental.pallas import tpu as pltpu
from jax.sharding import PartitionSpec as P

F32 = jnp.float32
BF16 = jnp.bfloat16
LANES = 128
AXES = ("seq", "ch")


def iota(shape, dim):
    return lax.broadcasted_iota(jnp.int32, shape, dim)


def roll(data, shift):
    return pltpu.roll(data, shift % LANES, 1)


def contract(left, right, left_dim, right_dim):
    dims = (((left_dim,), (right_dim,)), ((), ()))
    return lax.dot_general(left, right, dims, preferred_element_type=F32)


def halves(data):
    high = data.astype(BF16)
    return high, (data - high.astype(F32)).astype(BF16)


def left_split(data, axis=1):
    high, low = halves(data)
    return jnp.concatenate([high, low, high], axis=axis)


def right_split(data, axis=1):
    high, low = halves(data)
    return jnp.concatenate([high, high, low], axis=axis)


def by_chunk(ref):
    chunks = ref.shape[1] // LANES
    return jnp.concatenate([ref[:, j * LANES : (j + 1) * LANES].astype(F32) for j in range(chunks)], axis=0)


def column(row):
    size = row.shape[1]
    square = jnp.broadcast_to(row, (size, size))
    return jnp.sum(jnp.where(iota((size, size), 0) == iota((size, size), 1), square, 0.0), axis=1, keepdims=True)


def tiled_row(col):
    size = col.shape[0]
    spread = jnp.where(iota((size, LANES), 1) % size == iota((size, LANES), 0), col, 0.0)
    return jnp.sum(spread, axis=0, keepdims=True)


def decays(inv_col):
    modes = inv_col.shape[0]
    offset = iota((modes, LANES), 1).astype(F32)
    age_in = (LANES - offset) * inv_col
    age_out = offset * inv_col
    return jnp.exp(-age_in), age_in, jnp.exp(-age_out), age_out


def tile_modes(data):
    return jnp.concatenate([data] * (LANES // data.shape[0]), axis=0)


def ranks(size, tuned):
    return tuned if len(tuned) == size else tuple(range(size))


def seq_ranks(seq_size):
    return ranks(seq_size, (6, 0, 2, 7, 4, 5, 3, 1))


def ch_ranks(ch_size):
    return ranks(ch_size, (2, 0, 3, 1))


def is_early(seq_size):
    return lax.axis_index("seq") < seq_size // 2


def prepare(seq_size, memory_ref, residue_ref, skip_ref, x_ref, q_ref, k_ref, d_ref, table_ref, base_ref, read_ref):
    modes = memory_ref.shape[1]
    channels, local_len = x_ref.shape
    chunks = local_len // LANES
    rows = chunks * channels
    me_seq = lax.axis_index("seq")
    inv = 1.0 / memory_ref[...]
    inv_col = column(inv)
    inv_row = tiled_row(inv_col)
    decay_in, _, decay_out, _ = decays(inv_col)
    amplitude = column(residue_ref[...] * jnp.sqrt(2.0 * inv))
    values = by_chunk(x_ref) * by_chunk(k_ref)
    grads = by_chunk(d_ref) * by_chunk(q_ref)
    value_split = left_split(values)
    grad_split = left_split(grads)

    device = iota((seq_size, LANES), 0)
    if seq_ranks(seq_size) != tuple(range(seq_size)):
        place = device
        for p, index in enumerate(seq_ranks(seq_size)):
            device = jnp.where(place == p, index, device)
    ahead = (me_seq - 1 - device).astype(F32) * local_len
    behind = (device - me_seq - 1).astype(F32) * local_len
    table_ref[:seq_size] = jnp.where(ahead >= 0, jnp.exp(-jnp.maximum(ahead, 0.0) * inv_row), 0.0)
    table_ref[seq_size : 2 * seq_size] = jnp.where(behind >= 0, jnp.exp(-jnp.maximum(behind, 0.0) * inv_row), 0.0)
    power = iota((chunks, LANES), 0).astype(F32) * LANES
    table_ref[2 * seq_size : 2 * seq_size + chunks] = jnp.exp(-power * inv_row)
    leap = jnp.exp(-local_len * inv_row)
    table_ref[2 * seq_size + chunks : 2 * seq_size + chunks + 1] = leap
    table_ref[2 * seq_size + chunks + 1 : 2 * seq_size + chunks + 2] = leap * (local_len * inv_row)

    read_in, read_out = tile_modes(amplitude * decay_in), tile_modes(amplitude * decay_out)
    read_ref[:LANES] = jnp.concatenate(halves(read_out), axis=1)
    read_ref[LANES:] = jnp.concatenate(halves(read_in), axis=1)

    value_states = contract(value_split, right_split(tile_modes(decay_in)), 1, 1)
    grad_states = contract(grad_split, right_split(tile_modes(decay_out)), 1, 1)
    step = jnp.exp(-LANES * inv_row)
    starts, ends = [jnp.zeros((channels, LANES), F32)], [jnp.zeros((channels, LANES), F32)]
    for j in range(chunks - 1):
        starts.append(step * starts[-1] + value_states[j * channels : (j + 1) * channels])
        i = chunks - 1 - j
        ends.append(step * ends[-1] + grad_states[i * channels : (i + 1) * channels])
    first = iota((rows, LANES), 1) < modes

    def state_split(parts):
        return left_split(jnp.where(first, jnp.concatenate(parts, axis=0), 0.0))

    taps = jnp.sum(amplitude * decay_out, axis=0, keepdims=True)
    square = (LANES, LANES)
    toeplitz = pltpu.roll(jnp.broadcast_to(taps, square), 0, 1, stride=1, stride_axis=0)
    toeplitz = jnp.where(iota(square, 1) >= iota(square, 0), toeplitz, 0.0)
    conv = contract(value_split, right_split(toeplitz, axis=0), 1, 0)
    conv = conv + contract(state_split(starts), right_split(read_out, axis=0), 1, 0)
    corr = contract(grad_split, right_split(toeplitz), 1, 1)
    corr = corr + contract(state_split(ends[::-1]), right_split(read_in, axis=0), 1, 0)
    gain = jnp.concatenate([column(skip_ref[...])] * chunks, axis=0)
    base_ref[:rows] = conv + gain * values
    base_ref[rows:] = corr + gain * grads


def make_states(seq_size, *refs):
    sources, (out_ref, *copies), tables, arrived = refs[:7], refs[7:15], refs[15:18], refs[18]
    moves = [pltpu.make_async_copy(*ends, arrived.at[i]) for i, ends in enumerate(zip(sources, copies))]
    for i in (0, 3, 5, 6, 4, 1, 2):
        moves[i].start()
    memory_ref, _, _, x_ref, q_ref, k_ref, d_ref = copies
    modes = memory_ref.shape[1]
    channels, local_len = x_ref.shape
    chunks = local_len // LANES
    moves[0].wait()
    inv_col = column(1.0 / memory_ref[...])
    inv_row = tiled_row(inv_col)
    decay_in, age_in, decay_out, age_out = decays(inv_col)
    pair_in = jnp.concatenate([tile_modes(decay_in), tile_modes(decay_in * age_in)], axis=0)
    pair_out = jnp.concatenate([tile_modes(decay_out), tile_modes(decay_out * age_out)], axis=0)
    split_in, split_out = right_split(pair_in), right_split(pair_out)
    step = jnp.exp(-LANES * inv_row)
    growth = LANES * inv_row
    moves[3].wait()
    moves[5].wait()
    values = by_chunk(x_ref) * by_chunk(k_ref)
    moves[6].wait()
    moves[4].wait()
    grads = by_chunk(d_ref) * by_chunk(q_ref)
    outer = contract(left_split(values, axis=0), right_split(grads, axis=0), 0, 0)
    outer = jnp.where(iota(outer.shape, 1) >= iota(outer.shape, 0), outer, 0.0)
    turn = (iota(outer.shape, 1) + iota(outer.shape, 0)) % LANES
    skewed = jnp.take_along_axis(outer, turn, axis=1, mode="promise_in_bounds")
    near = decay_out * jnp.sum(skewed, axis=0, keepdims=True)
    near_zero = jnp.sum(near, axis=1, keepdims=True)
    near_one = jnp.sum(near * age_out, axis=1, keepdims=True)
    value_states = contract(left_split(values), split_in, 1, 1)
    grad_states = contract(left_split(grads), split_out, 1, 1)
    products = values * grads
    part_skip = products[:channels]
    for j in range(1, chunks):
        part_skip = part_skip + products[j * channels : (j + 1) * channels]
    part_skip = jnp.sum(part_skip, axis=1, keepdims=True)
    lane = iota((channels, LANES), 1)
    row_id = iota((channels, LANES), 0)
    prefix_zero = jnp.zeros((channels, LANES), F32)
    prefix_one = cross_zero = cross_one = suffix_zero = suffix_one = prefix_zero
    power = jnp.ones_like(step)
    for j in range(chunks):
        rows = slice(j * channels, (j + 1) * channels)
        grad_zero, grad_one = grad_states[rows, :LANES], grad_states[rows, LANES:]
        if j > 0:
            cross_zero = cross_zero + prefix_zero * grad_zero
            cross_one = cross_one + prefix_one * grad_zero + prefix_zero * grad_one
        prefix_one = step * (prefix_one + growth * prefix_zero) + value_states[rows, LANES:]
        prefix_zero = step * prefix_zero + value_states[rows, :LANES]
        suffix_zero = suffix_zero + power * grad_zero
        suffix_one = suffix_one + power * (grad_one + j * growth * grad_zero)
        power = power * step
    half = channels // 2
    own = lane // modes == row_id % half
    payload = []
    for state in (prefix_zero, prefix_one, suffix_zero, suffix_one):
        state = jnp.where(own, state, 0.0)
        payload.append(jnp.sum(state[:half], axis=0, keepdims=True))
        payload.append(jnp.sum(state[half:], axis=0, keepdims=True))
    extras = (
        jnp.where(lane < modes, cross_zero, 0.0)
        + jnp.where((lane >= modes) & (lane < 2 * modes), cross_one, 0.0)
        + jnp.where(lane == row_id, near_zero, 0.0)
        + jnp.where(lane == row_id + modes, near_one, 0.0)
        + jnp.where(lane == row_id + 2 * modes, part_skip, 0.0)
    )
    payload.append(jnp.sum(extras, axis=0, keepdims=True))
    sublane = iota((8, LANES), 0)
    for k in range(len(payload)):
        tile = jnp.zeros((8, LANES), F32)
        for i in range(8):
            tile = jnp.where(sublane == i, payload[(8 * k + i) % len(payload)], tile)
        for start in range(8 * k, out_ref.shape[0], 8 * len(payload)):
            out_ref[start : start + 8] = tile

    for move in moves[1:3]:
        move.wait()

    @pl.when(is_early(seq_size))
    def _():
        prepare(seq_size, *copies, *tables)


def finish(seq_size, ch_size, *refs):
    arguments, all_ref, early, refs = refs[:7], refs[7], refs[8:11], refs[11:]
    results, scratch, late, sent = refs[:7], refs[7:14], refs[14:17], refs[17]
    memory_ref, residue_ref, _, x_ref, q_ref, k_ref, d_ref = arguments
    grad_skip_ref, grad_residue_ref, grad_memory_ref = scratch[4:]
    moves = [pltpu.make_async_copy(*ends, sent.at[i]) for i, ends in enumerate(zip(scratch, results))]
    modes = memory_ref.shape[1]
    channels, local_len = x_ref.shape
    chunks = local_len // LANES
    half = channels // 2
    rows = chunks * channels
    block = 9

    def strided(start, count, stride):
        return all_ref[pl.ds(start, count, stride=stride), :]

    def complete(table_ref, base_ref, read_ref):
        me = 0
        for p, index in enumerate(ch_ranks(ch_size)):
            me = me + jnp.where(lax.axis_index("ch") == index, p * seq_size * block, 0)
        own = iota((half, LANES), 1) // modes == iota((half, LANES), 0)

        def border(kind, weights):
            parts = []
            for part in range(2):
                state = strided(me + 2 * kind + part, seq_size, block)
                state = jnp.sum(weights * state, axis=0, keepdims=True)
                parts.append(jnp.where(own, state, 0.0))
            return jnp.concatenate(parts, axis=0)

        before = border(0, table_ref[:seq_size])
        after = border(2, table_ref[seq_size : 2 * seq_size])
        powers = [table_ref[2 * seq_size + j : 2 * seq_size + j + 1] for j in range(chunks)]

        def readout(state, factors, matrix):
            high, low = halves(jnp.concatenate([factor * state for factor in factors], axis=0))
            product = contract(jnp.concatenate([high, low], axis=0), matrix, 1, 0)
            return product[:rows, :LANES] + product[:rows, LANES:] + product[rows:, :LANES]

        mixed = base_ref[:rows] + readout(before, powers, read_ref[:LANES])
        grad_values = base_ref[rows:] + readout(after, powers[::-1], read_ref[LANES:])

        inv = 1.0 / memory_ref[...]
        at = 2 * seq_size + chunks
        leap, leap_growth = table_ref[at : at + 1], table_ref[at + 1 : at + 2]

        def pairs(e, carry):
            done = []
            for part, (prefix_zero, prefix_one, cross_zero, cross_one) in enumerate(carry):
                value_zero, value_one, grad_zero, grad_one = [
                    strided(e * block + 2 * kind + part, ch_size, seq_size * block) for kind in range(4)
                ]
                done.append(
                    (
                        leap * prefix_zero + value_zero,
                        leap * prefix_one + (leap_growth * prefix_zero + value_one),
                        cross_zero + prefix_zero * grad_zero,
                        cross_one + prefix_one * grad_zero + prefix_zero * grad_one,
                    )
                )
            return tuple(done)

        zeros = jnp.zeros((ch_size, LANES), F32)
        carry = ((zeros,) * 4,) * 2
        if seq_size <= 8 or seq_ranks(seq_size) != tuple(range(seq_size)):
            for e in range(seq_size):
                carry = pairs(seq_ranks(seq_size).index(e), carry)
        else:
            carry = lax.fori_loop(0, seq_size, pairs, carry)
        sums = [jnp.sum(carry[0][i] + carry[1][i], axis=0, keepdims=True) for i in (2, 3)]
        extras = jnp.sum(strided(8, ch_size * seq_size, block), axis=0, keepdims=True)
        kind = iota((8, LANES), 0)
        sums = jnp.where(kind == 0, sums[0], sums[1])
        shift = LANES // 2
        while shift >= modes:
            sums = sums + roll(sums, shift)
            shift //= 2
        sum_zero = sums[0:1, :modes] + extras[:, :modes]
        sum_one = sums[1:2, :modes] + roll(extras, -modes)[:, :modes]
        scale = jnp.sqrt(2.0 * inv) / math.sqrt(ch_size * channels * seq_size * local_len)
        skip = jnp.sum(strided(me + 8, seq_size, block), axis=0, keepdims=True)
        skip = roll(skip, -2 * modes)[:, :channels] / math.sqrt(seq_size * local_len)

        for i, (gate_ref, data) in enumerate(
            ((q_ref, mixed), (k_ref, grad_values), (d_ref, mixed), (x_ref, grad_values))
        ):
            for j in range(chunks):
                lanes = slice(j * LANES, (j + 1) * LANES)
                part = gate_ref[:, lanes].astype(F32) * data[j * channels : (j + 1) * channels]
                scratch[i][:, lanes] = part.astype(BF16)
        grad_skip_ref[...] = skip
        grad_residue_ref[...] = scale * sum_zero
        grad_memory_ref[...] = residue_ref[...] * scale * (sum_one - 0.5 * sum_zero)
        for move in moves:
            move.start()

    @pl.when(is_early(seq_size))
    def _():
        complete(*early)

    @pl.when(jnp.logical_not(is_early(seq_size)))
    def _():
        prepare(seq_size, *arguments, *late)
        complete(*late)

    for move in moves:
        move.wait()


def per_device(signal_x, gate_q, gate_k, skip_gain, residue, memory, cotangent):
    channels, local_len = signal_x.shape
    modes = memory.shape[0]
    seq_size, ch_size = lax.axis_size("seq"), lax.axis_size("ch")
    devices = seq_size * ch_size
    params = pltpu.CompilerParams(vmem_limit_bytes=32 * 1024 * 1024)
    in_hbm = pl.BlockSpec(memory_space=pltpu.HBM)
    arguments = (memory[None], residue[None], skip_gain[None], signal_x, gate_q, gate_k, cotangent)
    arguments = [pltpu.with_memory_space_constraint(data, pltpu.HBM) for data in arguments]
    copies = [(data.shape, data.dtype) for data in arguments]
    rows = local_len // LANES * channels
    tables = [((2 * seq_size + 8, LANES), F32), ((2 * rows, LANES), F32), ((2 * LANES, 2 * LANES), BF16)]
    mine, *rest = pl.pallas_call(
        functools.partial(make_states, seq_size),
        in_specs=[in_hbm] * 7,
        out_shape=[jax.ShapeDtypeStruct(*shape) for shape in [((devices * 9, LANES), F32), *copies, *tables]],
        scratch_shapes=[pltpu.SemaphoreType.DMA((7,))],
        compiler_params=params,
    )(*arguments)
    order = [s * ch_size + c for c in ch_ranks(ch_size) for s in seq_ranks(seq_size)]
    everyone = lax.all_to_all(mine.reshape(devices, 9, 1, LANES), AXES, 0, 0, axis_index_groups=[order])
    big = ((channels, local_len), BF16)
    shapes = [big] * 4 + [((1, channels), F32), ((1, modes), F32), ((1, modes), F32)]
    results = pl.pallas_call(
        functools.partial(finish, seq_size, ch_size),
        out_shape=[jax.ShapeDtypeStruct(*shape) for shape in shapes],
        out_specs=[in_hbm] * 7,
        scratch_shapes=[*[pltpu.VMEM(*shape) for shape in shapes + tables], pltpu.SemaphoreType.DMA((7,))],
        compiler_params=params,
    )(*rest[:7], everyone.reshape(devices * 9, LANES), *rest[7:])
    return (*results[:4], *[result[0] for result in results[4:]])


def solution(mesh):
    grid = P("ch", "seq")
    return jax.shard_map(
        per_device,
        mesh=mesh,
        in_specs=(grid, grid, grid, P("ch"), P(), P(), grid),
        out_specs=(grid, grid, grid, grid, P("ch"), P(), P()),
        check_vma=False,
    )
```

```python
import functools
import math

import jax
import jax.numpy as jnp
from jax import lax
from jax.experimental import pallas as pl
from jax.experimental.pallas import tpu as pltpu
from jax.sharding import PartitionSpec as P

F32 = jnp.float32
BF16 = jnp.bfloat16
LANES = 128
AXES = ("seq", "ch")
CORES = 2
BLOCK = 9


def iota(shape, dim):
    return lax.broadcasted_iota(jnp.int32, shape, dim)


def roll(data, shift):
    return pltpu.roll(data, shift % LANES, 1)


def contract(left, right, left_dim, right_dim):
    dims = (((left_dim,), (right_dim,)), ((), ()))
    return lax.dot_general(left, right, dims, preferred_element_type=F32)


def halves(data):
    high = data.astype(BF16)
    return high, (data - high.astype(F32)).astype(BF16)


def left_split(data, axis=1):
    high, low = halves(data)
    return jnp.concatenate([high, low, high], axis=axis)


def right_split(data, axis=1):
    high, low = halves(data)
    return jnp.concatenate([high, high, low], axis=axis)


def by_chunk(ref):
    chunks = ref.shape[1] // LANES
    return jnp.concatenate([ref[:, j * LANES : (j + 1) * LANES].astype(F32) for j in range(chunks)], axis=0)


def column(row):
    size = row.shape[1]
    square = jnp.broadcast_to(row, (size, size))
    return jnp.sum(jnp.where(iota((size, size), 0) == iota((size, size), 1), square, 0.0), axis=1, keepdims=True)


def tiled_row(col):
    size = col.shape[0]
    spread = jnp.where(iota((size, LANES), 1) % size == iota((size, LANES), 0), col, 0.0)
    return jnp.sum(spread, axis=0, keepdims=True)


def decays(inv_col):
    modes = inv_col.shape[0]
    offset = iota((modes, LANES), 1).astype(F32)
    age_in = (LANES - offset) * inv_col
    age_out = offset * inv_col
    return jnp.exp(-age_in), age_in, jnp.exp(-age_out), age_out


def tile_modes(data):
    return jnp.concatenate([data] * (LANES // data.shape[0]), axis=0)


def ranks(size, tuned):
    return tuned if len(tuned) == size else tuple(range(size))


def seq_ranks(seq_size):
    return ranks(seq_size, (7, 0, 1, 4, 6, 3, 2, 5))


def chip_ranks(chips):
    return ranks(chips, (1, 0))


def is_early():
    return (lax.axis_index("seq") == 0) & (lax.axis_index("ch") < CORES)


def strided(ref, start, count, stride):
    return ref[pl.ds(start, count, stride=stride), :]


def prepare(seq_size, memory_ref, residue_ref, skip_ref, x_ref, q_ref, k_ref, d_ref, table_ref, base_ref, read_ref):
    modes = memory_ref.shape[1]
    channels, local_len = x_ref.shape
    chunks = local_len // LANES
    rows = chunks * channels
    me_seq = lax.axis_index("seq")
    inv = 1.0 / memory_ref[...]
    inv_col = column(inv)
    inv_row = tiled_row(inv_col)
    decay_in, _, decay_out, _ = decays(inv_col)
    amplitude = column(residue_ref[...] * jnp.sqrt(2.0 * inv))
    values = by_chunk(x_ref) * by_chunk(k_ref)
    grads = by_chunk(d_ref) * by_chunk(q_ref)
    value_split = left_split(values)
    grad_split = left_split(grads)

    device = iota((seq_size, LANES), 0)
    if seq_ranks(seq_size) != tuple(range(seq_size)):
        place = device
        for p, index in enumerate(seq_ranks(seq_size)):
            device = jnp.where(place == p, index, device)
    ahead = (me_seq - 1 - device).astype(F32) * local_len
    behind = (device - me_seq - 1).astype(F32) * local_len
    table_ref[:seq_size] = jnp.where(ahead >= 0, jnp.exp(-jnp.maximum(ahead, 0.0) * inv_row), 0.0)
    table_ref[seq_size : 2 * seq_size] = jnp.where(behind >= 0, jnp.exp(-jnp.maximum(behind, 0.0) * inv_row), 0.0)
    power = iota((chunks, LANES), 0).astype(F32) * LANES
    table_ref[2 * seq_size : 2 * seq_size + chunks] = jnp.exp(-power * inv_row)

    read_in, read_out = tile_modes(amplitude * decay_in), tile_modes(amplitude * decay_out)
    read_ref[:LANES] = jnp.concatenate(halves(read_out), axis=1)
    read_ref[LANES:] = jnp.concatenate(halves(read_in), axis=1)

    value_states = contract(value_split, right_split(tile_modes(decay_in)), 1, 1)
    grad_states = contract(grad_split, right_split(tile_modes(decay_out)), 1, 1)
    step = jnp.exp(-LANES * inv_row)
    starts, ends = [jnp.zeros((channels, LANES), F32)], [jnp.zeros((channels, LANES), F32)]
    for j in range(chunks - 1):
        starts.append(step * starts[-1] + value_states[j * channels : (j + 1) * channels])
        i = chunks - 1 - j
        ends.append(step * ends[-1] + grad_states[i * channels : (i + 1) * channels])
    first = iota((rows, LANES), 1) < modes

    def state_split(parts):
        return left_split(jnp.where(first, jnp.concatenate(parts, axis=0), 0.0))

    taps = jnp.sum(amplitude * decay_out, axis=0, keepdims=True)
    square = (LANES, LANES)
    toeplitz = pltpu.roll(jnp.broadcast_to(taps, square), 0, 1, stride=1, stride_axis=0)
    toeplitz = jnp.where(iota(square, 1) >= iota(square, 0), toeplitz, 0.0)
    conv = contract(value_split, right_split(toeplitz, axis=0), 1, 0)
    conv = conv + contract(state_split(starts), right_split(read_out, axis=0), 1, 0)
    corr = contract(grad_split, right_split(toeplitz), 1, 1)
    corr = corr + contract(state_split(ends[::-1]), right_split(read_in, axis=0), 1, 0)
    gain = jnp.concatenate([column(skip_ref[...])] * chunks, axis=0)
    base_ref[:rows] = conv + gain * values
    base_ref[rows:] = corr + gain * grads


def make_states(seq_size, *refs):
    sources, (out_ref, rates_ref, *copies), tables, arrived = refs[:7], refs[7:16], refs[16:19], refs[19]
    moves = [pltpu.make_async_copy(*ends, arrived.at[i]) for i, ends in enumerate(zip(sources, copies))]
    for i in (0, 3, 5, 6, 4, 1, 2):
        moves[i].start()
    memory_ref, _, _, x_ref, q_ref, k_ref, d_ref = copies
    modes = memory_ref.shape[1]
    channels, local_len = x_ref.shape
    chunks = local_len // LANES
    moves[0].wait()
    inv_col = column(1.0 / memory_ref[...])
    inv_row = tiled_row(inv_col)
    decay_in, age_in, decay_out, age_out = decays(inv_col)
    pair_in = jnp.concatenate([tile_modes(decay_in), tile_modes(decay_in * age_in)], axis=0)
    pair_out = jnp.concatenate([tile_modes(decay_out), tile_modes(decay_out * age_out)], axis=0)
    split_in, split_out = right_split(pair_in), right_split(pair_out)
    step = jnp.exp(-LANES * inv_row)
    growth = LANES * inv_row
    leap = jnp.exp(-local_len * inv_row)
    rates_ref[0:1] = leap
    rates_ref[1:2] = leap * (local_len * inv_row)
    moves[3].wait()
    moves[5].wait()
    values = by_chunk(x_ref) * by_chunk(k_ref)
    moves[6].wait()
    moves[4].wait()
    grads = by_chunk(d_ref) * by_chunk(q_ref)
    outer = contract(left_split(values, axis=0), right_split(grads, axis=0), 0, 0)
    outer = jnp.where(iota(outer.shape, 1) >= iota(outer.shape, 0), outer, 0.0)
    turn = (iota(outer.shape, 1) + iota(outer.shape, 0)) % LANES
    skewed = jnp.take_along_axis(outer, turn, axis=1, mode="promise_in_bounds")
    near = decay_out * jnp.sum(skewed, axis=0, keepdims=True)
    near_zero = jnp.sum(near, axis=1, keepdims=True)
    near_one = jnp.sum(near * age_out, axis=1, keepdims=True)
    value_states = contract(left_split(values), split_in, 1, 1)
    grad_states = contract(left_split(grads), split_out, 1, 1)
    products = values * grads
    part_skip = products[:channels]
    for j in range(1, chunks):
        part_skip = part_skip + products[j * channels : (j + 1) * channels]
    part_skip = jnp.sum(part_skip, axis=1, keepdims=True)
    lane = iota((channels, LANES), 1)
    row_id = iota((channels, LANES), 0)
    prefix_zero = jnp.zeros((channels, LANES), F32)
    prefix_one = cross_zero = cross_one = suffix_zero = suffix_one = prefix_zero
    power = jnp.ones_like(step)
    for j in range(chunks):
        rows = slice(j * channels, (j + 1) * channels)
        grad_zero, grad_one = grad_states[rows, :LANES], grad_states[rows, LANES:]
        if j > 0:
            cross_zero = cross_zero + prefix_zero * grad_zero
            cross_one = cross_one + prefix_one * grad_zero + prefix_zero * grad_one
        prefix_one = step * (prefix_one + growth * prefix_zero) + value_states[rows, LANES:]
        prefix_zero = step * prefix_zero + value_states[rows, :LANES]
        suffix_zero = suffix_zero + power * grad_zero
        suffix_one = suffix_one + power * (grad_one + j * growth * grad_zero)
        power = power * step
    half = channels // 2
    own = lane // modes == row_id % half
    payload = []
    for state in (prefix_zero, prefix_one, suffix_zero, suffix_one):
        state = jnp.where(own, state, 0.0)
        payload.append(jnp.sum(state[:half], axis=0, keepdims=True))
        payload.append(jnp.sum(state[half:], axis=0, keepdims=True))
    extras = (
        jnp.where(lane < modes, cross_zero, 0.0)
        + jnp.where((lane >= modes) & (lane < 2 * modes), cross_one, 0.0)
        + jnp.where(lane == row_id, near_zero, 0.0)
        + jnp.where(lane == row_id + modes, near_one, 0.0)
        + jnp.where(lane == row_id + 2 * modes, part_skip, 0.0)
    )
    payload.append(jnp.sum(extras, axis=0, keepdims=True))
    sublane = iota((8, LANES), 0)
    for k in range(len(payload)):
        tile = jnp.zeros((8, LANES), F32)
        for i in range(8):
            tile = jnp.where(sublane == i, payload[(8 * k + i) % len(payload)], tile)
        for start in range(8 * k, out_ref.shape[0], 8 * len(payload)):
            out_ref[start : start + 8] = tile

    for move in moves[1:3]:
        move.wait()

    @pl.when(is_early())
    def _():
        prepare(seq_size, *copies, *tables)


def pair_sums(seq_size, chips, rates_ref, all_ref, sums_ref):
    modes = LANES // 8
    leap, leap_growth = rates_ref[0:1], rates_ref[1:2]

    def pairs(e, carry):
        done = []
        for part, (prefix_zero, prefix_one, cross_zero, cross_one) in enumerate(carry):
            value_zero, value_one, grad_zero, grad_one = [
                strided(all_ref, e * BLOCK + 2 * kind + part, chips, seq_size * BLOCK) for kind in range(4)
            ]
            done.append(
                (
                    leap * prefix_zero + value_zero,
                    leap * prefix_one + (leap_growth * prefix_zero + value_one),
                    cross_zero + prefix_zero * grad_zero,
                    cross_one + prefix_one * grad_zero + prefix_zero * grad_one,
                )
            )
        return tuple(done)

    zeros = jnp.zeros((chips, LANES), F32)
    carry = ((zeros,) * 4,) * 2
    if seq_size <= 8 or seq_ranks(seq_size) != tuple(range(seq_size)):
        for e in range(seq_size):
            carry = pairs(seq_ranks(seq_size).index(e), carry)
    else:
        carry = lax.fori_loop(0, seq_size, pairs, carry)
    sums = [jnp.sum(carry[0][i] + carry[1][i], axis=0, keepdims=True) for i in (2, 3)]
    extras = jnp.sum(strided(all_ref, BLOCK - 1, chips * seq_size, BLOCK), axis=0, keepdims=True)
    sums = jnp.where(iota((8, LANES), 0) == 0, sums[0], sums[1])
    shift = LANES // 2
    while shift >= modes:
        sums = sums + roll(sums, shift)
        shift //= 2
    lane = iota((1, LANES), 1)
    sums_ref[...] = extras + jnp.where(lane < modes, sums[0:1], jnp.where(lane < 2 * modes, sums[1:2], 0.0))


def filter_grads(total, memory_ref, residue_ref, mine_ref, other_ref, *refs):
    results, scratch, sent = refs[:2], refs[2:4], refs[4]
    modes = memory_ref.shape[1]
    scale = jnp.sqrt(2.0 / memory_ref[...]) / math.sqrt(total)
    sums = mine_ref[...] + other_ref[...]
    sum_zero, sum_one = sums[:, :modes], roll(sums, -modes)[:, :modes]
    scratch[0][...] = scale * sum_zero
    scratch[1][...] = residue_ref[...] * scale * (sum_one - 0.5 * sum_zero)
    moves = [pltpu.make_async_copy(*ends, sent.at[i]) for i, ends in enumerate(zip(scratch, results))]
    for move in moves:
        move.start()
    for move in moves:
        move.wait()


def finish(seq_size, ch_size, *refs):
    arguments, all_ref, early, refs = refs[:7], refs[7], refs[8:11], refs[11:]
    results, scratch, late, sent = refs[:5], refs[5:10], refs[10:13], refs[13]
    _, _, _, x_ref, q_ref, k_ref, d_ref = arguments
    moves = [pltpu.make_async_copy(*ends, sent.at[i]) for i, ends in enumerate(zip(scratch, results))]
    channels, local_len = x_ref.shape
    modes = LANES // 8
    chunks = local_len // LANES
    half = channels // 2
    rows = chunks * channels

    def complete(table_ref, base_ref, read_ref):
        me = 0
        for p, index in enumerate(chip_ranks(ch_size // CORES)):
            me = me + jnp.where(lax.axis_index("ch") // CORES == index, p * seq_size * BLOCK, 0)
        own = iota((half, LANES), 1) // modes == iota((half, LANES), 0)

        def border(kind, weights):
            parts = []
            for part in range(2):
                state = strided(all_ref, me + 2 * kind + part, seq_size, BLOCK)
                state = jnp.sum(weights * state, axis=0, keepdims=True)
                parts.append(jnp.where(own, state, 0.0))
            return jnp.concatenate(parts, axis=0)

        before = border(0, table_ref[:seq_size])
        after = border(2, table_ref[seq_size : 2 * seq_size])
        powers = [table_ref[2 * seq_size + j : 2 * seq_size + j + 1] for j in range(chunks)]

        def readout(state, factors, matrix):
            high, low = halves(jnp.concatenate([factor * state for factor in factors], axis=0))
            product = contract(jnp.concatenate([high, low], axis=0), matrix, 1, 0)
            return product[:rows, :LANES] + product[:rows, LANES:] + product[rows:, :LANES]

        mixed = base_ref[:rows] + readout(before, powers, read_ref[:LANES])
        grad_values = base_ref[rows:] + readout(after, powers[::-1], read_ref[LANES:])

        skip = jnp.sum(strided(all_ref, me + BLOCK - 1, seq_size, BLOCK), axis=0, keepdims=True)
        skip = roll(skip, -2 * modes)[:, :channels] / math.sqrt(seq_size * local_len)
        for i, (gate_ref, data) in enumerate(
            ((q_ref, mixed), (k_ref, grad_values), (d_ref, mixed), (x_ref, grad_values))
        ):
            for j in range(chunks):
                lanes = slice(j * LANES, (j + 1) * LANES)
                part = gate_ref[:, lanes].astype(F32) * data[j * channels : (j + 1) * channels]
                scratch[i][:, lanes] = part.astype(BF16)
        scratch[4][...] = skip
        for move in moves:
            move.start()

    @pl.when(is_early())
    def _():
        complete(*early)

    @pl.when(jnp.logical_not(is_early()))
    def _():
        prepare(seq_size, *arguments, *late)
        complete(*late)

    for move in moves:
        move.wait()


def per_device(signal_x, gate_q, gate_k, skip_gain, residue, memory, cotangent):
    channels, local_len = signal_x.shape
    modes = memory.shape[0]
    seq_size, ch_size = lax.axis_size("seq"), lax.axis_size("ch")
    devices = seq_size * ch_size
    params = pltpu.CompilerParams(vmem_limit_bytes=32 * 1024 * 1024)
    in_hbm = pl.BlockSpec(memory_space=pltpu.HBM)
    arguments = (memory[None], residue[None], skip_gain[None], signal_x, gate_q, gate_k, cotangent)
    arguments = [pltpu.with_memory_space_constraint(data, pltpu.HBM) for data in arguments]
    copies = [(data.shape, data.dtype) for data in arguments]
    rows = local_len // LANES * channels
    chips = ch_size // CORES
    peers = chips * seq_size
    tables = [((2 * seq_size + 8, LANES), F32), ((2 * rows, LANES), F32), ((2 * LANES, 2 * LANES), BF16)]
    mine, rates, *rest = pl.pallas_call(
        functools.partial(make_states, seq_size),
        in_specs=[in_hbm] * 7,
        out_shape=[
            jax.ShapeDtypeStruct(*shape)
            for shape in [((peers * BLOCK, LANES), F32), ((8, LANES), F32), *copies, *tables]
        ],
        scratch_shapes=[pltpu.SemaphoreType.DMA((7,))],
        compiler_params=params,
    )(*arguments)
    copied, tables_here = rest[:7], rest[7:]
    groups = [
        [s * ch_size + chip * CORES + core for chip in chip_ranks(chips) for s in seq_ranks(seq_size)]
        for core in range(CORES)
    ]
    everyone = lax.all_to_all(mine.reshape(peers, BLOCK, 1, LANES), AXES, 0, 0, axis_index_groups=groups)
    everyone = everyone.reshape(peers * BLOCK, LANES)
    sums = pl.pallas_call(
        functools.partial(pair_sums, seq_size, chips),
        out_shape=jax.ShapeDtypeStruct((1, LANES), F32),
        compiler_params=params,
    )(rates, everyone)
    other = lax.ppermute(sums, "ch", [(i, i ^ 1) for i in range(ch_size)])
    big = ((channels, local_len), BF16)
    shapes = [big] * 4 + [((1, channels), F32)]
    results = pl.pallas_call(
        functools.partial(finish, seq_size, ch_size),
        out_shape=[jax.ShapeDtypeStruct(*shape) for shape in shapes],
        out_specs=[in_hbm] * 5,
        scratch_shapes=[*[pltpu.VMEM(*shape) for shape in shapes + tables], pltpu.SemaphoreType.DMA((5,))],
        compiler_params=params,
        cost_estimate=pl.CostEstimate(flops=20_000_000, bytes_accessed=1_000_000, transcendentals=10_000),
    )(*copied, everyone, *tables_here)
    small = [((1, modes), F32)] * 2
    filters = pl.pallas_call(
        functools.partial(filter_grads, ch_size * channels * seq_size * local_len),
        out_shape=[jax.ShapeDtypeStruct(*shape) for shape in small],
        out_specs=[in_hbm] * 2,
        scratch_shapes=[*[pltpu.VMEM(*shape) for shape in small], pltpu.SemaphoreType.DMA((2,))],
        compiler_params=params,
    )(copied[0], copied[1], sums, other)
    return (*results[:4], results[4][0], filters[0][0], filters[1][0])


def solution(mesh):
    grid = P("ch", "seq")
    return jax.shard_map(
        per_device,
        mesh=mesh,
        in_specs=(grid, grid, grid, P("ch"), P(), P(), grid),
        out_specs=(grid, grid, grid, grid, P("ch"), P(), P()),
        check_vma=False,
    )
```

```python
import functools
import math

import jax
import jax.numpy as jnp
from jax import lax
from jax.experimental import pallas as pl
from jax.experimental.pallas import tpu as pltpu
from jax.sharding import PartitionSpec as P

F32 = jnp.float32
BF16 = jnp.bfloat16
LANES = 128
AXES = ("seq", "ch")
CORES = 2
BLOCK = 9


def iota(shape, dim):
    return lax.broadcasted_iota(jnp.int32, shape, dim)


def roll(data, shift):
    return pltpu.roll(data, shift % LANES, 1)


def contract(left, right, left_dim, right_dim):
    dims = (((left_dim,), (right_dim,)), ((), ()))
    return lax.dot_general(left, right, dims, preferred_element_type=F32)


def halves(data):
    high = data.astype(BF16)
    return high, (data - high.astype(F32)).astype(BF16)


def left_split(data, axis=1):
    high, low = halves(data)
    return jnp.concatenate([high, low, high], axis=axis)


def right_split(data, axis=1):
    high, low = halves(data)
    return jnp.concatenate([high, high, low], axis=axis)


def by_chunk(ref):
    chunks = ref.shape[1] // LANES
    return jnp.concatenate([ref[:, j * LANES : (j + 1) * LANES].astype(F32) for j in range(chunks)], axis=0)


def column(row):
    size = row.shape[1]
    square = jnp.broadcast_to(row, (size, size))
    return jnp.sum(jnp.where(iota((size, size), 0) == iota((size, size), 1), square, 0.0), axis=1, keepdims=True)


def tiled_row(col):
    size = col.shape[0]
    spread = jnp.where(iota((size, LANES), 1) % size == iota((size, LANES), 0), col, 0.0)
    return jnp.sum(spread, axis=0, keepdims=True)


def decays(inv_col):
    modes = inv_col.shape[0]
    offset = iota((modes, LANES), 1).astype(F32)
    age_in = (LANES - offset) * inv_col
    age_out = offset * inv_col
    return jnp.exp(-age_in), age_in, jnp.exp(-age_out), age_out


def tile_modes(data):
    return jnp.concatenate([data] * (LANES // data.shape[0]), axis=0)


def ranks(size, tuned):
    return tuned if len(tuned) == size else tuple(range(size))


def seq_ranks(seq_size):
    return ranks(seq_size, (7, 0, 1, 4, 6, 3, 2, 5))


def chip_ranks(chips):
    return ranks(chips, (1, 0))


def is_early():
    return (lax.axis_index("seq") == 0) & (lax.axis_index("ch") < CORES)


def strided(ref, start, count, stride):
    return ref[pl.ds(start, count, stride=stride), :]


def prepare(seq_size, memory_ref, residue_ref, skip_ref, x_ref, q_ref, k_ref, d_ref, table_ref, base_ref, read_ref):
    modes = memory_ref.shape[1]
    channels, local_len = x_ref.shape
    chunks = local_len // LANES
    rows = chunks * channels
    me_seq = lax.axis_index("seq")
    inv = 1.0 / memory_ref[...]
    inv_col = column(inv)
    inv_row = tiled_row(inv_col)
    decay_in, _, decay_out, _ = decays(inv_col)
    amplitude = column(residue_ref[...] * jnp.sqrt(2.0 * inv))
    values = by_chunk(x_ref) * by_chunk(k_ref)
    grads = by_chunk(d_ref) * by_chunk(q_ref)
    value_split = left_split(values)
    grad_split = left_split(grads)

    device = iota((seq_size, LANES), 0)
    if seq_ranks(seq_size) != tuple(range(seq_size)):
        place = device
        for p, index in enumerate(seq_ranks(seq_size)):
            device = jnp.where(place == p, index, device)
    ahead = (me_seq - 1 - device).astype(F32) * local_len
    behind = (device - me_seq - 1).astype(F32) * local_len
    table_ref[:seq_size] = jnp.where(ahead >= 0, jnp.exp(-jnp.maximum(ahead, 0.0) * inv_row), 0.0)
    table_ref[seq_size : 2 * seq_size] = jnp.where(behind >= 0, jnp.exp(-jnp.maximum(behind, 0.0) * inv_row), 0.0)
    power = iota((chunks, LANES), 0).astype(F32) * LANES
    table_ref[2 * seq_size : 2 * seq_size + chunks] = jnp.exp(-power * inv_row)

    read_in, read_out = tile_modes(amplitude * decay_in), tile_modes(amplitude * decay_out)
    read_ref[:LANES] = jnp.concatenate(halves(read_out), axis=1)
    read_ref[LANES:] = jnp.concatenate(halves(read_in), axis=1)

    value_states = contract(value_split, right_split(tile_modes(decay_in)), 1, 1)
    grad_states = contract(grad_split, right_split(tile_modes(decay_out)), 1, 1)
    step = jnp.exp(-LANES * inv_row)
    starts, ends = [jnp.zeros((channels, LANES), F32)], [jnp.zeros((channels, LANES), F32)]
    for j in range(chunks - 1):
        starts.append(step * starts[-1] + value_states[j * channels : (j + 1) * channels])
        i = chunks - 1 - j
        ends.append(step * ends[-1] + grad_states[i * channels : (i + 1) * channels])
    first = iota((rows, LANES), 1) < modes

    def state_split(parts):
        return left_split(jnp.where(first, jnp.concatenate(parts, axis=0), 0.0))

    taps = jnp.sum(amplitude * decay_out, axis=0, keepdims=True)
    square = (LANES, LANES)
    toeplitz = pltpu.roll(jnp.broadcast_to(taps, square), 0, 1, stride=1, stride_axis=0)
    toeplitz = jnp.where(iota(square, 1) >= iota(square, 0), toeplitz, 0.0)
    conv = contract(value_split, right_split(toeplitz, axis=0), 1, 0)
    conv = conv + contract(state_split(starts), right_split(read_out, axis=0), 1, 0)
    corr = contract(grad_split, right_split(toeplitz), 1, 1)
    corr = corr + contract(state_split(ends[::-1]), right_split(read_in, axis=0), 1, 0)
    gain = jnp.concatenate([column(skip_ref[...])] * chunks, axis=0)
    base_ref[:rows] = conv + gain * values
    base_ref[rows:] = corr + gain * grads


def make_states(seq_size, *refs):
    sources, (out_ref, rates_ref, *copies), tables, arrived = refs[:7], refs[7:16], refs[16:19], refs[19]
    moves = [pltpu.make_async_copy(*ends, arrived.at[i]) for i, ends in enumerate(zip(sources, copies))]
    for i in (0, 3, 5, 6, 4, 1, 2):
        moves[i].start()
    memory_ref, _, _, x_ref, q_ref, k_ref, d_ref = copies
    modes = memory_ref.shape[1]
    channels, local_len = x_ref.shape
    chunks = local_len // LANES
    moves[0].wait()
    inv_col = column(1.0 / memory_ref[...])
    inv_row = tiled_row(inv_col)
    decay_in, age_in, decay_out, age_out = decays(inv_col)
    pair_in = jnp.concatenate([tile_modes(decay_in), tile_modes(decay_in * age_in)], axis=0)
    pair_out = jnp.concatenate([tile_modes(decay_out), tile_modes(decay_out * age_out)], axis=0)
    split_in, split_out = right_split(pair_in), right_split(pair_out)
    step = jnp.exp(-LANES * inv_row)
    growth = LANES * inv_row
    leap = jnp.exp(-local_len * inv_row)
    rates_ref[0:1] = leap
    rates_ref[1:2] = leap * (local_len * inv_row)
    moves[3].wait()
    moves[5].wait()
    values = by_chunk(x_ref) * by_chunk(k_ref)
    moves[6].wait()
    moves[4].wait()
    grads = by_chunk(d_ref) * by_chunk(q_ref)
    outer = contract(left_split(values, axis=0), right_split(grads, axis=0), 0, 0)
    outer = jnp.where(iota(outer.shape, 1) >= iota(outer.shape, 0), outer, 0.0)
    turn = (iota(outer.shape, 1) + iota(outer.shape, 0)) % LANES
    skewed = jnp.take_along_axis(outer, turn, axis=1, mode="promise_in_bounds")
    near = decay_out * jnp.sum(skewed, axis=0, keepdims=True)
    near_zero = jnp.sum(near, axis=1, keepdims=True)
    near_one = jnp.sum(near * age_out, axis=1, keepdims=True)
    value_states = contract(left_split(values), split_in, 1, 1)
    grad_states = contract(left_split(grads), split_out, 1, 1)
    products = values * grads
    part_skip = products[:channels]
    for j in range(1, chunks):
        part_skip = part_skip + products[j * channels : (j + 1) * channels]
    part_skip = jnp.sum(part_skip, axis=1, keepdims=True)
    lane = iota((channels, LANES), 1)
    row_id = iota((channels, LANES), 0)
    prefix_zero = jnp.zeros((channels, LANES), F32)
    prefix_one = cross_zero = cross_one = suffix_zero = suffix_one = prefix_zero
    power = jnp.ones_like(step)
    for j in range(chunks):
        rows = slice(j * channels, (j + 1) * channels)
        grad_zero, grad_one = grad_states[rows, :LANES], grad_states[rows, LANES:]
        if j > 0:
            cross_zero = cross_zero + prefix_zero * grad_zero
            cross_one = cross_one + prefix_one * grad_zero + prefix_zero * grad_one
        prefix_one = step * (prefix_one + growth * prefix_zero) + value_states[rows, LANES:]
        prefix_zero = step * prefix_zero + value_states[rows, :LANES]
        suffix_zero = suffix_zero + power * grad_zero
        suffix_one = suffix_one + power * (grad_one + j * growth * grad_zero)
        power = power * step
    half = channels // 2
    own = lane // modes == row_id % half
    payload = []
    for state in (prefix_zero, prefix_one, suffix_zero, suffix_one):
        state = jnp.where(own, state, 0.0)
        payload.append(jnp.sum(state[:half], axis=0, keepdims=True))
        payload.append(jnp.sum(state[half:], axis=0, keepdims=True))
    extras = (
        jnp.where(lane < modes, cross_zero, 0.0)
        + jnp.where((lane >= modes) & (lane < 2 * modes), cross_one, 0.0)
        + jnp.where(lane == row_id, near_zero, 0.0)
        + jnp.where(lane == row_id + modes, near_one, 0.0)
        + jnp.where(lane == row_id + 2 * modes, part_skip, 0.0)
    )
    payload.append(jnp.sum(extras, axis=0, keepdims=True))
    sublane = iota((8, LANES), 0)
    for k in range(len(payload)):
        tile = jnp.zeros((8, LANES), F32)
        for i in range(8):
            tile = jnp.where(sublane == i, payload[(8 * k + i) % len(payload)], tile)
        for start in range(8 * k, out_ref.shape[0], 8 * len(payload)):
            out_ref[start : start + 8] = tile

    for move in moves[1:3]:
        move.wait()

    @pl.when(is_early())
    def _():
        prepare(seq_size, *copies, *tables)


def pair_sums(seq_size, chips, rates_ref, all_ref, sums_ref):
    modes = LANES // 8
    leap, leap_growth = rates_ref[0:1], rates_ref[1:2]

    def pairs(e, carry):
        done = []
        for part, (prefix_zero, prefix_one, cross_zero, cross_one) in enumerate(carry):
            value_zero, value_one, grad_zero, grad_one = [
                strided(all_ref, e * BLOCK + 2 * kind + part, chips, seq_size * BLOCK) for kind in range(4)
            ]
            done.append(
                (
                    leap * prefix_zero + value_zero,
                    leap * prefix_one + (leap_growth * prefix_zero + value_one),
                    cross_zero + prefix_zero * grad_zero,
                    cross_one + prefix_one * grad_zero + prefix_zero * grad_one,
                )
            )
        return tuple(done)

    zeros = jnp.zeros((chips, LANES), F32)
    carry = ((zeros,) * 4,) * 2
    if seq_size <= 8 or seq_ranks(seq_size) != tuple(range(seq_size)):
        for e in range(seq_size):
            carry = pairs(seq_ranks(seq_size).index(e), carry)
    else:
        carry = lax.fori_loop(0, seq_size, pairs, carry)
    sums = [jnp.sum(carry[0][i] + carry[1][i], axis=0, keepdims=True) for i in (2, 3)]
    extras = jnp.sum(strided(all_ref, BLOCK - 1, chips * seq_size, BLOCK), axis=0, keepdims=True)
    kind = iota((8, LANES), 0)
    sums = jnp.where(kind == 0, sums[0], sums[1]) + jnp.where(iota((8, LANES), 1) // modes == kind, extras, 0.0)
    sums_ref[...] = sum([roll(sums, shift) for shift in range(modes, LANES, modes)], sums)


def filter_grads(total, memory_ref, residue_ref, mine_ref, other_ref, *refs):
    results, scratch, sent = refs[:2], refs[2:4], refs[4]
    modes = memory_ref.shape[1]
    scale = jnp.sqrt(2.0 / memory_ref[...]) / math.sqrt(total)
    sums = mine_ref[...] + other_ref[...]
    sum_zero, sum_one = sums[0:1, :modes], sums[1:2, :modes]
    scratch[0][...] = scale * sum_zero
    scratch[1][...] = residue_ref[...] * scale * (sum_one - 0.5 * sum_zero)
    moves = [pltpu.make_async_copy(*ends, sent.at[i]) for i, ends in enumerate(zip(scratch, results))]
    for move in moves:
        move.start()
    for move in moves:
        move.wait()


def finish(seq_size, ch_size, *refs):
    arguments, all_ref, early, refs = refs[:7], refs[7], refs[8:11], refs[11:]
    results, scratch, late, sent = refs[:5], refs[5:10], refs[10:13], refs[13]
    _, _, _, x_ref, q_ref, k_ref, d_ref = arguments
    moves = [pltpu.make_async_copy(*ends, sent.at[i]) for i, ends in enumerate(zip(scratch, results))]
    channels, local_len = x_ref.shape
    modes = LANES // 8
    chunks = local_len // LANES
    half = channels // 2
    rows = chunks * channels

    def complete(table_ref, base_ref, read_ref):
        me = 0
        for p, index in enumerate(chip_ranks(ch_size // CORES)):
            me = me + jnp.where(lax.axis_index("ch") // CORES == index, p * seq_size * BLOCK, 0)
        own = iota((half, LANES), 1) // modes == iota((half, LANES), 0)

        def border(kind, weights):
            parts = []
            for part in range(2):
                state = strided(all_ref, me + 2 * kind + part, seq_size, BLOCK)
                state = jnp.sum(weights * state, axis=0, keepdims=True)
                parts.append(jnp.where(own, state, 0.0))
            return jnp.concatenate(parts, axis=0)

        before = border(0, table_ref[:seq_size])
        after = border(2, table_ref[seq_size : 2 * seq_size])
        powers = [table_ref[2 * seq_size + j : 2 * seq_size + j + 1] for j in range(chunks)]

        def readout(state, factors, matrix):
            high, low = halves(jnp.concatenate([factor * state for factor in factors], axis=0))
            product = contract(jnp.concatenate([high, low], axis=0), matrix, 1, 0)
            return product[:rows, :LANES] + product[:rows, LANES:] + product[rows:, :LANES]

        mixed = base_ref[:rows] + readout(before, powers, read_ref[:LANES])
        grad_values = base_ref[rows:] + readout(after, powers[::-1], read_ref[LANES:])

        skip = jnp.sum(strided(all_ref, me + BLOCK - 1, seq_size, BLOCK), axis=0, keepdims=True)
        skip = roll(skip, -2 * modes)[:, :channels] / math.sqrt(seq_size * local_len)
        for i, (gate_ref, data) in enumerate(
            ((q_ref, mixed), (k_ref, grad_values), (d_ref, mixed), (x_ref, grad_values))
        ):
            for j in range(chunks):
                lanes = slice(j * LANES, (j + 1) * LANES)
                part = gate_ref[:, lanes].astype(F32) * data[j * channels : (j + 1) * channels]
                scratch[i][:, lanes] = part.astype(BF16)
        scratch[4][...] = skip
        for move in moves:
            move.start()

    @pl.when(is_early())
    def _():
        complete(*early)

    @pl.when(jnp.logical_not(is_early()))
    def _():
        prepare(seq_size, *arguments, *late)
        complete(*late)

    for move in moves:
        move.wait()


def per_device(signal_x, gate_q, gate_k, skip_gain, residue, memory, cotangent):
    channels, local_len = signal_x.shape
    modes = memory.shape[0]
    seq_size, ch_size = lax.axis_size("seq"), lax.axis_size("ch")
    devices = seq_size * ch_size
    params = pltpu.CompilerParams(vmem_limit_bytes=32 * 1024 * 1024)
    in_hbm = pl.BlockSpec(memory_space=pltpu.HBM)
    arguments = (memory[None], residue[None], skip_gain[None], signal_x, gate_q, gate_k, cotangent)
    arguments = [pltpu.with_memory_space_constraint(data, pltpu.HBM) for data in arguments]
    copies = [(data.shape, data.dtype) for data in arguments]
    rows = local_len // LANES * channels
    chips = ch_size // CORES
    peers = chips * seq_size
    tables = [((2 * seq_size + 8, LANES), F32), ((2 * rows, LANES), F32), ((2 * LANES, 2 * LANES), BF16)]
    mine, rates, *rest = pl.pallas_call(
        functools.partial(make_states, seq_size),
        in_specs=[in_hbm] * 7,
        out_shape=[
            jax.ShapeDtypeStruct(*shape)
            for shape in [((peers * BLOCK, LANES), F32), ((8, LANES), F32), *copies, *tables]
        ],
        scratch_shapes=[pltpu.SemaphoreType.DMA((7,))],
        compiler_params=params,
    )(*arguments)
    copied, tables_here = rest[:7], rest[7:]
    groups = [
        [s * ch_size + chip * CORES + core for chip in chip_ranks(chips) for s in seq_ranks(seq_size)]
        for core in range(CORES)
    ]
    everyone = lax.all_to_all(mine.reshape(peers, BLOCK, 1, LANES), AXES, 0, 0, axis_index_groups=groups)
    everyone = everyone.reshape(peers * BLOCK, LANES)
    sums = pl.pallas_call(
        functools.partial(pair_sums, seq_size, chips),
        out_shape=jax.ShapeDtypeStruct((8, LANES), F32),
        compiler_params=params,
    )(rates, everyone)
    other = lax.ppermute(sums, "ch", [(i, i ^ 1) for i in range(ch_size)])
    big = ((channels, local_len), BF16)
    shapes = [big] * 4 + [((1, channels), F32)]
    results = pl.pallas_call(
        functools.partial(finish, seq_size, ch_size),
        out_shape=[jax.ShapeDtypeStruct(*shape) for shape in shapes],
        out_specs=[in_hbm] * 5,
        scratch_shapes=[*[pltpu.VMEM(*shape) for shape in shapes + tables], pltpu.SemaphoreType.DMA((5,))],
        compiler_params=params,
        cost_estimate=pl.CostEstimate(flops=20_000_000, bytes_accessed=1_000_000, transcendentals=10_000),
    )(*copied, everyone, *tables_here)
    small = [((1, modes), F32)] * 2
    filters = pl.pallas_call(
        functools.partial(filter_grads, ch_size * channels * seq_size * local_len),
        out_shape=[jax.ShapeDtypeStruct(*shape) for shape in small],
        out_specs=[in_hbm] * 2,
        scratch_shapes=[*[pltpu.VMEM(*shape) for shape in small], pltpu.SemaphoreType.DMA((2,))],
        compiler_params=params,
    )(copied[0], copied[1], sums, other)
    return (*results[:4], results[4][0], filters[0][0], filters[1][0])


def solution(mesh):
    grid = P("ch", "seq")
    return jax.shard_map(
        per_device,
        mesh=mesh,
        in_specs=(grid, grid, grid, P("ch"), P(), P(), grid),
        out_specs=(grid, grid, grid, grid, P("ch"), P(), P()),
        check_vma=False,
    )
```

```python
import functools
import math

import jax
import jax.numpy as jnp
from jax import lax
from jax.experimental import pallas as pl
from jax.experimental.pallas import tpu as pltpu
from jax.sharding import PartitionSpec as P

F32 = jnp.float32
BF16 = jnp.bfloat16
LANES = 128
AXES = ("seq", "ch")
CORES = 2
BLOCK = 9


def iota(shape, dim):
    return lax.broadcasted_iota(jnp.int32, shape, dim)


def roll(data, shift):
    return pltpu.roll(data, shift % LANES, 1)


def contract(left, right, left_dim, right_dim):
    dims = (((left_dim,), (right_dim,)), ((), ()))
    return lax.dot_general(left, right, dims, preferred_element_type=F32)


def halves(data):
    high = data.astype(BF16)
    return high, (data - high.astype(F32)).astype(BF16)


def left_split(data, axis=1):
    high, low = halves(data)
    return jnp.concatenate([high, low, high], axis=axis)


def right_split(data, axis=1):
    high, low = halves(data)
    return jnp.concatenate([high, high, low], axis=axis)


def by_chunk(ref):
    chunks = ref.shape[1] // LANES
    return jnp.concatenate([ref[:, j * LANES : (j + 1) * LANES].astype(F32) for j in range(chunks)], axis=0)


def column(row):
    size = row.shape[1]
    square = jnp.broadcast_to(row, (size, size))
    return jnp.sum(jnp.where(iota((size, size), 0) == iota((size, size), 1), square, 0.0), axis=1, keepdims=True)


def tiled_row(col):
    size = col.shape[0]
    spread = jnp.where(iota((size, LANES), 1) % size == iota((size, LANES), 0), col, 0.0)
    return jnp.sum(spread, axis=0, keepdims=True)


def decays(inv_col):
    modes = inv_col.shape[0]
    offset = iota((modes, LANES), 1).astype(F32)
    age_in = (LANES - offset) * inv_col
    age_out = offset * inv_col
    return jnp.exp(-age_in), age_in, jnp.exp(-age_out), age_out


def tile_modes(data):
    return jnp.concatenate([data] * (LANES // data.shape[0]), axis=0)


def ranks(size, tuned):
    return tuned if len(tuned) == size else tuple(range(size))


def seq_ranks(seq_size):
    return ranks(seq_size, (7, 0, 1, 4, 6, 3, 2, 5))


def chip_ranks(chips):
    return ranks(chips, (1, 0))


def strided(ref, start, count, stride):
    return ref[pl.ds(start, count, stride=stride), :]


def local_parts(seq_size, rates_ref, values, grads, parameters, chunks, channels):
    rows = chunks * channels
    modes = (rates_ref.shape[0] - 8) // 2
    local_len = chunks * LANES
    me_seq = lax.axis_index("seq")
    inv_row = rates_ref[2:3]
    memory_ref, residue_ref, skip_ref = parameters
    amplitude = column(residue_ref[...] * jnp.sqrt(2.0 / memory_ref[...]))
    read_in, read_out = amplitude * rates_ref[8 : 8 + modes], amplitude * rates_ref[8 + modes :]
    value_split = left_split(values)
    grad_split = left_split(grads)

    taps = jnp.sum(read_out, axis=0, keepdims=True)
    square = (LANES, LANES)
    toeplitz = pltpu.roll(jnp.broadcast_to(taps, square), 0, 1, stride=1, stride_axis=0)
    toeplitz = jnp.where(iota(square, 1) >= iota(square, 0), toeplitz, 0.0)

    device = iota((seq_size, LANES), 0)
    if seq_ranks(seq_size) != tuple(range(seq_size)):
        place = device
        for p, index in enumerate(seq_ranks(seq_size)):
            device = jnp.where(place == p, index, device)
    ahead = (me_seq - 1 - device).astype(F32) * local_len
    behind = (device - me_seq - 1).astype(F32) * local_len
    weights = [jnp.where(far >= 0, jnp.exp(-jnp.maximum(far, 0.0) * inv_row), 0.0) for far in (ahead, behind)]
    powers = [jnp.exp(-float(j * LANES) * inv_row) for j in range(chunks)]

    conv = contract(value_split, right_split(toeplitz, axis=0), 1, 0)
    corr = contract(grad_split, right_split(toeplitz), 1, 1)
    gain = jnp.concatenate([column(skip_ref[...])] * chunks, axis=0)
    return weights, powers, conv + gain * values, corr + gain * grads, tile_modes(read_out), tile_modes(read_in)


def make_states(*refs):
    sources, (out_ref, rates_ref, starts_ref, ends_ref, *copies), arrived = refs[:7], refs[7:18], refs[18]
    moves = [pltpu.make_async_copy(*ends, arrived.at[i]) for i, ends in enumerate(zip(sources, copies))]
    for i in (0, 3, 5, 6, 4, 1, 2):
        moves[i].start()
    memory_ref, _, _, x_ref, q_ref, k_ref, d_ref = copies
    modes = memory_ref.shape[1]
    channels, local_len = x_ref.shape
    chunks = local_len // LANES
    moves[0].wait()
    inv_col = column(1.0 / memory_ref[...])
    inv_row = tiled_row(inv_col)
    decay_in, age_in, decay_out, age_out = decays(inv_col)
    pair_in = jnp.concatenate([tile_modes(decay_in), tile_modes(decay_in * age_in)], axis=0)
    pair_out = jnp.concatenate([tile_modes(decay_out), tile_modes(decay_out * age_out)], axis=0)
    split_in, split_out = right_split(pair_in), right_split(pair_out)
    step = jnp.exp(-LANES * inv_row)
    growth = LANES * inv_row
    leap = jnp.exp(-local_len * inv_row)
    rates_ref[0:1] = leap
    rates_ref[1:2] = leap * (local_len * inv_row)
    rates_ref[2:3] = inv_row
    rates_ref[8 : 8 + modes] = decay_in
    rates_ref[8 + modes :] = decay_out
    moves[3].wait()
    moves[5].wait()
    values = by_chunk(x_ref) * by_chunk(k_ref)
    moves[6].wait()
    moves[4].wait()
    grads = by_chunk(d_ref) * by_chunk(q_ref)
    outer = contract(left_split(values, axis=0), right_split(grads, axis=0), 0, 0)
    outer = jnp.where(iota(outer.shape, 1) >= iota(outer.shape, 0), outer, 0.0)
    turn = (iota(outer.shape, 1) + iota(outer.shape, 0)) % LANES
    skewed = jnp.take_along_axis(outer, turn, axis=1, mode="promise_in_bounds")
    near = decay_out * jnp.sum(skewed, axis=0, keepdims=True)
    near_zero = jnp.sum(near, axis=1, keepdims=True)
    near_one = jnp.sum(near * age_out, axis=1, keepdims=True)
    value_states = contract(left_split(values), split_in, 1, 1)
    grad_states = contract(left_split(grads), split_out, 1, 1)
    products = values * grads
    part_skip = products[:channels]
    for j in range(1, chunks):
        part_skip = part_skip + products[j * channels : (j + 1) * channels]
    part_skip = jnp.sum(part_skip, axis=1, keepdims=True)
    lane = iota((channels, LANES), 1)
    row_id = iota((channels, LANES), 0)
    prefix_zero = jnp.zeros((channels, LANES), F32)
    prefix_one = cross_zero = cross_one = suffix_zero = suffix_one = prefix_zero
    for j in range(chunks):
        rows = slice(j * channels, (j + 1) * channels)
        grad_zero, grad_one = grad_states[rows, :LANES], grad_states[rows, LANES:]
        if j > 0:
            cross_zero = cross_zero + prefix_zero * grad_zero
            cross_one = cross_one + prefix_one * grad_zero + prefix_zero * grad_one
        starts_ref[rows] = prefix_zero
        prefix_one = step * (prefix_one + growth * prefix_zero) + value_states[rows, LANES:]
        prefix_zero = step * prefix_zero + value_states[rows, :LANES]
    for j in range(chunks - 1, -1, -1):
        rows = slice(j * channels, (j + 1) * channels)
        ends_ref[rows] = suffix_zero
        suffix_one = step * (suffix_one + growth * suffix_zero) + grad_states[rows, LANES:]
        suffix_zero = step * suffix_zero + grad_states[rows, :LANES]
    half = channels // 2
    own = lane // modes == row_id % half
    payload = []
    for state in (prefix_zero, prefix_one, suffix_zero, suffix_one):
        state = jnp.where(own, state, 0.0)
        payload.append(jnp.sum(state[:half], axis=0, keepdims=True))
        payload.append(jnp.sum(state[half:], axis=0, keepdims=True))
    extras = (
        jnp.where(lane < modes, cross_zero, 0.0)
        + jnp.where((lane >= modes) & (lane < 2 * modes), cross_one, 0.0)
        + jnp.where(lane == row_id, near_zero, 0.0)
        + jnp.where(lane == row_id + modes, near_one, 0.0)
        + jnp.where(lane == row_id + 2 * modes, part_skip, 0.0)
    )
    payload.append(jnp.sum(extras, axis=0, keepdims=True))
    sublane = iota((8, LANES), 0)
    for k in range(len(payload)):
        tile = jnp.zeros((8, LANES), F32)
        for i in range(8):
            tile = jnp.where(sublane == i, payload[(8 * k + i) % len(payload)], tile)
        for start in range(8 * k, out_ref.shape[0], 8 * len(payload)):
            out_ref[start : start + 8] = tile

    for move in moves[1:3]:
        move.wait()


def pair_sums(seq_size, chips, rates_ref, all_ref, sums_ref):
    modes = LANES // 8
    leap, leap_growth = rates_ref[0:1], rates_ref[1:2]

    def pairs(e, carry):
        done = []
        for part, (prefix_zero, prefix_one, cross_zero, cross_one) in enumerate(carry):
            value_zero, value_one, grad_zero, grad_one = [
                strided(all_ref, e * BLOCK + 2 * kind + part, chips, seq_size * BLOCK) for kind in range(4)
            ]
            done.append(
                (
                    leap * prefix_zero + value_zero,
                    leap * prefix_one + (leap_growth * prefix_zero + value_one),
                    cross_zero + prefix_zero * grad_zero,
                    cross_one + prefix_one * grad_zero + prefix_zero * grad_one,
                )
            )
        return tuple(done)

    zeros = jnp.zeros((chips, LANES), F32)
    carry = ((zeros,) * 4,) * 2
    if seq_size <= 8 or seq_ranks(seq_size) != tuple(range(seq_size)):
        for e in range(seq_size):
            carry = pairs(seq_ranks(seq_size).index(e), carry)
    else:
        carry = lax.fori_loop(0, seq_size, pairs, carry)
    sums = [jnp.sum(carry[0][i] + carry[1][i], axis=0, keepdims=True) for i in (2, 3)]
    extras = jnp.sum(strided(all_ref, BLOCK - 1, chips * seq_size, BLOCK), axis=0, keepdims=True)
    kind = iota((8, LANES), 0)
    sums = jnp.where(kind == 0, sums[0], sums[1]) + jnp.where(iota((8, LANES), 1) // modes == kind, extras, 0.0)
    sums_ref[...] = sum([roll(sums, shift) for shift in range(modes, LANES, modes)], sums)


def filter_grads(total, memory_ref, residue_ref, mine_ref, other_ref, *refs):
    results, scratch, sent = refs[:2], refs[2:4], refs[4]
    modes = memory_ref.shape[1]
    scale = jnp.sqrt(2.0 / memory_ref[...]) / math.sqrt(total)
    sums = mine_ref[...] + other_ref[...]
    sum_zero, sum_one = sums[0:1, :modes], sums[1:2, :modes]
    scratch[0][...] = scale * sum_zero
    scratch[1][...] = residue_ref[...] * scale * (sum_one - 0.5 * sum_zero)
    moves = [pltpu.make_async_copy(*ends, sent.at[i]) for i, ends in enumerate(zip(scratch, results))]
    for move in moves:
        move.start()
    for move in moves:
        move.wait()


def finish(seq_size, ch_size, rates_ref, starts_ref, ends_ref, *refs):
    parameters, (x_ref, q_ref, k_ref, d_ref, all_ref), refs = refs[:3], refs[3:8], refs[8:]
    results, scratch, sent = refs[:5], refs[5:10], refs[10]
    moves = [pltpu.make_async_copy(*ends, sent.at[i]) for i, ends in enumerate(zip(scratch, results))]
    channels, local_len = x_ref.shape
    modes = LANES // 8
    chunks = local_len // LANES
    half = channels // 2
    rows = chunks * channels
    signal, gate_in = by_chunk(x_ref), by_chunk(k_ref)
    gate_out, cotangent = by_chunk(q_ref), by_chunk(d_ref)
    weights, powers, base_mixed, base_grad, read_out, read_in = local_parts(
        seq_size, rates_ref, signal * gate_in, cotangent * gate_out, parameters, chunks, channels
    )
    me = 0
    for p, index in enumerate(chip_ranks(ch_size // CORES)):
        me = me + jnp.where(lax.axis_index("ch") // CORES == index, p * seq_size * BLOCK, 0)
    own = iota((half, LANES), 1) // modes == iota((half, LANES), 0)

    def border(kind, weight):
        parts = []
        for part in range(2):
            state = strided(all_ref, me + 2 * kind + part, seq_size, BLOCK)
            state = jnp.sum(weight * state, axis=0, keepdims=True)
            parts.append(jnp.where(own, state, 0.0))
        return jnp.concatenate(parts, axis=0)

    mine = iota((rows, LANES), 1) // modes == iota((rows, LANES), 0) % half

    def readout(state, factors, states, matrix):
        state = jnp.concatenate([factor * state for factor in factors], axis=0) + jnp.where(mine, states, 0.0)
        return contract(left_split(state), right_split(matrix, axis=0), 1, 0)

    mixed = base_mixed + readout(border(0, weights[0]), powers, starts_ref[...], read_out)
    grad_values = base_grad + readout(border(2, weights[1]), powers[::-1], ends_ref[...], read_in)
    skip = jnp.sum(strided(all_ref, me + BLOCK - 1, seq_size, BLOCK), axis=0, keepdims=True)
    skip = roll(skip, -2 * modes)[:, :channels] / math.sqrt(seq_size * local_len)
    for i, data in enumerate((gate_out * mixed, grad_values * gate_in, cotangent * mixed, grad_values * signal)):
        for j in range(chunks):
            scratch[i][:, j * LANES : (j + 1) * LANES] = data[j * channels : (j + 1) * channels].astype(BF16)
    scratch[4][...] = skip
    for move in moves:
        move.start()
    for move in moves:
        move.wait()


def per_device(signal_x, gate_q, gate_k, skip_gain, residue, memory, cotangent):
    channels, local_len = signal_x.shape
    modes = memory.shape[0]
    seq_size, ch_size = lax.axis_size("seq"), lax.axis_size("ch")
    devices = seq_size * ch_size
    params = pltpu.CompilerParams(vmem_limit_bytes=32 * 1024 * 1024)
    in_hbm = pl.BlockSpec(memory_space=pltpu.HBM)
    arguments = (memory[None], residue[None], skip_gain[None], signal_x, gate_q, gate_k, cotangent)
    arguments = [pltpu.with_memory_space_constraint(data, pltpu.HBM) for data in arguments]
    copies = [(data.shape, data.dtype) for data in arguments]
    rows = local_len // LANES * channels
    chips = ch_size // CORES
    peers = chips * seq_size
    made = [((peers * BLOCK, LANES), F32), ((8 + 2 * modes, LANES), F32), ((rows, LANES), F32), ((rows, LANES), F32)]
    mine, rates, starts, ends, *copied = pl.pallas_call(
        make_states,
        in_specs=[in_hbm] * 7,
        out_shape=[jax.ShapeDtypeStruct(*shape) for shape in made + copies],
        scratch_shapes=[pltpu.SemaphoreType.DMA((7,))],
        compiler_params=params,
    )(*arguments)
    groups = [
        [s * ch_size + chip * CORES + core for chip in chip_ranks(chips) for s in seq_ranks(seq_size)]
        for core in range(CORES)
    ]
    everyone = lax.all_to_all(mine.reshape(peers, BLOCK, 1, LANES), AXES, 0, 0, axis_index_groups=groups)
    everyone = everyone.reshape(peers * BLOCK, LANES)
    sums = pl.pallas_call(
        functools.partial(pair_sums, seq_size, chips),
        out_shape=jax.ShapeDtypeStruct((8, LANES), F32),
        compiler_params=params,
    )(rates, everyone)
    other = lax.ppermute(sums, "ch", [(i, i ^ 1) for i in range(ch_size)])
    big = ((channels, local_len), BF16)
    shapes = [big] * 4 + [((1, channels), F32)]
    results = pl.pallas_call(
        functools.partial(finish, seq_size, ch_size),
        out_shape=[jax.ShapeDtypeStruct(*shape) for shape in shapes],
        out_specs=[in_hbm] * 5,
        scratch_shapes=[*[pltpu.VMEM(*shape) for shape in shapes], pltpu.SemaphoreType.DMA((5,))],
        compiler_params=params,
        cost_estimate=pl.CostEstimate(flops=20_000_000, bytes_accessed=1_000_000, transcendentals=10_000),
    )(rates, starts, ends, *copied, everyone)
    small = [((1, modes), F32)] * 2
    filters = pl.pallas_call(
        functools.partial(filter_grads, ch_size * channels * seq_size * local_len),
        out_shape=[jax.ShapeDtypeStruct(*shape) for shape in small],
        out_specs=[in_hbm] * 2,
        scratch_shapes=[*[pltpu.VMEM(*shape) for shape in small], pltpu.SemaphoreType.DMA((2,))],
        compiler_params=params,
    )(copied[0], copied[1], sums, other)
    return (*results[:4], results[4][0], filters[0][0], filters[1][0])


def solution(mesh):
    grid = P("ch", "seq")
    return jax.shard_map(
        per_device,
        mesh=mesh,
        in_specs=(grid, grid, grid, P("ch"), P(), P(), grid),
        out_specs=(grid, grid, grid, grid, P("ch"), P(), P()),
        check_vma=False,
    )
```

```python
import functools
import math

import jax
import jax.numpy as jnp
from jax import lax
from jax.experimental import pallas as pl
from jax.experimental.pallas import tpu as pltpu
from jax.sharding import PartitionSpec as P

F32 = jnp.float32
BF16 = jnp.bfloat16
LANES = 128
AXES = ("seq", "ch")
CORES = 2
BLOCK = 9


def iota(shape, dim):
    return lax.broadcasted_iota(jnp.int32, shape, dim)


def roll(data, shift):
    return pltpu.roll(data, shift % LANES, 1)


def contract(left, right, left_dim, right_dim):
    dims = (((left_dim,), (right_dim,)), ((), ()))
    return lax.dot_general(left, right, dims, preferred_element_type=F32)


def halves(data):
    high = data.astype(BF16)
    return high, (data - high.astype(F32)).astype(BF16)


def left_split(data, axis=1):
    high, low = halves(data)
    return jnp.concatenate([high, low, high], axis=axis)


def right_split(data, axis=1):
    high, low = halves(data)
    return jnp.concatenate([high, high, low], axis=axis)


def by_chunk(ref):
    chunks = ref.shape[1] // LANES
    return jnp.concatenate([ref[:, j * LANES : (j + 1) * LANES].astype(F32) for j in range(chunks)], axis=0)


def column(row):
    size = row.shape[1]
    square = jnp.broadcast_to(row, (size, size))
    return jnp.sum(jnp.where(iota((size, size), 0) == iota((size, size), 1), square, 0.0), axis=1, keepdims=True)


def tiled_row(col):
    size = col.shape[0]
    spread = jnp.where(iota((size, LANES), 1) % size == iota((size, LANES), 0), col, 0.0)
    return jnp.sum(spread, axis=0, keepdims=True)


def decays(inv_col):
    modes = inv_col.shape[0]
    offset = iota((modes, LANES), 1).astype(F32)
    age_in = (LANES - offset) * inv_col
    age_out = offset * inv_col
    return jnp.exp(-age_in), age_in, jnp.exp(-age_out), age_out


def tile_modes(data):
    return jnp.concatenate([data] * (LANES // data.shape[0]), axis=0)


def ranks(size, tuned):
    return tuned if len(tuned) == size else tuple(range(size))


def seq_ranks(seq_size):
    return ranks(seq_size, (5, 0, 4, 6, 1, 7, 2, 3))


def chip_ranks(chips):
    return ranks(chips, (1, 0))


def strided(ref, start, count, stride):
    return ref[pl.ds(start, count, stride=stride), :]


def local_parts(seq_size, rates_ref, values, grads, parameters, chunks, channels):
    rows = chunks * channels
    modes = (rates_ref.shape[0] - 8) // 2
    local_len = chunks * LANES
    me_seq = lax.axis_index("seq")
    inv_row = rates_ref[2:3]
    memory_ref, residue_ref, skip_ref = parameters
    amplitude = column(residue_ref[...] * jnp.sqrt(2.0 / memory_ref[...]))
    read_in, read_out = amplitude * rates_ref[8 : 8 + modes], amplitude * rates_ref[8 + modes :]
    value_split = left_split(values)
    grad_split = left_split(grads)

    taps = jnp.sum(read_out, axis=0, keepdims=True)
    square = (LANES, LANES)
    toeplitz = pltpu.roll(jnp.broadcast_to(taps, square), 0, 1, stride=1, stride_axis=0)
    toeplitz = jnp.where(iota(square, 1) >= iota(square, 0), toeplitz, 0.0)

    device = iota((seq_size, LANES), 0)
    if seq_ranks(seq_size) != tuple(range(seq_size)):
        place = device
        for p, index in enumerate(seq_ranks(seq_size)):
            device = jnp.where(place == p, index, device)
    ahead = (me_seq - 1 - device).astype(F32) * local_len
    behind = (device - me_seq - 1).astype(F32) * local_len
    weights = [jnp.where(far >= 0, jnp.exp(-jnp.maximum(far, 0.0) * inv_row), 0.0) for far in (ahead, behind)]
    powers = [jnp.exp(-float(j * LANES) * inv_row) for j in range(chunks)]

    conv = contract(value_split, right_split(toeplitz, axis=0), 1, 0)
    corr = contract(grad_split, right_split(toeplitz), 1, 1)
    gain = jnp.concatenate([column(skip_ref[...])] * chunks, axis=0)
    return weights, powers, conv + gain * values, corr + gain * grads, tile_modes(read_out), tile_modes(read_in)


def make_states(*refs):
    sources, (out_ref, rates_ref, starts_ref, ends_ref, *copies), arrived = refs[:7], refs[7:18], refs[18]
    moves = [pltpu.make_async_copy(*ends, arrived.at[i]) for i, ends in enumerate(zip(sources, copies))]
    for i in (0, 3, 5, 6, 4, 1, 2):
        moves[i].start()
    memory_ref, _, _, x_ref, q_ref, k_ref, d_ref = copies
    modes = memory_ref.shape[1]
    channels, local_len = x_ref.shape
    chunks = local_len // LANES
    moves[0].wait()
    inv_col = column(1.0 / memory_ref[...])
    inv_row = tiled_row(inv_col)
    decay_in, age_in, decay_out, age_out = decays(inv_col)
    pair_in = jnp.concatenate([tile_modes(decay_in), tile_modes(decay_in * age_in)], axis=0)
    pair_out = jnp.concatenate([tile_modes(decay_out), tile_modes(decay_out * age_out)], axis=0)
    split_in, split_out = right_split(pair_in), right_split(pair_out)
    step = jnp.exp(-LANES * inv_row)
    growth = LANES * inv_row
    leap = jnp.exp(-local_len * inv_row)
    rates_ref[0:1] = leap
    rates_ref[1:2] = leap * (local_len * inv_row)
    rates_ref[2:3] = inv_row
    rates_ref[8 : 8 + modes] = decay_in
    rates_ref[8 + modes :] = decay_out
    moves[3].wait()
    moves[5].wait()
    values = by_chunk(x_ref) * by_chunk(k_ref)
    moves[6].wait()
    moves[4].wait()
    grads = by_chunk(d_ref) * by_chunk(q_ref)
    outer = contract(left_split(values, axis=0), right_split(grads, axis=0), 0, 0)
    outer = jnp.where(iota(outer.shape, 1) >= iota(outer.shape, 0), outer, 0.0)
    turn = (iota(outer.shape, 1) + iota(outer.shape, 0)) % LANES
    skewed = jnp.take_along_axis(outer, turn, axis=1, mode="promise_in_bounds")
    near = decay_out * jnp.sum(skewed, axis=0, keepdims=True)
    near_zero = jnp.sum(near, axis=1, keepdims=True)
    near_one = jnp.sum(near * age_out, axis=1, keepdims=True)
    value_states = contract(left_split(values), split_in, 1, 1)
    grad_states = contract(left_split(grads), split_out, 1, 1)
    products = values * grads
    part_skip = products[:channels]
    for j in range(1, chunks):
        part_skip = part_skip + products[j * channels : (j + 1) * channels]
    part_skip = jnp.sum(part_skip, axis=1, keepdims=True)
    lane = iota((channels, LANES), 1)
    row_id = iota((channels, LANES), 0)
    prefix_zero = jnp.zeros((channels, LANES), F32)
    prefix_one = cross_zero = cross_one = suffix_zero = suffix_one = prefix_zero
    for j in range(chunks):
        rows = slice(j * channels, (j + 1) * channels)
        grad_zero, grad_one = grad_states[rows, :LANES], grad_states[rows, LANES:]
        if j > 0:
            cross_zero = cross_zero + prefix_zero * grad_zero
            cross_one = cross_one + prefix_one * grad_zero + prefix_zero * grad_one
        starts_ref[rows] = prefix_zero
        prefix_one = step * (prefix_one + growth * prefix_zero) + value_states[rows, LANES:]
        prefix_zero = step * prefix_zero + value_states[rows, :LANES]
    for j in range(chunks - 1, -1, -1):
        rows = slice(j * channels, (j + 1) * channels)
        ends_ref[rows] = suffix_zero
        suffix_one = step * (suffix_one + growth * suffix_zero) + grad_states[rows, LANES:]
        suffix_zero = step * suffix_zero + grad_states[rows, :LANES]
    half = channels // 2
    own = lane // modes == row_id % half
    payload = []
    for state in (prefix_zero, prefix_one, suffix_zero, suffix_one):
        state = jnp.where(own, state, 0.0)
        payload.append(jnp.sum(state[:half], axis=0, keepdims=True))
        payload.append(jnp.sum(state[half:], axis=0, keepdims=True))
    extras = (
        jnp.where(lane < modes, cross_zero, 0.0)
        + jnp.where((lane >= modes) & (lane < 2 * modes), cross_one, 0.0)
        + jnp.where(lane == row_id, near_zero, 0.0)
        + jnp.where(lane == row_id + modes, near_one, 0.0)
        + jnp.where(lane == row_id + 2 * modes, part_skip, 0.0)
    )
    payload.append(jnp.sum(extras, axis=0, keepdims=True))
    sublane = iota((8, LANES), 0)
    for k in range(len(payload)):
        tile = jnp.zeros((8, LANES), F32)
        for i in range(8):
            tile = jnp.where(sublane == i, payload[(8 * k + i) % len(payload)], tile)
        for start in range(8 * k, out_ref.shape[0], 8 * len(payload)):
            out_ref[start : start + 8] = tile

    for move in moves[1:3]:
        move.wait()


def pair_sums(seq_size, chips, rates_ref, all_ref, sums_ref):
    modes = LANES // 8
    leap, leap_growth = rates_ref[0:1], rates_ref[1:2]

    def pairs(e, carry):
        done = []
        for part, (prefix_zero, prefix_one, cross_zero, cross_one) in enumerate(carry):
            value_zero, value_one, grad_zero, grad_one = [
                strided(all_ref, e * BLOCK + 2 * kind + part, chips, seq_size * BLOCK) for kind in range(4)
            ]
            done.append(
                (
                    leap * prefix_zero + value_zero,
                    leap * prefix_one + (leap_growth * prefix_zero + value_one),
                    cross_zero + prefix_zero * grad_zero,
                    cross_one + prefix_one * grad_zero + prefix_zero * grad_one,
                )
            )
        return tuple(done)

    zeros = jnp.zeros((chips, LANES), F32)
    carry = ((zeros,) * 4,) * 2
    if seq_size <= 8 or seq_ranks(seq_size) != tuple(range(seq_size)):
        for e in range(seq_size):
            carry = pairs(seq_ranks(seq_size).index(e), carry)
    else:
        carry = lax.fori_loop(0, seq_size, pairs, carry)
    sums = [jnp.sum(carry[0][i] + carry[1][i], axis=0, keepdims=True) for i in (2, 3)]
    extras = jnp.sum(strided(all_ref, BLOCK - 1, chips * seq_size, BLOCK), axis=0, keepdims=True)
    kind = iota((8, LANES), 0)
    sums = jnp.where(kind == 0, sums[0], sums[1]) + jnp.where(iota((8, LANES), 1) // modes == kind, extras, 0.0)
    sums_ref[...] = sum([roll(sums, shift) for shift in range(modes, LANES, modes)], sums)


def filter_grads(total, memory_ref, residue_ref, mine_ref, other_ref, *refs):
    results, scratch, sent = refs[:2], refs[2:4], refs[4]
    modes = memory_ref.shape[1]
    scale = jnp.sqrt(2.0 / memory_ref[...]) / math.sqrt(total)
    sums = mine_ref[...] + other_ref[...]
    sum_zero, sum_one = sums[0:1, :modes], sums[1:2, :modes]
    scratch[0][...] = scale * sum_zero
    scratch[1][...] = residue_ref[...] * scale * (sum_one - 0.5 * sum_zero)
    moves = [pltpu.make_async_copy(*ends, sent.at[i]) for i, ends in enumerate(zip(scratch, results))]
    for move in moves:
        move.start()
    for move in moves:
        move.wait()


def finish(seq_size, ch_size, rates_ref, starts_ref, ends_ref, *refs):
    parameters, (x_ref, q_ref, k_ref, d_ref, all_ref), refs = refs[:3], refs[3:8], refs[8:]
    results, scratch, sent = refs[:5], refs[5:10], refs[10]
    moves = [pltpu.make_async_copy(*ends, sent.at[i]) for i, ends in enumerate(zip(scratch, results))]
    channels, local_len = x_ref.shape
    modes = LANES // 8
    chunks = local_len // LANES
    half = channels // 2
    rows = chunks * channels
    signal, gate_in = by_chunk(x_ref), by_chunk(k_ref)
    gate_out, cotangent = by_chunk(q_ref), by_chunk(d_ref)
    weights, powers, base_mixed, base_grad, read_out, read_in = local_parts(
        seq_size, rates_ref, signal * gate_in, cotangent * gate_out, parameters, chunks, channels
    )
    me = 0
    for p, index in enumerate(chip_ranks(ch_size // CORES)):
        me = me + jnp.where(lax.axis_index("ch") // CORES == index, p * seq_size * BLOCK, 0)
    own = iota((half, LANES), 1) // modes == iota((half, LANES), 0)

    def border(kind, weight):
        parts = []
        for part in range(2):
            state = strided(all_ref, me + 2 * kind + part, seq_size, BLOCK)
            state = jnp.sum(weight * state, axis=0, keepdims=True)
            parts.append(jnp.where(own, state, 0.0))
        return jnp.concatenate(parts, axis=0)

    mine = iota((rows, LANES), 1) // modes == iota((rows, LANES), 0) % half

    def readout(state, factors, states, matrix):
        state = jnp.concatenate([factor * state for factor in factors], axis=0) + jnp.where(mine, states, 0.0)
        return contract(left_split(state), right_split(matrix, axis=0), 1, 0)

    mixed = base_mixed + readout(border(0, weights[0]), powers, starts_ref[...], read_out)
    grad_values = base_grad + readout(border(2, weights[1]), powers[::-1], ends_ref[...], read_in)
    skip = jnp.sum(strided(all_ref, me + BLOCK - 1, seq_size, BLOCK), axis=0, keepdims=True)
    skip = roll(skip, -2 * modes)[:, :channels] / math.sqrt(seq_size * local_len)
    for i, data in enumerate((gate_out * mixed, grad_values * gate_in, cotangent * mixed, grad_values * signal)):
        for j in range(chunks):
            scratch[i][:, j * LANES : (j + 1) * LANES] = data[j * channels : (j + 1) * channels].astype(BF16)
    scratch[4][...] = skip
    for move in moves:
        move.start()
    for move in moves:
        move.wait()


def per_device(signal_x, gate_q, gate_k, skip_gain, residue, memory, cotangent):
    channels, local_len = signal_x.shape
    modes = memory.shape[0]
    seq_size, ch_size = lax.axis_size("seq"), lax.axis_size("ch")
    devices = seq_size * ch_size
    params = pltpu.CompilerParams(vmem_limit_bytes=32 * 1024 * 1024)
    in_hbm = pl.BlockSpec(memory_space=pltpu.HBM)
    arguments = (memory[None], residue[None], skip_gain[None], signal_x, gate_q, gate_k, cotangent)
    arguments = [pltpu.with_memory_space_constraint(data, pltpu.HBM) for data in arguments]
    copies = [(data.shape, data.dtype) for data in arguments]
    rows = local_len // LANES * channels
    chips = ch_size // CORES
    peers = chips * seq_size
    made = [((peers * BLOCK, LANES), F32), ((8 + 2 * modes, LANES), F32), ((rows, LANES), F32), ((rows, LANES), F32)]
    mine, rates, starts, ends, *copied = pl.pallas_call(
        make_states,
        in_specs=[in_hbm] * 7,
        out_shape=[jax.ShapeDtypeStruct(*shape) for shape in made + copies],
        scratch_shapes=[pltpu.SemaphoreType.DMA((7,))],
        compiler_params=params,
    )(*arguments)
    groups = [
        [s * ch_size + chip * CORES + core for chip in chip_ranks(chips) for s in seq_ranks(seq_size)]
        for core in range(CORES)
    ]
    everyone = lax.all_to_all(mine.reshape(peers, BLOCK, 1, LANES), AXES, 0, 0, axis_index_groups=groups)
    everyone = everyone.reshape(peers * BLOCK, LANES)
    sums = pl.pallas_call(
        functools.partial(pair_sums, seq_size, chips),
        out_shape=jax.ShapeDtypeStruct((8, LANES), F32),
        compiler_params=params,
    )(rates, everyone)
    other = lax.ppermute(sums, "ch", [(i, i ^ 1) for i in range(ch_size)])
    big = ((channels, local_len), BF16)
    shapes = [big] * 4 + [((1, channels), F32)]
    results = pl.pallas_call(
        functools.partial(finish, seq_size, ch_size),
        out_shape=[jax.ShapeDtypeStruct(*shape) for shape in shapes],
        out_specs=[in_hbm] * 5,
        scratch_shapes=[*[pltpu.VMEM(*shape) for shape in shapes], pltpu.SemaphoreType.DMA((5,))],
        compiler_params=params,
        cost_estimate=pl.CostEstimate(flops=20_000_000, bytes_accessed=1_000_000, transcendentals=10_000),
    )(rates, starts, ends, *copied, everyone)
    small = [((1, modes), F32)] * 2
    filters = pl.pallas_call(
        functools.partial(filter_grads, ch_size * channels * seq_size * local_len),
        out_shape=[jax.ShapeDtypeStruct(*shape) for shape in small],
        out_specs=[in_hbm] * 2,
        scratch_shapes=[*[pltpu.VMEM(*shape) for shape in small], pltpu.SemaphoreType.DMA((2,))],
        compiler_params=params,
    )(copied[0], copied[1], sums, other)
    return (*results[:4], results[4][0], filters[0][0], filters[1][0])


def solution(mesh):
    grid = P("ch", "seq")
    return jax.shard_map(
        per_device,
        mesh=mesh,
        in_specs=(grid, grid, grid, P("ch"), P(), P(), grid),
        out_specs=(grid, grid, grid, grid, P("ch"), P(), P()),
        check_vma=False,
    )
```

```python
import functools
import math

import jax
import jax.numpy as jnp
from jax import lax
from jax.experimental import pallas as pl
from jax.experimental.pallas import tpu as pltpu
from jax.sharding import PartitionSpec as P

F32 = jnp.float32
BF16 = jnp.bfloat16
LANES = 128
AXES = ("seq", "ch")
CORES = 2
BLOCK = 9


def iota(shape, dim):
    return lax.broadcasted_iota(jnp.int32, shape, dim)


def roll(data, shift):
    return pltpu.roll(data, shift % LANES, 1)


def contract(left, right, left_dim, right_dim):
    dims = (((left_dim,), (right_dim,)), ((), ()))
    return lax.dot_general(left, right, dims, preferred_element_type=F32)


def halves(data):
    high = data.astype(BF16)
    return high, (data - high.astype(F32)).astype(BF16)


def left_split(data, axis=1):
    high, low = halves(data)
    return jnp.concatenate([high, low, high], axis=axis)


def right_split(data, axis=1):
    high, low = halves(data)
    return jnp.concatenate([high, high, low], axis=axis)


def by_chunk(ref):
    chunks = ref.shape[1] // LANES
    return jnp.concatenate([ref[:, j * LANES : (j + 1) * LANES].astype(F32) for j in range(chunks)], axis=0)


def column(row):
    size = row.shape[1]
    square = jnp.broadcast_to(row, (size, size))
    return jnp.sum(jnp.where(iota((size, size), 0) == iota((size, size), 1), square, 0.0), axis=1, keepdims=True)


def tiled_row(col):
    size = col.shape[0]
    spread = jnp.where(iota((size, LANES), 1) % size == iota((size, LANES), 0), col, 0.0)
    return jnp.sum(spread, axis=0, keepdims=True)


def decays(inv_col):
    modes = inv_col.shape[0]
    offset = iota((modes, LANES), 1).astype(F32)
    age_in = (LANES - offset) * inv_col
    age_out = offset * inv_col
    return jnp.exp(-age_in), age_in, jnp.exp(-age_out), age_out


def tile_modes(data):
    return jnp.concatenate([data] * (LANES // data.shape[0]), axis=0)


def ranks(size, tuned):
    return tuned if len(tuned) == size else tuple(range(size))


def seq_ranks(seq_size):
    return ranks(seq_size, (5, 0, 4, 6, 1, 7, 2, 3))


def chip_ranks(chips):
    return ranks(chips, (1, 0))


def strided(ref, start, count, stride):
    return ref[pl.ds(start, count, stride=stride), :]


def local_parts(seq_size, rates_ref, values, grads, parameters, chunks, channels):
    rows = chunks * channels
    modes = (rates_ref.shape[0] - 8) // 2
    local_len = chunks * LANES
    me_seq = lax.axis_index("seq")
    inv_row = rates_ref[2:3]
    memory_ref, residue_ref, skip_ref = parameters
    amplitude = column(residue_ref[...] * jnp.sqrt(2.0 / memory_ref[...]))
    read_in, read_out = amplitude * rates_ref[8 : 8 + modes], amplitude * rates_ref[8 + modes :]
    value_split = left_split(values)
    grad_split = left_split(grads)

    taps = jnp.sum(read_out, axis=0, keepdims=True)
    square = (LANES, LANES)
    toeplitz = pltpu.roll(jnp.broadcast_to(taps, square), 0, 1, stride=1, stride_axis=0)
    toeplitz = jnp.where(iota(square, 1) >= iota(square, 0), toeplitz, 0.0)

    device = iota((seq_size, LANES), 0)
    if seq_ranks(seq_size) != tuple(range(seq_size)):
        place = device
        for p, index in enumerate(seq_ranks(seq_size)):
            device = jnp.where(place == p, index, device)
    ahead = (me_seq - 1 - device).astype(F32) * local_len
    behind = (device - me_seq - 1).astype(F32) * local_len
    weights = [jnp.where(far >= 0, jnp.exp(-jnp.maximum(far, 0.0) * inv_row), 0.0) for far in (ahead, behind)]
    powers = [jnp.exp(-float(j * LANES) * inv_row) for j in range(chunks)]

    conv = contract(value_split, right_split(toeplitz, axis=0), 1, 0)
    corr = contract(grad_split, right_split(toeplitz), 1, 1)
    gain = jnp.concatenate([column(skip_ref[...])] * chunks, axis=0)
    return weights, powers, conv + gain * values, corr + gain * grads, tile_modes(read_out), tile_modes(read_in)


def make_states(*refs):
    sources, (out_ref, rates_ref, starts_ref, ends_ref, *copies), arrived = refs[:7], refs[7:18], refs[18]
    moves = [pltpu.make_async_copy(*ends, arrived.at[i]) for i, ends in enumerate(zip(sources, copies))]
    for i in (0, 3, 5, 6, 4, 1, 2):
        moves[i].start()
    memory_ref, _, _, x_ref, q_ref, k_ref, d_ref = copies
    modes = memory_ref.shape[1]
    channels, local_len = x_ref.shape
    chunks = local_len // LANES
    moves[0].wait()
    inv_col = column(1.0 / memory_ref[...])
    inv_row = tiled_row(inv_col)
    decay_in, age_in, decay_out, age_out = decays(inv_col)
    pair_in = jnp.concatenate([tile_modes(decay_in), tile_modes(decay_in * age_in)], axis=0)
    pair_out = jnp.concatenate([tile_modes(decay_out), tile_modes(decay_out * age_out)], axis=0)
    split_in, split_out = right_split(pair_in), right_split(pair_out)
    step = jnp.exp(-LANES * inv_row)
    growth = LANES * inv_row
    leap = jnp.exp(-local_len * inv_row)
    rates_ref[0:1] = leap
    rates_ref[1:2] = leap * (local_len * inv_row)
    rates_ref[2:3] = inv_row
    rates_ref[8 : 8 + modes] = decay_in
    rates_ref[8 + modes :] = decay_out
    moves[3].wait()
    moves[5].wait()
    values = by_chunk(x_ref) * by_chunk(k_ref)
    moves[6].wait()
    moves[4].wait()
    grads = by_chunk(d_ref) * by_chunk(q_ref)
    outer = contract(left_split(values, axis=0), right_split(grads, axis=0), 0, 0)
    outer = jnp.where(iota(outer.shape, 1) >= iota(outer.shape, 0), outer, 0.0)
    turn = (iota(outer.shape, 1) + iota(outer.shape, 0)) % LANES
    skewed = jnp.take_along_axis(outer, turn, axis=1, mode="promise_in_bounds")
    near = decay_out * jnp.sum(skewed, axis=0, keepdims=True)
    near_zero = jnp.sum(near, axis=1, keepdims=True)
    near_one = jnp.sum(near * age_out, axis=1, keepdims=True)
    value_states = contract(left_split(values), split_in, 1, 1)
    grad_states = contract(left_split(grads), split_out, 1, 1)
    products = values * grads
    part_skip = products[:channels]
    for j in range(1, chunks):
        part_skip = part_skip + products[j * channels : (j + 1) * channels]
    part_skip = jnp.sum(part_skip, axis=1, keepdims=True)
    lane = iota((channels, LANES), 1)
    row_id = iota((channels, LANES), 0)
    prefix_zero = jnp.zeros((channels, LANES), F32)
    prefix_one = cross_zero = cross_one = suffix_zero = suffix_one = prefix_zero
    for j in range(chunks):
        rows = slice(j * channels, (j + 1) * channels)
        grad_zero, grad_one = grad_states[rows, :LANES], grad_states[rows, LANES:]
        if j > 0:
            cross_zero = cross_zero + prefix_zero * grad_zero
            cross_one = cross_one + prefix_one * grad_zero + prefix_zero * grad_one
        starts_ref[rows] = prefix_zero
        prefix_one = step * (prefix_one + growth * prefix_zero) + value_states[rows, LANES:]
        prefix_zero = step * prefix_zero + value_states[rows, :LANES]
    for j in range(chunks - 1, -1, -1):
        rows = slice(j * channels, (j + 1) * channels)
        ends_ref[rows] = suffix_zero
        suffix_one = step * (suffix_one + growth * suffix_zero) + grad_states[rows, LANES:]
        suffix_zero = step * suffix_zero + grad_states[rows, :LANES]
    half = channels // 2
    own = lane // modes == row_id % half
    payload = []
    for state in (prefix_zero, prefix_one, suffix_zero, suffix_one):
        state = jnp.where(own, state, 0.0)
        payload.append(jnp.sum(state[:half], axis=0, keepdims=True))
        payload.append(jnp.sum(state[half:], axis=0, keepdims=True))
    extras = (
        jnp.where(lane < modes, cross_zero, 0.0)
        + jnp.where((lane >= modes) & (lane < 2 * modes), cross_one, 0.0)
        + jnp.where(lane == row_id, near_zero, 0.0)
        + jnp.where(lane == row_id + modes, near_one, 0.0)
        + jnp.where(lane == row_id + 2 * modes, part_skip, 0.0)
    )
    payload.append(jnp.sum(extras, axis=0, keepdims=True))
    sublane = iota((8, LANES), 0)
    for k in range(len(payload)):
        tile = jnp.zeros((8, LANES), F32)
        for i in range(8):
            tile = jnp.where(sublane == i, payload[(8 * k + i) % len(payload)], tile)
        for start in range(8 * k, out_ref.shape[0], 8 * len(payload)):
            out_ref[start : start + 8] = tile

    for move in moves[1:3]:
        move.wait()


def pair_sums(seq_size, chips, rates_ref, all_ref, sums_ref):
    modes = LANES // 8
    leap, leap_growth = rates_ref[0:1], rates_ref[1:2]

    def pairs(e, carry):
        done = []
        for part, (prefix_zero, prefix_one, cross_zero, cross_one) in enumerate(carry):
            value_zero, value_one, grad_zero, grad_one = [
                strided(all_ref, e * BLOCK + 2 * kind + part, chips, seq_size * BLOCK) for kind in range(4)
            ]
            done.append(
                (
                    leap * prefix_zero + value_zero,
                    leap * prefix_one + (leap_growth * prefix_zero + value_one),
                    cross_zero + prefix_zero * grad_zero,
                    cross_one + prefix_one * grad_zero + prefix_zero * grad_one,
                )
            )
        return tuple(done)

    zeros = jnp.zeros((chips, LANES), F32)
    carry = ((zeros,) * 4,) * 2
    if seq_size <= 8 or seq_ranks(seq_size) != tuple(range(seq_size)):
        for e in range(seq_size):
            carry = pairs(seq_ranks(seq_size).index(e), carry)
    else:
        carry = lax.fori_loop(0, seq_size, pairs, carry)
    sums = [jnp.sum(carry[0][i] + carry[1][i], axis=0, keepdims=True) for i in (2, 3)]
    extras = jnp.sum(strided(all_ref, BLOCK - 1, chips * seq_size, BLOCK), axis=0, keepdims=True)
    kind = iota((8, LANES), 0)
    sums = jnp.where(kind == 0, sums[0], sums[1]) + jnp.where(iota((8, LANES), 1) // modes == kind, extras, 0.0)
    sums_ref[...] = sum([roll(sums, shift) for shift in range(modes, LANES, modes)], sums)


def filter_grads(total, memory_ref, residue_ref, mine_ref, other_ref, *refs):
    results, scratch, sent = refs[:2], refs[2:4], refs[4]
    modes = memory_ref.shape[1]
    scale = jnp.sqrt(2.0 / memory_ref[...]) / math.sqrt(total)
    sums = mine_ref[...] + other_ref[...]
    sum_zero, sum_one = sums[0:1, :modes], sums[1:2, :modes]
    scratch[0][...] = scale * sum_zero
    scratch[1][...] = residue_ref[...] * scale * (sum_one - 0.5 * sum_zero)
    moves = [pltpu.make_async_copy(*ends, sent.at[i]) for i, ends in enumerate(zip(scratch, results))]
    for move in moves:
        move.start()
    for move in moves:
        move.wait()


def finish(seq_size, ch_size, rates_ref, starts_ref, ends_ref, *refs):
    parameters, (x_ref, q_ref, k_ref, d_ref, all_ref), refs = refs[:3], refs[3:8], refs[8:]
    results, scratch, sent = refs[:5], refs[5:10], refs[10]
    moves = [pltpu.make_async_copy(*ends, sent.at[i]) for i, ends in enumerate(zip(scratch, results))]
    channels, local_len = x_ref.shape
    modes = LANES // 8
    chunks = local_len // LANES
    half = channels // 2
    rows = chunks * channels
    signal, gate_in = by_chunk(x_ref), by_chunk(k_ref)
    gate_out, cotangent = by_chunk(q_ref), by_chunk(d_ref)
    weights, powers, base_mixed, base_grad, read_out, read_in = local_parts(
        seq_size, rates_ref, signal * gate_in, cotangent * gate_out, parameters, chunks, channels
    )
    me = 0
    for p, index in enumerate(chip_ranks(ch_size // CORES)):
        me = me + jnp.where(lax.axis_index("ch") // CORES == index, p * seq_size * BLOCK, 0)
    own = iota((half, LANES), 1) // modes == iota((half, LANES), 0)

    def border(kind, weight):
        parts = []
        for part in range(2):
            state = strided(all_ref, me + 2 * kind + part, seq_size, BLOCK)
            state = jnp.sum(weight * state, axis=0, keepdims=True)
            parts.append(jnp.where(own, state, 0.0))
        return jnp.concatenate(parts, axis=0)

    mine = iota((rows, LANES), 1) // modes == iota((rows, LANES), 0) % half

    def readout(state, factors, states, matrix):
        state = jnp.concatenate([factor * state for factor in factors], axis=0) + jnp.where(mine, states, 0.0)
        return contract(left_split(state), right_split(matrix, axis=0), 1, 0)

    mixed = base_mixed + readout(border(0, weights[0]), powers, starts_ref[...], read_out)
    grad_values = base_grad + readout(border(2, weights[1]), powers[::-1], ends_ref[...], read_in)
    skip = jnp.sum(strided(all_ref, me + BLOCK - 1, seq_size, BLOCK), axis=0, keepdims=True)
    skip = roll(skip, -2 * modes)[:, :channels] / math.sqrt(seq_size * local_len)
    for i, data in enumerate((gate_out * mixed, grad_values * gate_in, cotangent * mixed, grad_values * signal)):
        for j in range(chunks):
            scratch[i][:, j * LANES : (j + 1) * LANES] = data[j * channels : (j + 1) * channels].astype(BF16)
    scratch[4][...] = skip
    for move in moves:
        move.start()
    for move in moves:
        move.wait()


def per_device(signal_x, gate_q, gate_k, skip_gain, residue, memory, cotangent):
    channels, local_len = signal_x.shape
    modes = memory.shape[0]
    seq_size, ch_size = lax.axis_size("seq"), lax.axis_size("ch")
    devices = seq_size * ch_size
    params = pltpu.CompilerParams(vmem_limit_bytes=32 * 1024 * 1024)
    in_hbm = pl.BlockSpec(memory_space=pltpu.HBM)
    arguments = (memory[None], residue[None], skip_gain[None], signal_x, gate_q, gate_k, cotangent)
    arguments = [pltpu.with_memory_space_constraint(data, pltpu.HBM) for data in arguments]
    copies = [(data.shape, data.dtype) for data in arguments]
    rows = local_len // LANES * channels
    chips = ch_size // CORES
    peers = chips * seq_size
    made = [((peers * BLOCK, LANES), F32), ((8 + 2 * modes, LANES), F32), ((rows, LANES), F32), ((rows, LANES), F32)]
    mine, rates, starts, ends, *copied = pl.pallas_call(
        make_states,
        in_specs=[in_hbm] * 7,
        out_shape=[jax.ShapeDtypeStruct(*shape) for shape in made + copies],
        scratch_shapes=[pltpu.SemaphoreType.DMA((7,))],
        compiler_params=params,
    )(*arguments)
    groups = [
        [s * ch_size + chip * CORES + (core + chip) % CORES for chip in chip_ranks(chips) for s in seq_ranks(seq_size)]
        for core in range(CORES)
    ]
    everyone = lax.all_to_all(mine.reshape(peers, BLOCK, 1, LANES), AXES, 0, 0, axis_index_groups=groups)
    everyone = everyone.reshape(peers * BLOCK, LANES)
    sums = pl.pallas_call(
        functools.partial(pair_sums, seq_size, chips),
        out_shape=jax.ShapeDtypeStruct((8, LANES), F32),
        compiler_params=params,
    )(rates, everyone)
    other = lax.ppermute(sums, "ch", [(i, i ^ 1) for i in range(ch_size)])
    big = ((channels, local_len), BF16)
    shapes = [big] * 4 + [((1, channels), F32)]
    results = pl.pallas_call(
        functools.partial(finish, seq_size, ch_size),
        out_shape=[jax.ShapeDtypeStruct(*shape) for shape in shapes],
        out_specs=[in_hbm] * 5,
        scratch_shapes=[*[pltpu.VMEM(*shape) for shape in shapes], pltpu.SemaphoreType.DMA((5,))],
        compiler_params=params,
        cost_estimate=pl.CostEstimate(flops=20_000_000, bytes_accessed=1_000_000, transcendentals=10_000),
    )(rates, starts, ends, *copied, everyone)
    small = [((1, modes), F32)] * 2
    filters = pl.pallas_call(
        functools.partial(filter_grads, ch_size * channels * seq_size * local_len),
        out_shape=[jax.ShapeDtypeStruct(*shape) for shape in small],
        out_specs=[in_hbm] * 2,
        scratch_shapes=[*[pltpu.VMEM(*shape) for shape in small], pltpu.SemaphoreType.DMA((2,))],
        compiler_params=params,
    )(copied[0], copied[1], sums, other)
    return (*results[:4], results[4][0], filters[0][0], filters[1][0])


def solution(mesh):
    grid = P("ch", "seq")
    return jax.shard_map(
        per_device,
        mesh=mesh,
        in_specs=(grid, grid, grid, P("ch"), P(), P(), grid),
        out_specs=(grid, grid, grid, grid, P("ch"), P(), P()),
        check_vma=False,
    )
```

```python
import functools
import math

import jax
import jax.numpy as jnp
from jax import lax
from jax.experimental import pallas as pl
from jax.experimental.pallas import tpu as pltpu
from jax.sharding import PartitionSpec as P

F32 = jnp.float32
BF16 = jnp.bfloat16
LANES = 128
AXES = ("seq", "ch")
CORES = 2
BLOCK = 9


def iota(shape, dim):
    return lax.broadcasted_iota(jnp.int32, shape, dim)


def roll(data, shift):
    return pltpu.roll(data, shift % LANES, 1)


def contract(left, right, left_dim, right_dim):
    dims = (((left_dim,), (right_dim,)), ((), ()))
    return lax.dot_general(left, right, dims, preferred_element_type=F32)


def halves(data):
    high = data.astype(BF16)
    return high, (data - high.astype(F32)).astype(BF16)


def left_split(data, axis=1):
    high, low = halves(data)
    return jnp.concatenate([high, low, high], axis=axis)


def right_split(data, axis=1):
    high, low = halves(data)
    return jnp.concatenate([high, high, low], axis=axis)


def by_chunk(ref):
    chunks = ref.shape[1] // LANES
    return jnp.concatenate([ref[:, j * LANES : (j + 1) * LANES].astype(F32) for j in range(chunks)], axis=0)


def column(row):
    size = row.shape[1]
    square = jnp.broadcast_to(row, (size, size))
    return jnp.sum(jnp.where(iota((size, size), 0) == iota((size, size), 1), square, 0.0), axis=1, keepdims=True)


def tiled_row(col):
    size = col.shape[0]
    spread = jnp.where(iota((size, LANES), 1) % size == iota((size, LANES), 0), col, 0.0)
    return jnp.sum(spread, axis=0, keepdims=True)


def decays(inv_col):
    modes = inv_col.shape[0]
    offset = iota((modes, LANES), 1).astype(F32)
    age_in = (LANES - offset) * inv_col
    age_out = offset * inv_col
    return jnp.exp(-age_in), age_in, jnp.exp(-age_out), age_out


def tile_modes(data):
    return jnp.concatenate([data] * (LANES // data.shape[0]), axis=0)


def ranks(size, tuned):
    return tuned if len(tuned) == size else tuple(range(size))


def seq_ranks(seq_size):
    return ranks(seq_size, (5, 0, 4, 6, 1, 7, 2, 3))


def chip_ranks(chips):
    return ranks(chips, (1, 0))


def strided(ref, start, count, stride):
    return ref[pl.ds(start, count, stride=stride), :]


def local_parts(seq_size, rates_ref, values, grads, parameters, chunks, channels):
    rows = chunks * channels
    modes = (rates_ref.shape[0] - 8) // 2
    local_len = chunks * LANES
    me_seq = lax.axis_index("seq")
    inv_row = rates_ref[2:3]
    memory_ref, residue_ref, skip_ref = parameters
    amplitude = column(residue_ref[...] * jnp.sqrt(2.0 / memory_ref[...]))
    read_in, read_out = amplitude * rates_ref[8 : 8 + modes], amplitude * rates_ref[8 + modes :]
    value_split = left_split(values)
    grad_split = left_split(grads)

    taps = jnp.sum(read_out, axis=0, keepdims=True)
    square = (LANES, LANES)
    toeplitz = pltpu.roll(jnp.broadcast_to(taps, square), 0, 1, stride=1, stride_axis=0)
    toeplitz = jnp.where(iota(square, 1) >= iota(square, 0), toeplitz, 0.0)

    device = iota((seq_size, LANES), 0)
    if seq_ranks(seq_size) != tuple(range(seq_size)):
        place = device
        for p, index in enumerate(seq_ranks(seq_size)):
            device = jnp.where(place == p, index, device)
    ahead = (me_seq - 1 - device).astype(F32) * local_len
    behind = (device - me_seq - 1).astype(F32) * local_len
    weights = [jnp.where(far >= 0, jnp.exp(-jnp.maximum(far, 0.0) * inv_row), 0.0) for far in (ahead, behind)]
    powers = [jnp.exp(-float(j * LANES) * inv_row) for j in range(chunks)]

    conv = contract(value_split, right_split(toeplitz, axis=0), 1, 0)
    corr = contract(grad_split, right_split(toeplitz), 1, 1)
    gain = jnp.concatenate([column(skip_ref[...])] * chunks, axis=0)
    return weights, powers, conv + gain * values, corr + gain * grads, tile_modes(read_out), tile_modes(read_in)


def make_states(*refs):
    sources, (out_ref, rates_ref, starts_ref, ends_ref, *copies), arrived = refs[:7], refs[7:18], refs[18]
    moves = [pltpu.make_async_copy(*ends, arrived.at[i]) for i, ends in enumerate(zip(sources, copies))]
    for i in (0, 6, 4, 3, 5, 1, 2):
        moves[i].start()
    memory_ref, _, _, x_ref, q_ref, k_ref, d_ref = copies
    modes = memory_ref.shape[1]
    channels, local_len = x_ref.shape
    chunks = local_len // LANES
    moves[0].wait()
    inv_col = column(1.0 / memory_ref[...])
    inv_row = tiled_row(inv_col)
    decay_in, age_in, decay_out, age_out = decays(inv_col)
    pair_in = jnp.concatenate([tile_modes(decay_in), tile_modes(decay_in * age_in)], axis=0)
    pair_out = jnp.concatenate([tile_modes(decay_out), tile_modes(decay_out * age_out)], axis=0)
    split_in, split_out = right_split(pair_in), right_split(pair_out)
    step = jnp.exp(-LANES * inv_row)
    growth = LANES * inv_row
    leap = jnp.exp(-local_len * inv_row)
    rates_ref[0:1] = leap
    rates_ref[1:2] = leap * (local_len * inv_row)
    rates_ref[2:3] = inv_row
    rates_ref[3:4, :modes] = jnp.sqrt(2.0 / memory_ref[...])
    rates_ref[8 : 8 + modes] = decay_in
    rates_ref[8 + modes :] = decay_out
    moves[6].wait()
    moves[4].wait()
    grads = by_chunk(d_ref) * by_chunk(q_ref)
    moves[3].wait()
    moves[5].wait()
    values = by_chunk(x_ref) * by_chunk(k_ref)
    outer = contract(left_split(values, axis=0), right_split(grads, axis=0), 0, 0)
    outer = jnp.where(iota(outer.shape, 1) >= iota(outer.shape, 0), outer, 0.0)
    turn = (iota(outer.shape, 1) + iota(outer.shape, 0)) % LANES
    skewed = jnp.take_along_axis(outer, turn, axis=1, mode="promise_in_bounds")
    near = decay_out * jnp.sum(skewed, axis=0, keepdims=True)
    near_zero = jnp.sum(near, axis=1, keepdims=True)
    near_one = jnp.sum(near * age_out, axis=1, keepdims=True)
    value_states = contract(left_split(values), split_in, 1, 1)
    grad_states = contract(left_split(grads), split_out, 1, 1)
    products = values * grads
    part_skip = products[:channels]
    for j in range(1, chunks):
        part_skip = part_skip + products[j * channels : (j + 1) * channels]
    part_skip = jnp.sum(part_skip, axis=1, keepdims=True)
    lane = iota((channels, LANES), 1)
    row_id = iota((channels, LANES), 0)
    prefix_zero = jnp.zeros((channels, LANES), F32)
    prefix_one = cross_zero = cross_one = suffix_zero = suffix_one = prefix_zero
    for j in range(chunks):
        rows = slice(j * channels, (j + 1) * channels)
        grad_zero, grad_one = grad_states[rows, :LANES], grad_states[rows, LANES:]
        if j > 0:
            cross_zero = cross_zero + prefix_zero * grad_zero
            cross_one = cross_one + prefix_one * grad_zero + prefix_zero * grad_one
        starts_ref[rows] = prefix_zero
        prefix_one = step * (prefix_one + growth * prefix_zero) + value_states[rows, LANES:]
        prefix_zero = step * prefix_zero + value_states[rows, :LANES]
    for j in range(chunks - 1, -1, -1):
        rows = slice(j * channels, (j + 1) * channels)
        ends_ref[rows] = suffix_zero
        suffix_one = step * (suffix_one + growth * suffix_zero) + grad_states[rows, LANES:]
        suffix_zero = step * suffix_zero + grad_states[rows, :LANES]
    half = channels // 2
    own = lane // modes == row_id % half
    payload = []
    for state in (prefix_zero, prefix_one, suffix_zero, suffix_one):
        state = jnp.where(own, state, 0.0)
        payload.append(jnp.sum(state[:half], axis=0, keepdims=True))
        payload.append(jnp.sum(state[half:], axis=0, keepdims=True))
    extras = (
        jnp.where(lane < modes, cross_zero, 0.0)
        + jnp.where((lane >= modes) & (lane < 2 * modes), cross_one, 0.0)
        + jnp.where(lane == row_id, near_zero, 0.0)
        + jnp.where(lane == row_id + modes, near_one, 0.0)
        + jnp.where(lane == row_id + 2 * modes, part_skip, 0.0)
    )
    payload.append(jnp.sum(extras, axis=0, keepdims=True))
    sublane = iota((8, LANES), 0)
    for k in range(len(payload)):
        tile = jnp.zeros((8, LANES), F32)
        for i in range(8):
            tile = jnp.where(sublane == i, payload[(8 * k + i) % len(payload)], tile)
        for start in range(8 * k, out_ref.shape[0], 8 * len(payload)):
            out_ref[start : start + 8] = tile

    for move in moves[1:3]:
        move.wait()


def pair_sums(seq_size, chips, rates_ref, all_ref, sums_ref):
    modes = LANES // 8
    leap, leap_growth = rates_ref[0:1], rates_ref[1:2]

    def pairs(e, carry):
        done = []
        for part, (prefix_zero, prefix_one, cross_zero, cross_one) in enumerate(carry):
            value_zero, value_one, grad_zero, grad_one = [
                strided(all_ref, e * BLOCK + 2 * kind + part, chips, seq_size * BLOCK) for kind in range(4)
            ]
            done.append(
                (
                    leap * prefix_zero + value_zero,
                    leap * prefix_one + (leap_growth * prefix_zero + value_one),
                    cross_zero + prefix_zero * grad_zero,
                    cross_one + prefix_one * grad_zero + prefix_zero * grad_one,
                )
            )
        return tuple(done)

    zeros = jnp.zeros((chips, LANES), F32)
    carry = ((zeros,) * 4,) * 2
    if seq_size <= 8 or seq_ranks(seq_size) != tuple(range(seq_size)):
        for e in range(seq_size):
            carry = pairs(seq_ranks(seq_size).index(e), carry)
    else:
        carry = lax.fori_loop(0, seq_size, pairs, carry)
    sums = [jnp.sum(carry[0][i] + carry[1][i], axis=0, keepdims=True) for i in (2, 3)]
    extras = jnp.sum(strided(all_ref, BLOCK - 1, chips * seq_size, BLOCK), axis=0, keepdims=True)
    kind = iota((8, LANES), 0)
    sums = jnp.where(kind == 0, sums[0], sums[1]) + jnp.where(iota((8, LANES), 1) // modes == kind, extras, 0.0)
    sums_ref[...] = sum([roll(sums, shift) for shift in range(modes, LANES, modes)], sums)


def filter_grads(total, rates_ref, residue_ref, mine_ref, other_ref, *refs):
    results, scratch, sent = refs[:2], refs[2:4], refs[4]
    modes = residue_ref.shape[1]
    scale = rates_ref[3:4, :modes] * (1.0 / math.sqrt(total))
    sums = mine_ref[...] + other_ref[...]
    sum_zero, sum_one = sums[0:1, :modes], sums[1:2, :modes]
    scratch[0][...] = scale * sum_zero
    scratch[1][...] = residue_ref[...] * scale * (sum_one - 0.5 * sum_zero)
    moves = [pltpu.make_async_copy(*ends, sent.at[i]) for i, ends in enumerate(zip(scratch, results))]
    for move in moves:
        move.start()
    for move in moves:
        move.wait()


def finish(seq_size, ch_size, rates_ref, starts_ref, ends_ref, *refs):
    parameters, (x_ref, q_ref, k_ref, d_ref, all_ref), refs = refs[:3], refs[3:8], refs[8:]
    results, scratch, sent = refs[:5], refs[5:10], refs[10]
    moves = [pltpu.make_async_copy(*ends, sent.at[i]) for i, ends in enumerate(zip(scratch, results))]
    channels, local_len = x_ref.shape
    modes = LANES // 8
    chunks = local_len // LANES
    half = channels // 2
    rows = chunks * channels
    signal, gate_in = by_chunk(x_ref), by_chunk(k_ref)
    gate_out, cotangent = by_chunk(q_ref), by_chunk(d_ref)
    weights, powers, base_mixed, base_grad, read_out, read_in = local_parts(
        seq_size, rates_ref, signal * gate_in, cotangent * gate_out, parameters, chunks, channels
    )
    me = 0
    for p, index in enumerate(chip_ranks(ch_size // CORES)):
        me = me + jnp.where(lax.axis_index("ch") // CORES == index, p * seq_size * BLOCK, 0)
    own = iota((half, LANES), 1) // modes == iota((half, LANES), 0)

    def border(kind, weight):
        parts = []
        for part in range(2):
            state = strided(all_ref, me + 2 * kind + part, seq_size, BLOCK)
            state = jnp.sum(weight * state, axis=0, keepdims=True)
            parts.append(jnp.where(own, state, 0.0))
        return jnp.concatenate(parts, axis=0)

    mine = iota((rows, LANES), 1) // modes == iota((rows, LANES), 0) % half

    def readout(state, factors, states, matrix):
        state = jnp.concatenate([factor * state for factor in factors], axis=0) + jnp.where(mine, states, 0.0)
        return contract(left_split(state), right_split(matrix, axis=0), 1, 0)

    mixed = base_mixed + readout(border(0, weights[0]), powers, starts_ref[...], read_out)
    grad_values = base_grad + readout(border(2, weights[1]), powers[::-1], ends_ref[...], read_in)
    skip = jnp.sum(strided(all_ref, me + BLOCK - 1, seq_size, BLOCK), axis=0, keepdims=True)
    skip = roll(skip, -2 * modes)[:, :channels] / math.sqrt(seq_size * local_len)
    for i, data in enumerate((gate_out * mixed, grad_values * gate_in, cotangent * mixed, grad_values * signal)):
        for j in range(chunks):
            scratch[i][:, j * LANES : (j + 1) * LANES] = data[j * channels : (j + 1) * channels].astype(BF16)
    scratch[4][...] = skip
    for move in moves:
        move.start()
    for move in moves:
        move.wait()


def per_device(signal_x, gate_q, gate_k, skip_gain, residue, memory, cotangent):
    channels, local_len = signal_x.shape
    modes = memory.shape[0]
    seq_size, ch_size = lax.axis_size("seq"), lax.axis_size("ch")
    devices = seq_size * ch_size
    params = pltpu.CompilerParams(vmem_limit_bytes=32 * 1024 * 1024)
    in_hbm = pl.BlockSpec(memory_space=pltpu.HBM)
    arguments = (memory[None], residue[None], skip_gain[None], signal_x, gate_q, gate_k, cotangent)
    arguments = [pltpu.with_memory_space_constraint(data, pltpu.HBM) for data in arguments]
    copies = [(data.shape, data.dtype) for data in arguments]
    rows = local_len // LANES * channels
    chips = ch_size // CORES
    peers = chips * seq_size
    made = [((peers * BLOCK, LANES), F32), ((8 + 2 * modes, LANES), F32), ((rows, LANES), F32), ((rows, LANES), F32)]
    mine, rates, starts, ends, *copied = pl.pallas_call(
        make_states,
        in_specs=[in_hbm] * 7,
        out_shape=[jax.ShapeDtypeStruct(*shape) for shape in made + copies],
        scratch_shapes=[pltpu.SemaphoreType.DMA((7,))],
        compiler_params=params,
    )(*arguments)
    groups = [
        [s * ch_size + chip * CORES + (core + chip) % CORES for chip in chip_ranks(chips) for s in seq_ranks(seq_size)]
        for core in range(CORES)
    ]
    everyone = lax.all_to_all(mine.reshape(peers, BLOCK, 1, LANES), AXES, 0, 0, axis_index_groups=groups)
    everyone = everyone.reshape(peers * BLOCK, LANES)
    sums = pl.pallas_call(
        functools.partial(pair_sums, seq_size, chips),
        out_shape=jax.ShapeDtypeStruct((8, LANES), F32),
        compiler_params=params,
    )(rates, everyone)
    other = lax.ppermute(sums, "ch", [(i, i ^ 1) for i in range(ch_size)])
    big = ((channels, local_len), BF16)
    shapes = [big] * 4 + [((1, channels), F32)]
    results = pl.pallas_call(
        functools.partial(finish, seq_size, ch_size),
        out_shape=[jax.ShapeDtypeStruct(*shape) for shape in shapes],
        out_specs=[in_hbm] * 5,
        scratch_shapes=[*[pltpu.VMEM(*shape) for shape in shapes], pltpu.SemaphoreType.DMA((5,))],
        compiler_params=params,
        cost_estimate=pl.CostEstimate(flops=20_000_000, bytes_accessed=1_000_000, transcendentals=10_000),
    )(rates, starts, ends, *copied, everyone)
    small = [((1, modes), F32)] * 2
    filters = pl.pallas_call(
        functools.partial(filter_grads, ch_size * channels * seq_size * local_len),
        out_shape=[jax.ShapeDtypeStruct(*shape) for shape in small],
        out_specs=[in_hbm] * 2,
        scratch_shapes=[*[pltpu.VMEM(*shape) for shape in small], pltpu.SemaphoreType.DMA((2,))],
        compiler_params=params,
    )(rates, copied[1], sums, other)
    return (*results[:4], results[4][0], filters[0][0], filters[1][0])


def solution(mesh):
    grid = P("ch", "seq")
    return jax.shard_map(
        per_device,
        mesh=mesh,
        in_specs=(grid, grid, grid, P("ch"), P(), P(), grid),
        out_specs=(grid, grid, grid, grid, P("ch"), P(), P()),
        check_vma=False,
    )
```

```python
import functools
import math

import jax
import jax.numpy as jnp
from jax import lax
from jax.experimental import pallas as pl
from jax.experimental.pallas import tpu as pltpu
from jax.sharding import PartitionSpec as P

F32 = jnp.float32
BF16 = jnp.bfloat16
LANES = 128
AXES = ("seq", "ch")
CORES = 2
BLOCK = 9


def iota(shape, dim):
    return lax.broadcasted_iota(jnp.int32, shape, dim)


def roll(data, shift):
    return pltpu.roll(data, shift % LANES, 1)


def contract(left, right, left_dim, right_dim):
    dims = (((left_dim,), (right_dim,)), ((), ()))
    return lax.dot_general(left, right, dims, preferred_element_type=F32)


def halves(data):
    high = data.astype(BF16)
    return high, (data - high.astype(F32)).astype(BF16)


def left_split(data, axis=1):
    high, low = halves(data)
    return jnp.concatenate([high, low, high], axis=axis)


def right_split(data, axis=1):
    high, low = halves(data)
    return jnp.concatenate([high, high, low], axis=axis)


def by_chunk(ref):
    chunks = ref.shape[1] // LANES
    return jnp.concatenate([ref[:, j * LANES : (j + 1) * LANES].astype(F32) for j in range(chunks)], axis=0)


def column(row):
    size = row.shape[1]
    square = jnp.broadcast_to(row, (size, size))
    return jnp.sum(jnp.where(iota((size, size), 0) == iota((size, size), 1), square, 0.0), axis=1, keepdims=True)


def tiled_row(col):
    size = col.shape[0]
    spread = jnp.where(iota((size, LANES), 1) % size == iota((size, LANES), 0), col, 0.0)
    return jnp.sum(spread, axis=0, keepdims=True)


def decays(inv_col):
    modes = inv_col.shape[0]
    offset = iota((modes, LANES), 1).astype(F32)
    age_in = (LANES - offset) * inv_col
    age_out = offset * inv_col
    return jnp.exp(-age_in), age_in, jnp.exp(-age_out), age_out


def tile_modes(data):
    return jnp.concatenate([data] * (LANES // data.shape[0]), axis=0)


def ranks(size, tuned):
    return tuned if len(tuned) == size else tuple(range(size))


def seq_ranks(seq_size):
    return ranks(seq_size, (5, 0, 4, 6, 1, 7, 2, 3))


def chip_ranks(chips):
    return ranks(chips, (1, 0))


def strided(ref, start, count, stride):
    return ref[pl.ds(start, count, stride=stride), :]


def local_parts(seq_size, rates_ref, values, grads, parameters, chunks, channels):
    rows = chunks * channels
    modes = (rates_ref.shape[0] - 8) // 2
    local_len = chunks * LANES
    me_seq = lax.axis_index("seq")
    inv_row = rates_ref[2:3]
    memory_ref, residue_ref, skip_ref = parameters
    amplitude = column(residue_ref[...] * jnp.sqrt(2.0 / memory_ref[...]))
    read_in, read_out = amplitude * rates_ref[8 : 8 + modes], amplitude * rates_ref[8 + modes :]
    value_split = left_split(values)
    grad_split = left_split(grads)

    taps = jnp.sum(read_out, axis=0, keepdims=True)
    square = (LANES, LANES)
    toeplitz = pltpu.roll(jnp.broadcast_to(taps, square), 0, 1, stride=1, stride_axis=0)
    toeplitz = jnp.where(iota(square, 1) >= iota(square, 0), toeplitz, 0.0)

    device = iota((seq_size, LANES), 0)
    if seq_ranks(seq_size) != tuple(range(seq_size)):
        place = device
        for p, index in enumerate(seq_ranks(seq_size)):
            device = jnp.where(place == p, index, device)
    ahead = (me_seq - 1 - device).astype(F32) * local_len
    behind = (device - me_seq - 1).astype(F32) * local_len
    weights = [jnp.where(far >= 0, jnp.exp(-jnp.maximum(far, 0.0) * inv_row), 0.0) for far in (ahead, behind)]
    powers = [jnp.exp(-float(j * LANES) * inv_row) for j in range(chunks)]

    conv = contract(value_split, right_split(toeplitz, axis=0), 1, 0)
    corr = contract(grad_split, right_split(toeplitz), 1, 1)
    gain = jnp.concatenate([column(skip_ref[...])] * chunks, axis=0)
    return weights, powers, conv + gain * values, corr + gain * grads, tile_modes(read_out), tile_modes(read_in)


def make_states(*refs):
    sources, (out_ref, rates_ref, starts_ref, ends_ref, *copies), arrived = refs[:7], refs[7:18], refs[18]
    moves = [pltpu.make_async_copy(*ends, arrived.at[i]) for i, ends in enumerate(zip(sources, copies))]
    for i in (0, 3, 5, 6, 4, 1, 2):
        moves[i].start()
    memory_ref, _, _, x_ref, q_ref, k_ref, d_ref = copies
    modes = memory_ref.shape[1]
    channels, local_len = x_ref.shape
    chunks = local_len // LANES
    moves[0].wait()
    inv_col = column(1.0 / memory_ref[...])
    inv_row = tiled_row(inv_col)
    decay_in, age_in, decay_out, age_out = decays(inv_col)
    pair_in = jnp.concatenate([tile_modes(decay_in), tile_modes(decay_in * age_in)], axis=0)
    pair_out = jnp.concatenate([tile_modes(decay_out), tile_modes(decay_out * age_out)], axis=0)
    split_in, split_out = right_split(pair_in), right_split(pair_out)
    step = jnp.exp(-LANES * inv_row)
    growth = LANES * inv_row
    leap = jnp.exp(-local_len * inv_row)
    rates_ref[0:1] = leap
    rates_ref[1:2] = leap * (local_len * inv_row)
    rates_ref[2:3] = inv_row
    rates_ref[8 : 8 + modes] = decay_in
    rates_ref[8 + modes :] = decay_out
    moves[3].wait()
    moves[5].wait()
    values = by_chunk(x_ref) * by_chunk(k_ref)
    moves[6].wait()
    moves[4].wait()
    grads = by_chunk(d_ref) * by_chunk(q_ref)
    outer = contract(left_split(values, axis=0), right_split(grads, axis=0), 0, 0)
    outer = jnp.where(iota(outer.shape, 1) >= iota(outer.shape, 0), outer, 0.0)
    turn = (iota(outer.shape, 1) + iota(outer.shape, 0)) % LANES
    skewed = jnp.take_along_axis(outer, turn, axis=1, mode="promise_in_bounds")
    near = decay_out * jnp.sum(skewed, axis=0, keepdims=True)
    near_zero = jnp.sum(near, axis=1, keepdims=True)
    near_one = jnp.sum(near * age_out, axis=1, keepdims=True)
    value_states = contract(left_split(values), split_in, 1, 1)
    grad_states = contract(left_split(grads), split_out, 1, 1)
    products = values * grads
    part_skip = products[:channels]
    for j in range(1, chunks):
        part_skip = part_skip + products[j * channels : (j + 1) * channels]
    part_skip = jnp.sum(part_skip, axis=1, keepdims=True)
    lane = iota((channels, LANES), 1)
    row_id = iota((channels, LANES), 0)
    prefix_zero = jnp.zeros((channels, LANES), F32)
    prefix_one = cross_zero = cross_one = suffix_zero = suffix_one = prefix_zero
    for j in range(chunks):
        rows = slice(j * channels, (j + 1) * channels)
        grad_zero, grad_one = grad_states[rows, :LANES], grad_states[rows, LANES:]
        if j > 0:
            cross_zero = cross_zero + prefix_zero * grad_zero
            cross_one = cross_one + prefix_one * grad_zero + prefix_zero * grad_one
        starts_ref[rows] = prefix_zero
        prefix_one = step * (prefix_one + growth * prefix_zero) + value_states[rows, LANES:]
        prefix_zero = step * prefix_zero + value_states[rows, :LANES]
    for j in range(chunks - 1, -1, -1):
        rows = slice(j * channels, (j + 1) * channels)
        ends_ref[rows] = suffix_zero
        suffix_one = step * (suffix_one + growth * suffix_zero) + grad_states[rows, LANES:]
        suffix_zero = step * suffix_zero + grad_states[rows, :LANES]
    half = channels // 2
    own = lane // modes == row_id % half
    payload = []
    for state in (prefix_zero, prefix_one, suffix_zero, suffix_one):
        state = jnp.where(own, state, 0.0)
        payload.append(jnp.sum(state[:half], axis=0, keepdims=True))
        payload.append(jnp.sum(state[half:], axis=0, keepdims=True))
    extras = (
        jnp.where(lane < modes, cross_zero, 0.0)
        + jnp.where((lane >= modes) & (lane < 2 * modes), cross_one, 0.0)
        + jnp.where(lane == row_id, near_zero, 0.0)
        + jnp.where(lane == row_id + modes, near_one, 0.0)
        + jnp.where(lane == row_id + 2 * modes, part_skip, 0.0)
    )
    payload.append(jnp.sum(extras, axis=0, keepdims=True))
    sublane = iota((8, LANES), 0)
    for k in range(len(payload)):
        tile = jnp.zeros((8, LANES), F32)
        for i in range(8):
            tile = jnp.where(sublane == i, payload[(8 * k + i) % len(payload)], tile)
        for start in range(8 * k, out_ref.shape[0], 8 * len(payload)):
            out_ref[start : start + 8] = tile

    for move in moves[1:3]:
        move.wait()


def pair_sums(seq_size, chips, rates_ref, all_ref, sums_ref):
    modes = LANES // 8
    leap, leap_growth = rates_ref[0:1], rates_ref[1:2]

    def pairs(e, carry):
        done = []
        for part, (prefix_zero, prefix_one, cross_zero, cross_one) in enumerate(carry):
            value_zero, value_one, grad_zero, grad_one = [
                strided(all_ref, e * BLOCK + 2 * kind + part, chips, seq_size * BLOCK) for kind in range(4)
            ]
            done.append(
                (
                    leap * prefix_zero + value_zero,
                    leap * prefix_one + (leap_growth * prefix_zero + value_one),
                    cross_zero + prefix_zero * grad_zero,
                    cross_one + prefix_one * grad_zero + prefix_zero * grad_one,
                )
            )
        return tuple(done)

    zeros = jnp.zeros((chips, LANES), F32)
    carry = ((zeros,) * 4,) * 2
    if seq_size <= 8 or seq_ranks(seq_size) != tuple(range(seq_size)):
        for e in range(seq_size):
            carry = pairs(seq_ranks(seq_size).index(e), carry)
    else:
        carry = lax.fori_loop(0, seq_size, pairs, carry)
    sums = [jnp.sum(carry[0][i] + carry[1][i], axis=0, keepdims=True) for i in (2, 3)]
    extras = jnp.sum(strided(all_ref, BLOCK - 1, chips * seq_size, BLOCK), axis=0, keepdims=True)
    kind = iota((2, LANES), 0)
    sums = jnp.where(kind == 0, sums[0], sums[1]) + jnp.where(iota((2, LANES), 1) // modes == kind, extras, 0.0)
    sums_ref[...] = sum([roll(sums, shift) for shift in range(modes, LANES, modes)], sums)


def filter_grads(total, memory_ref, residue_ref, mine_ref, other_ref, *refs):
    results, scratch, sent = refs[:2], refs[2:4], refs[4]
    modes = memory_ref.shape[1]
    scale = jnp.sqrt(2.0 / memory_ref[...]) / math.sqrt(total)
    sums = mine_ref[...] + other_ref[...]
    sum_zero, sum_one = sums[0:1, :modes], sums[1:2, :modes]
    scratch[0][...] = scale * sum_zero
    scratch[1][...] = residue_ref[...] * scale * (sum_one - 0.5 * sum_zero)
    moves = [pltpu.make_async_copy(*ends, sent.at[i]) for i, ends in enumerate(zip(scratch, results))]
    for move in moves:
        move.start()
    for move in moves:
        move.wait()


def finish(seq_size, ch_size, rates_ref, starts_ref, ends_ref, *refs):
    parameters, (x_ref, q_ref, k_ref, d_ref, all_ref), refs = refs[:3], refs[3:8], refs[8:]
    results, scratch, sent = refs[:5], refs[5:10], refs[10]
    moves = [pltpu.make_async_copy(*ends, sent.at[i]) for i, ends in enumerate(zip(scratch, results))]
    channels, local_len = x_ref.shape
    modes = LANES // 8
    chunks = local_len // LANES
    half = channels // 2
    rows = chunks * channels
    signal, gate_in = by_chunk(x_ref), by_chunk(k_ref)
    gate_out, cotangent = by_chunk(q_ref), by_chunk(d_ref)
    weights, powers, base_mixed, base_grad, read_out, read_in = local_parts(
        seq_size, rates_ref, signal * gate_in, cotangent * gate_out, parameters, chunks, channels
    )
    me = 0
    for p, index in enumerate(chip_ranks(ch_size // CORES)):
        me = me + jnp.where(lax.axis_index("ch") // CORES == index, p * seq_size * BLOCK, 0)
    own = iota((half, LANES), 1) // modes == iota((half, LANES), 0)

    def border(kind, weight):
        parts = []
        for part in range(2):
            state = strided(all_ref, me + 2 * kind + part, seq_size, BLOCK)
            state = jnp.sum(weight * state, axis=0, keepdims=True)
            parts.append(jnp.where(own, state, 0.0))
        return jnp.concatenate(parts, axis=0)

    mine = iota((rows, LANES), 1) // modes == iota((rows, LANES), 0) % half

    def readout(state, factors, states, matrix):
        state = jnp.concatenate([factor * state for factor in factors], axis=0) + jnp.where(mine, states, 0.0)
        return contract(left_split(state), right_split(matrix, axis=0), 1, 0)

    mixed = base_mixed + readout(border(0, weights[0]), powers, starts_ref[...], read_out)
    grad_values = base_grad + readout(border(2, weights[1]), powers[::-1], ends_ref[...], read_in)
    skip = jnp.sum(strided(all_ref, me + BLOCK - 1, seq_size, BLOCK), axis=0, keepdims=True)
    skip = roll(skip, -2 * modes)[:, :channels] / math.sqrt(seq_size * local_len)
    for i, data in enumerate((gate_out * mixed, grad_values * gate_in, cotangent * mixed, grad_values * signal)):
        for j in range(chunks):
            scratch[i][:, j * LANES : (j + 1) * LANES] = data[j * channels : (j + 1) * channels].astype(BF16)
    scratch[4][...] = skip
    for move in moves:
        move.start()
    for move in moves:
        move.wait()


def per_device(signal_x, gate_q, gate_k, skip_gain, residue, memory, cotangent):
    channels, local_len = signal_x.shape
    modes = memory.shape[0]
    seq_size, ch_size = lax.axis_size("seq"), lax.axis_size("ch")
    devices = seq_size * ch_size
    params = pltpu.CompilerParams(vmem_limit_bytes=32 * 1024 * 1024)
    in_hbm = pl.BlockSpec(memory_space=pltpu.HBM)
    arguments = (memory[None], residue[None], skip_gain[None], signal_x, gate_q, gate_k, cotangent)
    arguments = [pltpu.with_memory_space_constraint(data, pltpu.HBM) for data in arguments]
    copies = [(data.shape, data.dtype) for data in arguments]
    rows = local_len // LANES * channels
    chips = ch_size // CORES
    peers = chips * seq_size
    made = [((peers * BLOCK, LANES), F32), ((8 + 2 * modes, LANES), F32), ((rows, LANES), F32), ((rows, LANES), F32)]
    mine, rates, starts, ends, *copied = pl.pallas_call(
        make_states,
        in_specs=[in_hbm] * 7,
        out_shape=[jax.ShapeDtypeStruct(*shape) for shape in made + copies],
        scratch_shapes=[pltpu.SemaphoreType.DMA((7,))],
        compiler_params=params,
    )(*arguments)
    groups = [
        [s * ch_size + chip * CORES + (core + chip) % CORES for chip in chip_ranks(chips) for s in seq_ranks(seq_size)]
        for core in range(CORES)
    ]
    everyone = lax.all_to_all(mine.reshape(peers, BLOCK, 1, LANES), AXES, 0, 0, axis_index_groups=groups)
    everyone = everyone.reshape(peers * BLOCK, LANES)
    sums = pl.pallas_call(
        functools.partial(pair_sums, seq_size, chips),
        out_shape=jax.ShapeDtypeStruct((2, LANES), F32),
        compiler_params=params,
    )(rates, everyone)
    other = lax.ppermute(sums, "ch", [(i, i ^ 1) for i in range(ch_size)])
    big = ((channels, local_len), BF16)
    shapes = [big] * 4 + [((1, channels), F32)]
    results = pl.pallas_call(
        functools.partial(finish, seq_size, ch_size),
        out_shape=[jax.ShapeDtypeStruct(*shape) for shape in shapes],
        out_specs=[in_hbm] * 5,
        scratch_shapes=[*[pltpu.VMEM(*shape) for shape in shapes], pltpu.SemaphoreType.DMA((5,))],
        compiler_params=params,
        cost_estimate=pl.CostEstimate(flops=20_000_000, bytes_accessed=1_000_000, transcendentals=10_000),
    )(rates, starts, ends, *copied, everyone)
    small = [((1, modes), F32)] * 2
    filters = pl.pallas_call(
        functools.partial(filter_grads, ch_size * channels * seq_size * local_len),
        out_shape=[jax.ShapeDtypeStruct(*shape) for shape in small],
        out_specs=[in_hbm] * 2,
        scratch_shapes=[*[pltpu.VMEM(*shape) for shape in small], pltpu.SemaphoreType.DMA((2,))],
        compiler_params=params,
    )(copied[0], copied[1], sums, other)
    return (*results[:4], results[4][0], filters[0][0], filters[1][0])


def solution(mesh):
    grid = P("ch", "seq")
    return jax.shard_map(
        per_device,
        mesh=mesh,
        in_specs=(grid, grid, grid, P("ch"), P(), P(), grid),
        out_specs=(grid, grid, grid, grid, P("ch"), P(), P()),
        check_vma=False,
    )
```

```python
import functools
import math

import jax
import jax.numpy as jnp
from jax import lax
from jax.experimental import pallas as pl
from jax.experimental.pallas import tpu as pltpu
from jax.sharding import PartitionSpec as P

F32 = jnp.float32
BF16 = jnp.bfloat16
LANES = 128
AXES = ("seq", "ch")
CORES = 2
BLOCK = 9


def iota(shape, dim):
    return lax.broadcasted_iota(jnp.int32, shape, dim)


def roll(data, shift):
    return pltpu.roll(data, shift % LANES, 1)


def contract(left, right, left_dim, right_dim):
    dims = (((left_dim,), (right_dim,)), ((), ()))
    return lax.dot_general(left, right, dims, preferred_element_type=F32)


def halves(data):
    high = data.astype(BF16)
    return high, (data - high.astype(F32)).astype(BF16)


def left_split(data, axis=1):
    high, low = halves(data)
    return jnp.concatenate([high, low, high], axis=axis)


def right_split(data, axis=1):
    high, low = halves(data)
    return jnp.concatenate([high, high, low], axis=axis)


def by_chunk(ref):
    chunks = ref.shape[1] // LANES
    return jnp.concatenate([ref[:, j * LANES : (j + 1) * LANES].astype(F32) for j in range(chunks)], axis=0)


def column(row):
    size = row.shape[1]
    square = jnp.broadcast_to(row, (size, size))
    return jnp.sum(jnp.where(iota((size, size), 0) == iota((size, size), 1), square, 0.0), axis=1, keepdims=True)


def tiled_row(col):
    size = col.shape[0]
    spread = jnp.where(iota((size, LANES), 1) % size == iota((size, LANES), 0), col, 0.0)
    return jnp.sum(spread, axis=0, keepdims=True)


def decays(inv_col):
    modes = inv_col.shape[0]
    offset = iota((modes, LANES), 1).astype(F32)
    age_in = (LANES - offset) * inv_col
    age_out = offset * inv_col
    return jnp.exp(-age_in), age_in, jnp.exp(-age_out), age_out


def tile_modes(data):
    return jnp.concatenate([data] * (LANES // data.shape[0]), axis=0)


def ranks(size, tuned):
    return tuned if len(tuned) == size else tuple(range(size))


def seq_ranks(seq_size):
    return ranks(seq_size, (5, 0, 4, 6, 1, 7, 2, 3))


def chip_ranks(chips):
    return ranks(chips, (1, 0))


def strided(ref, start, count, stride):
    return ref[pl.ds(start, count, stride=stride), :]


def local_parts(seq_size, rates_ref, values, grads, parameters, chunks, channels):
    rows = chunks * channels
    modes = (rates_ref.shape[0] - 8) // 2
    local_len = chunks * LANES
    me_seq = lax.axis_index("seq")
    inv_row = rates_ref[2:3]
    memory_ref, residue_ref, skip_ref = parameters
    amplitude = column(residue_ref[...] * jnp.sqrt(2.0 / memory_ref[...]))
    read_in, read_out = amplitude * rates_ref[8 : 8 + modes], amplitude * rates_ref[8 + modes :]
    value_split = left_split(values)
    grad_split = left_split(grads)

    taps = jnp.sum(read_out, axis=0, keepdims=True)
    square = (LANES, LANES)
    toeplitz = pltpu.roll(jnp.broadcast_to(taps, square), 0, 1, stride=1, stride_axis=0)
    toeplitz = jnp.where(iota(square, 1) >= iota(square, 0), toeplitz, 0.0)

    device = iota((seq_size, LANES), 0)
    if seq_ranks(seq_size) != tuple(range(seq_size)):
        place = device
        for p, index in enumerate(seq_ranks(seq_size)):
            device = jnp.where(place == p, index, device)
    ahead = (me_seq - 1 - device).astype(F32) * local_len
    behind = (device - me_seq - 1).astype(F32) * local_len
    weights = [jnp.where(far >= 0, jnp.exp(-jnp.maximum(far, 0.0) * inv_row), 0.0) for far in (ahead, behind)]
    powers = [jnp.exp(-float(j * LANES) * inv_row) for j in range(chunks)]

    conv = contract(value_split, right_split(toeplitz, axis=0), 1, 0)
    corr = contract(grad_split, right_split(toeplitz), 1, 1)
    gain = jnp.concatenate([column(skip_ref[...])] * chunks, axis=0)
    return weights, powers, conv + gain * values, corr + gain * grads, tile_modes(read_out), tile_modes(read_in)


def make_states(*refs):
    sources, (out_ref, rates_ref, starts_ref, ends_ref, *copies), arrived = refs[:7], refs[7:18], refs[18]
    moves = [pltpu.make_async_copy(*ends, arrived.at[i]) for i, ends in enumerate(zip(sources, copies))]
    for i in (0, 3, 5, 6, 4, 1, 2):
        moves[i].start()
    memory_ref, _, _, x_ref, q_ref, k_ref, d_ref = copies
    modes = memory_ref.shape[1]
    channels, local_len = x_ref.shape
    chunks = local_len // LANES
    moves[0].wait()
    inv_col = column(1.0 / memory_ref[...])
    inv_row = tiled_row(inv_col)
    decay_in, age_in, decay_out, age_out = decays(inv_col)
    pair_in = jnp.concatenate([tile_modes(decay_in), tile_modes(decay_in * age_in)], axis=0)
    pair_out = jnp.concatenate([tile_modes(decay_out), tile_modes(decay_out * age_out)], axis=0)
    split_in, split_out = right_split(pair_in), right_split(pair_out)
    step = jnp.exp(-LANES * inv_row)
    growth = LANES * inv_row
    leap = jnp.exp(-local_len * inv_row)
    rates_ref[0:1] = leap
    rates_ref[1:2] = leap * (local_len * inv_row)
    rates_ref[2:3] = inv_row
    rates_ref[8 : 8 + modes] = decay_in
    rates_ref[8 + modes :] = decay_out
    moves[3].wait()
    moves[5].wait()
    values = by_chunk(x_ref) * by_chunk(k_ref)
    moves[6].wait()
    moves[4].wait()
    grads = by_chunk(d_ref) * by_chunk(q_ref)
    outer = contract(left_split(values, axis=0), right_split(grads, axis=0), 0, 0)
    outer = jnp.where(iota(outer.shape, 1) >= iota(outer.shape, 0), outer, 0.0)
    turn = (iota(outer.shape, 1) + iota(outer.shape, 0)) % LANES
    skewed = jnp.take_along_axis(outer, turn, axis=1, mode="promise_in_bounds")
    near = decay_out * jnp.sum(skewed, axis=0, keepdims=True)
    near_zero = jnp.sum(near, axis=1, keepdims=True)
    near_one = jnp.sum(near * age_out, axis=1, keepdims=True)
    value_states = contract(left_split(values), split_in, 1, 1)
    grad_states = contract(left_split(grads), split_out, 1, 1)
    products = values * grads
    part_skip = products[:channels]
    for j in range(1, chunks):
        part_skip = part_skip + products[j * channels : (j + 1) * channels]
    part_skip = jnp.sum(part_skip, axis=1, keepdims=True)
    lane = iota((channels, LANES), 1)
    row_id = iota((channels, LANES), 0)
    prefix_zero = jnp.zeros((channels, LANES), F32)
    prefix_one = cross_zero = cross_one = suffix_zero = suffix_one = prefix_zero
    for j in range(chunks):
        rows = slice(j * channels, (j + 1) * channels)
        grad_zero, grad_one = grad_states[rows, :LANES], grad_states[rows, LANES:]
        if j > 0:
            cross_zero = cross_zero + prefix_zero * grad_zero
            cross_one = cross_one + prefix_one * grad_zero + prefix_zero * grad_one
        starts_ref[rows] = prefix_zero
        prefix_one = step * (prefix_one + growth * prefix_zero) + value_states[rows, LANES:]
        prefix_zero = step * prefix_zero + value_states[rows, :LANES]
    for j in range(chunks - 1, -1, -1):
        rows = slice(j * channels, (j + 1) * channels)
        ends_ref[rows] = suffix_zero
        suffix_one = step * (suffix_one + growth * suffix_zero) + grad_states[rows, LANES:]
        suffix_zero = step * suffix_zero + grad_states[rows, :LANES]
    half = channels // 2
    own = lane // modes == row_id % half
    payload = []
    for state in (prefix_zero, prefix_one, suffix_zero, suffix_one):
        state = jnp.where(own, state, 0.0)
        payload.append(jnp.sum(state[:half], axis=0, keepdims=True))
        payload.append(jnp.sum(state[half:], axis=0, keepdims=True))
    extras = (
        jnp.where(lane < modes, cross_zero, 0.0)
        + jnp.where((lane >= modes) & (lane < 2 * modes), cross_one, 0.0)
        + jnp.where(lane == row_id, near_zero, 0.0)
        + jnp.where(lane == row_id + modes, near_one, 0.0)
        + jnp.where(lane == row_id + 2 * modes, part_skip, 0.0)
    )
    payload.append(jnp.sum(extras, axis=0, keepdims=True))
    sublane = iota((8, LANES), 0)
    for k in range(len(payload)):
        tile = jnp.zeros((8, LANES), F32)
        for i in range(8):
            tile = jnp.where(sublane == i, payload[(8 * k + i) % len(payload)], tile)
        for start in range(8 * k, out_ref.shape[0], 8 * len(payload)):
            out_ref[start : start + 8] = tile

    for move in moves[1:3]:
        move.wait()


def pair_sums(seq_size, chips, rates_ref, all_ref, sums_ref):
    modes = LANES // 8
    leap, leap_growth = rates_ref[0:1], rates_ref[1:2]

    def pairs(e, carry):
        done = []
        for part, (prefix_zero, prefix_one, cross_zero, cross_one) in enumerate(carry):
            value_zero, value_one, grad_zero, grad_one = [
                strided(all_ref, e * BLOCK + 2 * kind + part, chips, seq_size * BLOCK) for kind in range(4)
            ]
            done.append(
                (
                    leap * prefix_zero + value_zero,
                    leap * prefix_one + (leap_growth * prefix_zero + value_one),
                    cross_zero + prefix_zero * grad_zero,
                    cross_one + prefix_one * grad_zero + prefix_zero * grad_one,
                )
            )
        return tuple(done)

    zeros = jnp.zeros((chips, LANES), F32)
    carry = ((zeros,) * 4,) * 2
    if seq_size <= 8 or seq_ranks(seq_size) != tuple(range(seq_size)):
        for e in range(seq_size):
            carry = pairs(seq_ranks(seq_size).index(e), carry)
    else:
        carry = lax.fori_loop(0, seq_size, pairs, carry)
    sums = [jnp.sum(carry[0][i] + carry[1][i], axis=0, keepdims=True) for i in (2, 3)]
    extras = jnp.sum(strided(all_ref, BLOCK - 1, chips * seq_size, BLOCK), axis=0, keepdims=True)
    kind = iota((8, LANES), 0)
    sums = jnp.where(kind == 0, sums[0], sums[1]) + jnp.where(iota((8, LANES), 1) // modes == kind, extras, 0.0)
    sums_ref[...] = sum([roll(sums, shift) for shift in range(modes, LANES, modes)], sums)


def filter_grads(total, memory_ref, residue_ref, mine_ref, other_ref, *refs):
    results, scratch, sent = refs[:2], refs[2:4], refs[4]
    modes = memory_ref.shape[1]
    scale = jnp.sqrt(2.0 / memory_ref[...]) / math.sqrt(total)
    sums = mine_ref[...] + other_ref[...]
    sum_zero, sum_one = sums[0:1, :modes], sums[1:2, :modes]
    scratch[0][...] = scale * sum_zero
    scratch[1][...] = residue_ref[...] * scale * (sum_one - 0.5 * sum_zero)
    moves = [pltpu.make_async_copy(*ends, sent.at[i]) for i, ends in enumerate(zip(scratch, results))]
    for move in moves:
        move.start()
    for move in moves:
        move.wait()


def finish(seq_size, ch_size, rates_ref, starts_ref, ends_ref, *refs):
    parameters, (x_ref, q_ref, k_ref, d_ref, all_ref), refs = refs[:3], refs[3:8], refs[8:]
    results, scratch, sent = refs[:5], refs[5:10], refs[10]
    moves = [pltpu.make_async_copy(*ends, sent.at[i]) for i, ends in enumerate(zip(scratch, results))]
    channels, local_len = x_ref.shape
    modes = LANES // 8
    chunks = local_len // LANES
    half = channels // 2
    rows = chunks * channels
    signal, gate_in = by_chunk(x_ref), by_chunk(k_ref)
    gate_out, cotangent = by_chunk(q_ref), by_chunk(d_ref)
    weights, powers, base_mixed, base_grad, read_out, read_in = local_parts(
        seq_size, rates_ref, signal * gate_in, cotangent * gate_out, parameters, chunks, channels
    )
    me = 0
    for p, index in enumerate(chip_ranks(ch_size // CORES)):
        me = me + jnp.where(lax.axis_index("ch") // CORES == index, p * seq_size * BLOCK, 0)
    own = iota((half, LANES), 1) // modes == iota((half, LANES), 0)

    def border(kind, weight):
        parts = []
        for part in range(2):
            state = strided(all_ref, me + 2 * kind + part, seq_size, BLOCK)
            state = jnp.sum(weight * state, axis=0, keepdims=True)
            parts.append(jnp.where(own, state, 0.0))
        return jnp.concatenate(parts, axis=0)

    mine = iota((rows, LANES), 1) // modes == iota((rows, LANES), 0) % half

    def readout(state, factors, states, matrix):
        state = jnp.concatenate([factor * state for factor in factors], axis=0) + jnp.where(mine, states, 0.0)
        return contract(left_split(state), right_split(matrix, axis=0), 1, 0)

    mixed = base_mixed + readout(border(0, weights[0]), powers, starts_ref[...], read_out)
    grad_values = base_grad + readout(border(2, weights[1]), powers[::-1], ends_ref[...], read_in)
    skip = jnp.sum(strided(all_ref, me + BLOCK - 1, seq_size, BLOCK), axis=0, keepdims=True)
    skip = roll(skip, -2 * modes)[:, :channels] / math.sqrt(seq_size * local_len)
    for i, data in enumerate((gate_out * mixed, grad_values * gate_in, cotangent * mixed, grad_values * signal)):
        for j in range(chunks):
            scratch[i][:, j * LANES : (j + 1) * LANES] = data[j * channels : (j + 1) * channels].astype(BF16)
    scratch[4][...] = skip
    for move in moves:
        move.start()
    for move in moves:
        move.wait()


def per_device(signal_x, gate_q, gate_k, skip_gain, residue, memory, cotangent):
    channels, local_len = signal_x.shape
    modes = memory.shape[0]
    seq_size, ch_size = lax.axis_size("seq"), lax.axis_size("ch")
    devices = seq_size * ch_size
    params = pltpu.CompilerParams(vmem_limit_bytes=32 * 1024 * 1024)
    in_hbm = pl.BlockSpec(memory_space=pltpu.HBM)
    arguments = (memory[None], residue[None], skip_gain[None], signal_x, gate_q, gate_k, cotangent)
    arguments = [pltpu.with_memory_space_constraint(data, pltpu.HBM) for data in arguments]
    copies = [(data.shape, data.dtype) for data in arguments]
    rows = local_len // LANES * channels
    chips = ch_size // CORES
    peers = chips * seq_size
    made = [((peers * BLOCK, LANES), F32), ((8 + 2 * modes, LANES), F32), ((rows, LANES), F32), ((rows, LANES), F32)]
    mine, rates, starts, ends, *copied = pl.pallas_call(
        make_states,
        in_specs=[in_hbm] * 7,
        out_shape=[jax.ShapeDtypeStruct(*shape) for shape in made + copies],
        scratch_shapes=[pltpu.SemaphoreType.DMA((7,))],
        compiler_params=params,
    )(*arguments)
    groups = [
        [s * ch_size + chip * CORES + (core + chip) % CORES for chip in chip_ranks(chips) for s in seq_ranks(seq_size)]
        for core in reversed(range(CORES))
    ]
    everyone = lax.all_to_all(mine.reshape(peers, BLOCK, 1, LANES), AXES, 0, 0, axis_index_groups=groups)
    everyone = everyone.reshape(peers * BLOCK, LANES)
    sums = pl.pallas_call(
        functools.partial(pair_sums, seq_size, chips),
        out_shape=jax.ShapeDtypeStruct((8, LANES), F32),
        compiler_params=params,
    )(rates, everyone)
    other = lax.ppermute(sums, "ch", [(i, i ^ 1) for i in range(ch_size)])
    big = ((channels, local_len), BF16)
    shapes = [big] * 4 + [((1, channels), F32)]
    results = pl.pallas_call(
        functools.partial(finish, seq_size, ch_size),
        out_shape=[jax.ShapeDtypeStruct(*shape) for shape in shapes],
        out_specs=[in_hbm] * 5,
        scratch_shapes=[*[pltpu.VMEM(*shape) for shape in shapes], pltpu.SemaphoreType.DMA((5,))],
        compiler_params=params,
        cost_estimate=pl.CostEstimate(flops=20_000_000, bytes_accessed=1_000_000, transcendentals=10_000),
    )(rates, starts, ends, *copied, everyone)
    small = [((1, modes), F32)] * 2
    filters = pl.pallas_call(
        functools.partial(filter_grads, ch_size * channels * seq_size * local_len),
        out_shape=[jax.ShapeDtypeStruct(*shape) for shape in small],
        out_specs=[in_hbm] * 2,
        scratch_shapes=[*[pltpu.VMEM(*shape) for shape in small], pltpu.SemaphoreType.DMA((2,))],
        compiler_params=params,
    )(copied[0], copied[1], sums, other)
    return (*results[:4], results[4][0], filters[0][0], filters[1][0])


def solution(mesh):
    grid = P("ch", "seq")
    return jax.shard_map(
        per_device,
        mesh=mesh,
        in_specs=(grid, grid, grid, P("ch"), P(), P(), grid),
        out_specs=(grid, grid, grid, grid, P("ch"), P(), P()),
        check_vma=False,
    )
```
